32 devices in a mesh: section: 2 (over x), dp: 4 (over z), tensor: 4 (over y, core).
Axes of the slice: x: 2, y: 2, z: 4, core: 2. Of those that a mesh axis runs over, the one named last changes fastest.
Arguments:
- tokens: bfloat16 [8, 2048, 768], P('dp', 'tensor'), may hold values from -6 to 6
- qkv_weight: bfloat16 [2, 3, 768, 768], P('section', None, None, 'tensor'), may hold values from -0.21875 to 0.21875
- out_weight: bfloat16 [2, 768, 768], P('section', 'tensor'), may hold values from -2.5 to 2.5
- up_weight: bfloat16 [2, 768, 3072], P('section', None, 'tensor'), may hold values from -0.21875 to 0.21875
- down_weight: bfloat16 [2, 3072, 768], P('section', 'tensor'), may hold values from -0.109375 to 0.109375
- vectors: float32 [2, 3, 768], P('section'), may hold values from -4 to 4
- lengths: int32 [8], P('dp'), may hold values from 1024 to 2048, as said below
- selected: int32 [8, 256], P('dp'), may hold values from 0 to 2047, as said below
- cotangent: bfloat16 [8, 2048, 768], P('dp', 'tensor'), may hold values from -6 to 6
Outputs:
- section_results: float32 [2, 8, 2048, 768], P('section', 'dp', 'tensor')
- qkv_grad: float32 [2, 3, 768, 768], P('section', None, 'dp', 'tensor')
- out_proj_grad: float32 [2, 768, 768], P('section', 'tensor', 'dp')
- up_grad: float32 [2, 768, 3072], P('section', 'dp', 'tensor')
- down_grad: float32 [2, 3072, 768], P('section', 'tensor', 'dp')
- vector_grad: float32 [2, 3, 768], P('section', None, 'dp')
The draws below stay inside these ranges and needn't reach their ends.
Inputs may be any that keep to these rules, and one draw needn't show every extreme that they name: `lengths`: in each group of 2 consecutive sequences one has length 2048; every length is at least half of 2048. `selected`: each row holds 256 distinct positions in increasing order, all below that sequence's length.
All inputs are finite; a program needn't handle non-finite values.
Results may differ from the reference program's by a relative error of at most 0.02.
Values may be sent and summed in bfloat16 or wider, within the bound.
No kernel may reach another device: no remote copies, remote signals or barrier semaphores. Data moves between devices by JAX's collectives and lax.ppermute only.
A program may use at most 256 MiB of HBM per device.

```python
import jax
import jax.numpy as jnp
from jax import lax

D = 768
HEADS = 12
FF = 3072
HDIM = 64
SLOT = 2048
CAP = 256
SEQS = 2
SEQ_ALL = 8


def routing_tables(key):
    base = jax.random.fold_in(key, 11)
    first_key, second_key, third_key = jax.random.split(base, 3)
    lengths = jax.random.randint(first_key, (SEQ_ALL,), SLOT // 2, SLOT + 1)
    groups = SEQ_ALL // SEQS
    full_at = jax.random.randint(second_key, (groups,), 0, SEQS)
    full_mask = (jnp.arange(SEQS)[None, :] == full_at[:, None]).reshape(SEQ_ALL)
    lengths = jnp.where(full_mask, SLOT, lengths).astype(jnp.int32)
    scores = jax.random.randint(third_key, (SEQ_ALL, SLOT), 0, 65536)
    positions = jnp.arange(SLOT, dtype=jnp.int32)
    keyed = scores * SLOT + positions[None, :]
    keyed = jnp.where(positions[None, :] < lengths[:, None], keyed, -1 - positions[None, :])
    unused, picked = lax.top_k(keyed, CAP)
    return (lengths, jnp.sort(picked, axis=1).astype(jnp.int32))


def draw_lengths(key, part):
    return routing_tables(key)[0]


def draw_selected(key, part):
    return routing_tables(key)[1]


def draw_vectors(key, part):
    base = jax.random.fold_in(key, 23)
    gain_key, router_key = jax.random.split(base)
    gains = 1.0 + 0.15 * jnp.clip(jax.random.normal(gain_key, (2, 3, D), jnp.float32), -2.0, 2.0)
    router = jnp.clip(jax.random.normal(router_key, (2, 3, D), jnp.float32), -4.0, 4.0)
    marked = (jnp.arange(2)[:, None] == 0) & (jnp.arange(3)[None, :] == 2)
    return jnp.where(marked[:, :, None], router, gains).astype(jnp.float32)


def steps_of(key, dims, cuts, smallest, high):
    def one(dim, blocks):
        draws = jax.random.uniform(jax.random.fold_in(jax.random.fold_in(key, 6), dim), (blocks,), jnp.float32, smallest / len(cuts), high / len(cuts))
        return jnp.repeat(jnp.exp(draws), dims[dim] // blocks).reshape((-1,) + (1,) * (len(dims) - dim - 1))

    level = one(*cuts[0])
    for cut in cuts[1:]:
        level = level * one(*cut)
    return level


def bell_draw(key, shape, width, bound, pieces=(), kind=jnp.bfloat16):
    values = width * jax.random.normal(key, shape, jnp.float32)
    if pieces:
        values = values * steps_of(key, shape, pieces, -0.22, 0.18)
    return jnp.clip(values, -bound, bound).astype(kind)


def setup_inputs(seed: int = 0) -> dict:
    arg_keys = jax.random.split(jax.random.key(seed), 10)
    return {
        "tokens": bell_draw(arg_keys[0], (SEQ_ALL, SLOT, D), 1.0, 6.0, ((0, 4), (1, 4))),
        "qkv_weight": bell_draw(arg_keys[1], (2, 3, D, D), D ** -0.5, 0.21875, ((0, 2), (3, 4))),
        "out_weight": bell_draw(arg_keys[2], (2, D, D), (max(D // 128, 1)) ** -0.5, 2.5, ((0, 2), (1, 4))),
        "up_weight": bell_draw(arg_keys[3], (2, D, FF), D ** -0.5, 0.21875, ((0, 2), (2, 4))),
        "down_weight": bell_draw(arg_keys[4], (2, FF, D), FF ** -0.5, 0.109375, ((0, 2), (1, 4))),
        "vectors": draw_vectors(jax.random.fold_in(arg_keys[9], 71), 0),
        "lengths": draw_lengths(jax.random.fold_in(arg_keys[9], 71), 0),
        "selected": draw_selected(jax.random.fold_in(arg_keys[9], 71), 0),
        "cotangent": bell_draw(arg_keys[8], (SEQ_ALL, SLOT, D), 1.0, 6.0, ((0, 4), (1, 4))),
    }


EPSILON = 1e-06
PRECISE = lax.Precision.HIGHEST
NEGATIVE = -1e+30

@jax.custom_vjp
def low(v):
    return lax.optimization_barrier(v.astype(jnp.bfloat16)).astype(jnp.float32)

@jax.custom_vjp
def low_back(v):
    return v

def low_keep(v):
    return (low(v), None)

def low_pass(kept, grad):
    return (grad,)

def back_keep(v):
    return (v, None)

def back_low(kept, grad):
    return (low(grad),)
low.defvjp(low_keep, low_pass)
low_back.defvjp(back_keep, back_low)

def both_ways(value):
    return low_back(low(value))

def norm_rows(values, gain):
    return values * lax.rsqrt(lax.optimization_barrier(jnp.mean(values * values, axis=-1, keepdims=True)) + EPSILON) * gain

def product(left, right):
    return jnp.dot(left, right, precision=PRECISE, preferred_element_type=jnp.float32)

def attend(normed, packed_weight, mix_weight, places, length):
    row_count = normed.shape[0]
    packed = jnp.einsum('rd,kdc->krc', normed, packed_weight, precision=PRECISE)
    queries = both_ways(packed[0]).reshape(row_count, HEADS, HDIM)
    keys_all = both_ways(packed[1]).reshape(row_count, HEADS, HDIM)
    values_all = both_ways(packed[2]).reshape(row_count, HEADS, HDIM)
    raw = low_back(jnp.einsum('qhd,khd->hqk', queries, keys_all, precision=PRECISE))
    allowed = (places[None, :] <= places[:, None]) & (places < length)[None, :]
    scores = jnp.where(allowed[None], raw * HDIM ** (-0.5), NEGATIVE)
    highest = lax.optimization_barrier(jnp.max(scores, axis=-1, keepdims=True))
    expos = jnp.exp(scores - highest)
    probs = expos / lax.optimization_barrier(jnp.sum(expos, axis=-1, keepdims=True))
    mixed = jnp.einsum('hqk,khd->qhd', low(probs), values_all, precision=PRECISE)
    mixed = both_ways(mixed.reshape(row_count, D))
    return product(mixed, mix_weight)

def layer(rows, gains, packed_weight, mix_weight, widen_weight, narrow_weight, places, length):
    normed = low(norm_rows(rows, gains[0]))
    attn = low_back(attend(normed, packed_weight, mix_weight, places, length))
    middle = rows + attn
    normed2 = low(norm_rows(middle, gains[1]))
    pre = low_back(product(normed2, widen_weight))
    act = low(jax.nn.gelu(pre))
    mlp = low_back(product(act, narrow_weight))
    return (attn, mlp, middle)

def one_sequence(params, row_block, places, length):
    packed_weight, mix_weight, widen_weight, narrow_weight, vectors = params
    picked = low_back(row_block[places])
    router = jnp.dot(picked, vectors[0, 2], precision=PRECISE) * D ** (-0.5)
    attn, mlp, middle = layer(picked, vectors[0], packed_weight[0], mix_weight[0], widen_weight[0], narrow_weight[0], places, length)
    update = router[:, None] * (attn + mlp)
    layer_out = both_ways(row_block.at[places].add(update))
    positions = jnp.arange(SLOT, dtype=jnp.int32)
    attn_two, mlp_two, middle_two = layer(layer_out, vectors[1], packed_weight[1], mix_weight[1], widen_weight[1], narrow_weight[1], positions, length)
    return norm_rows(middle_two + mlp_two, vectors[1, 2])

def reference(tokens, qkv_weight, out_weight, up_weight, down_weight, vectors, lengths, selected, cotangent):
    params = (qkv_weight.astype(jnp.float32), out_weight.astype(jnp.float32), up_weight.astype(jnp.float32), down_weight.astype(jnp.float32), vectors)
    inputs = tokens.astype(jnp.float32)
    stepper = jax.checkpoint(one_sequence)

    def whole(weights, rows):
        return lax.map(lambda element: stepper(weights, element[0], element[1], element[2]), (rows, selected, lengths))
    result, pullback = jax.vjp(whole, params, inputs)
    param_grads, input_grad = pullback(cotangent.astype(jnp.float32))
    stacked = jnp.stack([input_grad, result])
    return (stacked, param_grads[0], param_grads[1], param_grads[2], param_grads[3], param_grads[4])
```

```python
import functools

import jax
import jax.numpy as jnp
from jax import lax
from jax.experimental import pallas as pl
from jax.experimental.pallas import tpu as pltpu
from jax.sharding import PartitionSpec as P

HEADS = 12
EPSILON = 1e-06
NEGATIVE = -1e30
BF = jnp.bfloat16
F32 = jnp.float32
PAD = 256
MIB = 1 << 20


def swap(block, axis, bit):
    count = lax.axis_size(axis)
    return lax.ppermute(block, axis, [(i, i ^ bit) for i in range(count)])


def hop(block, source, target):
    return lax.ppermute(block, "section", [(source, target)])


def dot(left, right):
    return lax.dot_general(left, right, (((1,), (0,)), ((), ())), preferred_element_type=F32)


def dot_nt(left, right):
    return lax.dot_general(left, right, (((1,), (1,)), ((), ())), preferred_element_type=F32)


def dot_tn(left, right):
    return lax.dot_general(left, right, (((0,), (0,)), ((), ())), preferred_element_type=F32)


def unit_rows(values):
    scale = lax.rsqrt(jnp.mean(values * values, axis=-1, keepdims=True) + EPSILON)
    return values * scale, scale


def norm_back(unit, scale, gain, grad):
    e = grad * gain
    return scale * (e - unit * jnp.mean(e * unit, axis=-1, keepdims=True))


def gelu_pair(x):
    c = 0.7978845608028654
    a = 0.044715
    xx = x * x
    th = jnp.tanh(c * (x + a * (x * xx)))
    half = 0.5 * (1.0 + th)
    slope = half + (0.5 * x) * (1.0 - th * th) * (c * (1.0 + (3.0 * a) * xx))
    return x * half, slope


def lanes(rows, width):
    return lax.broadcasted_iota(jnp.int32, (rows, width), 1)


def subs(rows, width):
    return lax.broadcasted_iota(jnp.int32, (rows, width), 0)


def head_of(values, lane, head, width):
    zero = jnp.zeros_like(values)
    return jnp.where((lane >= head * width) & (lane < (head + 1) * width), values, zero)


def three_pieces(column):
    first = column.astype(BF)
    rest = column - first.astype(F32)
    second = rest.astype(BF)
    third = (rest - second.astype(F32)).astype(BF)
    return first, second, third


def params(limit=56, grid=None):
    if grid is None:
        return pltpu.CompilerParams(vmem_limit_bytes=limit * MIB)
    return pltpu.CompilerParams(
        vmem_limit_bytes=limit * MIB, dimension_semantics=("arbitrary",) * grid
    )


VM = pl.BlockSpec(memory_space=pltpu.VMEM)
SM = pl.BlockSpec(memory_space=pltpu.SMEM)
HB = pl.BlockSpec(memory_space=pl.ANY)


def shape(dims, dtype):
    return jax.ShapeDtypeStruct(dims, dtype)


def halves_out(partial, low, keep_ref, send_ref):
    pick = partial.shape[0] // 2
    half = pick // 2
    for s in range(2):
        first = partial[s * pick : s * pick + half]
        second = partial[s * pick + half : (s + 1) * pick]
        keep_ref[s] = jnp.where(low == 0, first, second).astype(BF)
        send_ref[s] = jnp.where(low == 0, second, first).astype(BF)


def halves_in(own_ref, other_ref, low):
    parts = []
    for s in range(2):
        own, other = own_ref[s].astype(F32), other_ref[s].astype(F32)
        parts.append(jnp.where(low == 0, own, other))
        parts.append(jnp.where(low == 0, other, own))
    return jnp.concatenate(parts, 0)


def pick_kernel(info, rows_ref, sel_ref, keep_ref, send_ref):
    tensor, low = info[0], info[2]
    own = rows_ref.shape[1]
    pick = sel_ref.shape[1]
    parts = []
    for s in range(2):
        table = (sel_ref[s] == lanes(pick, own) + tensor * own).astype(F32).astype(BF)
        parts.append(dot(table, rows_ref[s]))
    halves_out(jnp.concatenate(parts, 0), low, keep_ref, send_ref)


def pick_rows(info, rows, sel_col):
    _, _, d = rows.shape
    pick = sel_col.shape[1]
    out = shape((2, pick // 2, d), BF)
    return pl.pallas_call(
        pick_kernel,
        out_shape=(out, out),
        in_specs=[SM, VM, VM],
        out_specs=(VM, VM),
        compiler_params=params(),
        name="pick",
    )(info, rows, sel_col)


def routed_attn_kernel(
    heads, info, own_ref, other_ref, gains_ref, qkv_ref, mix_ref,
    picked_ref, normed_ref, q_ref, k_ref, v_ref, mixed_ref, keep_ref, send_ref,
):
    low = info[2]
    picked = halves_in(own_ref, other_ref, low)
    picked_ref[...] = picked.astype(BF)
    unit, _ = unit_rows(picked)
    normed = (unit * gains_ref[0:1, :]).astype(BF)
    normed_ref[...] = normed
    width = qkv_ref.shape[2] // heads
    q = dot(normed, qkv_ref[0]).astype(BF)
    k = dot(normed, qkv_ref[1]).astype(BF)
    v = dot(normed, qkv_ref[2]).astype(BF)
    q = (q.astype(F32) * width ** (-0.5)).astype(BF)
    q_ref[...] = q
    k_ref[...] = k
    v_ref[...] = v
    pick = picked.shape[0] // 2
    lane = lanes(pick, heads * width)
    allowed = lanes(pick, pick) <= subs(pick, pick)
    parts = []
    for s in range(2):
        span = slice(s * pick, (s + 1) * pick)
        total = jnp.zeros((pick, heads * width), F32)
        for h in range(heads):
            scores = dot_nt(head_of(q[span], lane, h, width), k[span])
            scores = jnp.where(allowed, scores, NEGATIVE)
            expos = jnp.exp(scores - jnp.max(scores, axis=-1, keepdims=True))
            probs = expos / jnp.sum(expos, axis=-1, keepdims=True)
            total = total + dot(probs.astype(BF), head_of(v[span], lane, h, width))
        parts.append(total.astype(BF))
    mixed = jnp.concatenate(parts, 0)
    mixed_ref[...] = mixed
    halves_out(dot(mixed, mix_ref[...]), low, keep_ref, send_ref)


def routed_attn(info, own, other, gains, qkv_w, mix_w, heads):
    _, half, d = own.shape
    rows = 4 * half
    cols = qkv_w.shape[2]
    part = shape((2, half, d), BF)
    wide, narrow = shape((rows, d), BF), shape((rows, cols), BF)
    return pl.pallas_call(
        functools.partial(routed_attn_kernel, heads),
        out_shape=(wide, wide, narrow, narrow, narrow, narrow, part, part),
        in_specs=[SM] + [VM] * 5,
        out_specs=(VM,) * 8,
        compiler_params=params(),
        name="routed_attn",
    )(info, own, other, gains, qkv_w, mix_w)


def routed_mlp_kernel(
    info, picked_ref, own_ref, other_ref, gains_ref, up_ref, down_ref,
    attn_ref, normed_ref, act_ref, slope_ref, keep_ref, send_ref,
):
    low = info[2]
    attn = halves_in(own_ref, other_ref, low)
    attn_ref[...] = attn.astype(BF)
    unit, _ = unit_rows(picked_ref[...].astype(F32) + attn)
    normed = (unit * gains_ref[1:2, :]).astype(BF)
    normed_ref[...] = normed
    act, slope = gelu_pair(dot(normed, up_ref[...]))
    act = act.astype(BF)
    act_ref[...] = act
    slope_ref[...] = slope
    halves_out(dot(act, down_ref[...]), low, keep_ref, send_ref)


def routed_mlp(info, picked, own, other, gains, up_w, down_w):
    rows, d = picked.shape
    hidden = up_w.shape[1]
    part = shape((2, rows // 4, d), BF)
    return pl.pallas_call(
        routed_mlp_kernel,
        out_shape=(
            shape((rows, d), BF), shape((rows, d), BF), shape((rows, hidden), BF),
            shape((rows, hidden), F32), part, part,
        ),
        in_specs=[SM] + [VM] * 6,
        out_specs=(VM,) * 6,
        compiler_params=params(),
        name="routed_mlp",
    )(info, picked, own, other, gains, up_w, down_w)


def update_kernel(picked_ref, attn_ref, mlp_ref, mlp2_ref, gains_ref, both_ref, update_ref):
    d = picked_ref.shape[2]
    weight = gains_ref[2:3, :] * d ** (-0.5)
    for s in range(2):
        router = jnp.sum(picked_ref[s].astype(F32) * weight, axis=-1, keepdims=True)
        both = attn_ref[s].astype(F32) + (mlp_ref[s].astype(F32) + mlp2_ref[s].astype(F32))
        both_ref[s] = both.astype(BF)
        update_ref[s] = (router * both).astype(BF)


def make_update(picked_half, attn_half, mlp_half, mlp_far, gains):
    out = shape(picked_half.shape, BF)
    return pl.pallas_call(
        update_kernel,
        out_shape=(out, out),
        in_specs=[VM] * 5,
        out_specs=(VM, VM),
        compiler_params=params(),
        name="update",
    )(picked_half, attn_half, mlp_half, mlp_far, gains)


def routed_back_mlp_kernel(
    info, sel_own, sel_other, picked_ref, attn_ref, gains_ref, slope_ref, up_ref, down_ref,
    d_sel_ref, d_mlp_ref, d_pre_ref, gain_ref, keep_ref, send_ref,
):
    low = info[2]
    d = picked_ref.shape[1]
    d_sel = halves_in(sel_own, sel_other, low)
    d_sel_ref[...] = d_sel
    picked = picked_ref[...].astype(F32)
    router = jnp.sum(picked * (gains_ref[2:3, :] * d ** (-0.5)), axis=-1, keepdims=True)
    d_mlp = (router * d_sel).astype(BF)
    d_mlp_ref[...] = d_mlp
    d_pre = (dot_nt(d_mlp, down_ref[...]) * slope_ref[...]).astype(BF)
    d_pre_ref[...] = d_pre
    d_normed = dot_nt(d_pre, up_ref[...])
    unit, _ = unit_rows(picked + attn_ref[...].astype(F32))
    gain_ref[...] = jnp.sum(d_normed * unit, axis=0, keepdims=True)
    halves_out(d_normed, low, keep_ref, send_ref)


def routed_back_mlp(info, sel_own, sel_other, picked, attn, gains, slope, up_w, down_w):
    rows, d = picked.shape
    hidden = up_w.shape[1]
    part = shape((2, rows // 4, d), BF)
    return pl.pallas_call(
        routed_back_mlp_kernel,
        out_shape=(
            shape((rows, d), F32), shape((rows, d), BF), shape((rows, hidden), BF),
            shape((1, d), F32), part, part,
        ),
        in_specs=[SM] + [VM] * 8,
        out_specs=(VM,) * 6,
        compiler_params=params(),
        name="routed_back_mlp",
    )(info, sel_own, sel_other, picked, attn, gains, slope, up_w, down_w)


def routed_back_attn_kernel(
    heads, info, own_ref, other_ref, d_sel_ref, picked_ref, attn_ref, both_own, both_other,
    gains_ref, q_ref, k_ref, v_ref, qkv_ref, mix_ref,
    d_mid_ref, d_low_ref, d_qkv_ref, vec_ref, keep_ref, send_ref,
):
    low = info[2]
    rows, d = picked_ref.shape
    d_normed2 = halves_in(own_ref, other_ref, low)
    picked = picked_ref[...].astype(F32)
    d_sel = d_sel_ref[...]
    router_row = gains_ref[2:3, :] * d ** (-0.5)
    router = jnp.sum(picked * router_row, axis=-1, keepdims=True)
    unit2, scale2 = unit_rows(picked + attn_ref[...].astype(F32))
    d_mid = norm_back(unit2, scale2, gains_ref[1:2, :], d_normed2)
    both = halves_in(both_own, both_other, low)
    d_router = jnp.sum(d_sel * both, axis=-1, keepdims=True)
    d_mid_ref[...] = d_mid + d_router * router_row
    d_weight = jnp.sum(picked * d_router, axis=0, keepdims=True) * d ** (-0.5)
    vec_ref[1:2, :] = jnp.where(info[0] == 0, d_weight, jnp.zeros_like(d_weight))
    d_low = (router * d_sel + d_mid).astype(BF)
    d_low_ref[...] = d_low
    d_mixed = dot_nt(d_low, mix_ref[...]).astype(BF)
    width = qkv_ref.shape[2] // heads
    pick = rows // 2
    lane = lanes(pick, heads * width)
    allowed = subs(pick, pick) <= lanes(pick, pick)
    dq_parts, dk_parts, dv_parts = [], [], []
    for s in range(2):
        span = slice(s * pick, (s + 1) * pick)
        q, k, v, dm = q_ref[span, :], k_ref[span, :], v_ref[span, :], d_mixed[span]
        dq = jnp.zeros((pick, heads * width), F32)
        dk, dv = dq, dq
        for h in range(heads):
            qh, kh = head_of(q, lane, h, width), head_of(k, lane, h, width)
            dh = head_of(dm, lane, h, width)
            scores = jnp.where(allowed, dot_nt(k, qh), NEGATIVE)
            expos = jnp.exp(scores - jnp.max(scores, axis=0, keepdims=True))
            probs = expos / jnp.sum(expos, axis=0, keepdims=True)
            d_probs = dot_nt(v, dh)
            inner = jnp.sum(probs * d_probs, axis=0, keepdims=True)
            d_scores = (probs * (d_probs - inner)).astype(BF)
            dv = dv + dot(probs.astype(BF), dh)
            dk = dk + dot(d_scores, qh)
            dq = dq + dot_tn(d_scores, kh)
        dq_parts.append(dq * width ** (-0.5))
        dk_parts.append(dk)
        dv_parts.append(dv)
    d_normed = jnp.zeros((rows, d), F32)
    for i, parts in enumerate((dq_parts, dk_parts, dv_parts)):
        whole = jnp.concatenate(parts, 0).astype(BF)
        d_qkv_ref[i] = whole
        d_normed = d_normed + dot_nt(whole, qkv_ref[i])
    unit, _ = unit_rows(picked)
    vec_ref[0:1, :] = jnp.sum(d_normed * unit, axis=0, keepdims=True)
    halves_out(d_normed, low, keep_ref, send_ref)


def routed_back_attn(
    info, own, other, d_sel, picked, attn, both_own, both_other, gains, q, k, v, qkv_w, mix_w, heads
):
    rows, d = picked.shape
    part = shape((2, rows // 4, d), BF)
    return pl.pallas_call(
        functools.partial(routed_back_attn_kernel, heads),
        out_shape=(
            shape((rows, d), F32), shape((rows, d), BF), shape((3,) + q.shape, BF),
            shape((2, d), F32), part, part,
        ),
        in_specs=[SM] + [VM] * 13,
        out_specs=(VM,) * 6,
        compiler_params=params(),
        name="routed_back_attn",
    )(info, own, other, d_sel, picked, attn, both_own, both_other, gains, q, k, v, qkv_w, mix_w)


def finish_kernel(
    info, own_ref, other_ref, d_mid_ref, picked_ref, gains_ref, sel_ref,
    d_rows_ref, far_ref, result_ref, out_ref,
):
    tensor, section, low = info[0], info[1], info[2]
    own = d_rows_ref.shape[0]
    pick = sel_ref.shape[2]

    @pl.when(section == 0)
    def _():
        d_normed = halves_in(own_ref, other_ref, low)
        unit, scale = unit_rows(picked_ref[...].astype(F32))
        d_picked = d_mid_ref[...] + norm_back(unit, scale, gains_ref[0:1, :], d_normed)
        d_picked = d_picked.astype(BF)
        for s in range(2):
            table = (sel_ref[s] == subs(own, pick) + tensor * own).astype(F32).astype(BF)
            base = (d_rows_ref if s == 0 else far_ref)[...].astype(F32)
            out_ref[s] = base + dot(table, d_picked[s * pick : (s + 1) * pick])

    @pl.when(section != 0)
    def _():
        out_ref[0] = far_ref[...].astype(F32)
        out_ref[1] = result_ref[...]


def finish(info, own, other, d_mid, picked, gains, sel_row, d_rows, far, result):
    rows, d = d_rows.shape
    return pl.pallas_call(
        finish_kernel,
        out_shape=shape((2, rows, d), F32),
        in_specs=[SM] + [VM] * 9,
        out_specs=VM,
        compiler_params=params(),
        name="finish",
    )(info, own, other, d_mid, picked, gains, sel_row, d_rows, far, result)


def project_kernel(
    heads, width, info, tok0, tok1, tok2, tok3, upd_own, upd_other, sel_ref, gains_ref, qkv_ref,
    rows_ref, normed_ref, q_ref, k_ref, v_ref, buf,
):
    tensor, low, length = info[0], info[2], info[3]
    r = pl.program_id(0)
    own, d = buf.shape
    for i, tok in enumerate((tok0, tok1, tok2, tok3)):
        @pl.when(r == i)
        def _():
            buf[...] = tok[...]

    place = jnp.bitwise_xor(r, tensor) * own
    pick = sel_ref.shape[1]
    first, second = upd_own[...], upd_other[...]
    update = jnp.concatenate(
        [jnp.where(low == 0, first, second), jnp.where(low == 0, second, first)], 0
    )
    table = (sel_ref[...] == subs(own, pick) + place).astype(F32).astype(BF)
    rows = (buf[...].astype(F32) + dot(table, update)).astype(BF)

    @pl.when(r == 0)
    def _():
        rows_ref[...] = rows

    unit, _ = unit_rows(rows.astype(F32))
    normed = (unit * gains_ref[0:1, :]).astype(BF)
    normed_ref[0] = normed
    lane = lanes(own, PAD)
    cols = heads * width
    one, zero = jnp.float32(1), jnp.float32(0)
    q = dot(normed, qkv_ref[0]).astype(BF).astype(F32) * width ** (-0.5)
    q_ref[0] = jnp.where(lane == cols + 3, one, q).astype(BF)
    key_at = subs(own, PAD) + place
    extra = jnp.where(lane < cols + 3, one, jnp.where(key_at < length, zero, NEGATIVE))
    k = dot(normed, qkv_ref[1])
    k_ref[0] = jnp.where((lane >= cols) & (lane < cols + 4), extra, k).astype(BF)
    v = dot(normed, qkv_ref[2])
    v_ref[0] = jnp.where((lane >= cols) & (lane < cols + 3), one, v).astype(BF)


def project(info, toks, upd_own, upd_other, sel, gains, qkv_w, heads, width):
    own, d = toks[0].shape
    count = len(toks)
    full = lambda dims: pl.BlockSpec(dims, lambda r, info: (0,) * len(dims))
    placed = lambda w: pl.BlockSpec((1, own, w), lambda r, info: (jnp.bitwise_xor(r, info[0]), 0, 0))
    padded = shape((count, own, PAD), BF)
    return pl.pallas_call(
        functools.partial(project_kernel, heads, width),
        out_shape=(shape((own, d), BF), shape((count, own, d), BF), padded, padded, padded),
        grid_spec=pltpu.PrefetchScalarGridSpec(
            num_scalar_prefetch=1,
            grid=(count,),
            in_specs=[full((own, d))] * 4
            + [full(upd_own.shape)] * 2
            + [full(sel.shape), full(gains.shape), full(qkv_w.shape)],
            out_specs=(full((own, d)), placed(d), placed(PAD), placed(PAD), placed(PAD)),
            scratch_shapes=[pltpu.VMEM((own, d), BF)],
        ),
        compiler_params=params(grid=1),
        name="project",
    )(info, *toks, upd_own, upd_other, sel, gains, qkv_w)


def attention_kernel(heads, width, info, q_ref, k_ref, v_ref, mix_ref, part_ref, mixed_ref, lse_ref):
    i = pl.program_id(0)
    block = q_ref.shape[1]
    cols = heads * width
    steps = k_ref.shape[0] // block

    def run(step):
        span = (step + 1) * block
        q = q_ref[0]
        lane = lanes(block, PAD)
        total = jnp.zeros((block, PAD), F32)
        lse = jnp.zeros((block, 128), F32)
        zero = jnp.zeros_like(q)
        for h in range(heads):
            here = (lane >= h * width) & (lane < (h + 1) * width)
            qh = jnp.where(here | (lane == cols + 3), q, zero)
            scores = dot_nt(qh, k_ref[0:span, :])
            causal = lanes(block, block) <= subs(block, block)
            tail = jnp.where(causal, scores[:, span - block :], NEGATIVE)
            high = jnp.max(tail, axis=-1, keepdims=True)
            if step:
                high = jnp.maximum(high, jnp.max(scores[:, : span - block], axis=-1, keepdims=True))
            probs = jnp.exp(tail - high).astype(BF)
            if step:
                probs = jnp.concatenate(
                    [jnp.exp(scores[:, : span - block] - high).astype(BF), probs], 1
                )
            out = dot(probs, v_ref[0:span, :])
            norm = jnp.sum(jnp.where(lane == cols, out, 0.0), axis=-1, keepdims=True)
            total = jnp.where(here, out / norm, total)
            lse = jnp.where(lanes(block, 128) == h, high + jnp.log(norm), lse)
        lse_ref[...] = lse
        mixed = total.astype(BF)
        mixed_ref[...] = mixed
        part_ref[0] = dot(mixed, mix_ref[...]).astype(BF)

    for step in range(steps):
        @pl.when(i == step)
        def _():
            run(step)


def attention(info, q, k, v, mix_w, heads, width, block=256):
    count, own, _ = q.shape
    total = count * own
    d = mix_w.shape[1]
    per = own // block
    k, v = k.reshape(total, PAD), v.reshape(total, PAD)
    full = lambda dims: pl.BlockSpec(dims, lambda i, info: (0,) * len(dims))
    return pl.pallas_call(
        functools.partial(attention_kernel, heads, width),
        out_shape=(shape((count, own, d), BF), shape((total, PAD), BF), shape((total, 128), F32)),
        grid_spec=pltpu.PrefetchScalarGridSpec(
            num_scalar_prefetch=1,
            grid=(total // block,),
            in_specs=[
                pl.BlockSpec((1, block, PAD), lambda i, info: (i // per, i % per, 0)),
                full(k.shape), full(v.shape), full(mix_w.shape),
            ],
            out_specs=(
                pl.BlockSpec(
                    (1, block, d),
                    lambda i, info: (jnp.bitwise_xor(i // per, info[0]), i % per, 0),
                ),
                pl.BlockSpec((block, PAD), lambda i, info: (i, 0)),
                pl.BlockSpec((block, 128), lambda i, info: (i, 0)),
            ),
        ),
        compiler_params=params(grid=1),
        name="attention",
    )(info, q, k, v, mix_w)


def mlp_kernel(
    rows_ref, near_ref, far_ref, cot_ref, gains_ref, up0, up1, up2, up3, dn0, dn1, dn2, dn3,
    result_ref, d_mid_ref, d_mid_low_ref, normed_ref, d_mlp_ref, act_ref, d_pre_ref, vec_ref,
    up_v, down_v, slope_v, sems,
):
    copies = []
    for i, (up, down) in enumerate(((up0, dn0), (up1, dn1), (up2, dn2), (up3, dn3))):
        a = pltpu.make_async_copy(up, up_v.at[i], sems.at[2 * i])
        b = pltpu.make_async_copy(down, down_v.at[i], sems.at[2 * i + 1])
        a.start()
        b.start()
        copies.append((a, b))
    attn = near_ref[...].astype(F32) + far_ref[...].astype(F32)
    middle = rows_ref[...].astype(F32) + attn
    unit2, scale2 = unit_rows(middle)
    normed = (unit2 * gains_ref[1:2, :]).astype(BF)
    normed_ref[...] = normed
    mlp = jnp.zeros_like(middle)
    for i in range(4):
        copies[i][0].wait()
        act, slope = gelu_pair(dot(normed, up_v[i]))
        act = act.astype(BF)
        act_ref[i] = act
        slope_v[i] = slope
        copies[i][1].wait()
        mlp = mlp + dot(act, down_v[i])
    unit3, scale3 = unit_rows(middle + mlp)
    gain3 = gains_ref[2:3, :]
    result_ref[...] = unit3 * gain3
    cot = cot_ref[...].astype(F32)
    vec_ref[1:2, :] = jnp.sum(cot * unit3, axis=0, keepdims=True)
    d_final = norm_back(unit3, scale3, gain3, cot)
    d_mlp = d_final.astype(BF)
    d_mlp_ref[...] = d_mlp
    d_normed = jnp.zeros_like(middle)
    for i in range(4):
        d_pre = (dot_nt(d_mlp, down_v[i]) * slope_v[i]).astype(BF)
        d_pre_ref[i] = d_pre
        d_normed = d_normed + dot_nt(d_pre, up_v[i])
    vec_ref[0:1, :] = jnp.sum(d_normed * unit2, axis=0, keepdims=True)
    d_mid = d_final + norm_back(unit2, scale2, gains_ref[1:2, :], d_normed)
    d_mid_ref[...] = d_mid
    d_mid_low_ref[...] = d_mid.astype(BF)


def mlp_pass(rows, near, far, cot, gains, ups, downs):
    own, d = rows.shape
    hidden = ups[0].shape[1]
    wide, low = shape((own, d), F32), shape((own, d), BF)
    packed = shape((4, own, hidden), BF)
    return pl.pallas_call(
        mlp_kernel,
        out_shape=(wide, wide, low, low, low, packed, packed, shape((2, d), F32)),
        in_specs=[VM] * 5 + [HB] * 8,
        out_specs=(VM,) * 8,
        scratch_shapes=[
            pltpu.VMEM((4, d, hidden), BF),
            pltpu.VMEM((4, hidden, d), BF),
            pltpu.VMEM((4, own, hidden), F32),
            pltpu.SemaphoreType.DMA((8,)),
        ],
        compiler_params=params(60),
        name="dense_mlp",
    )(rows, near, far, cot, gains, *ups, *downs)


def attention_back_kernel(
    heads, width, block, info, g0, g1, g2, g3, q_ref, k_ref, v_ref, mixed_ref, lse_ref, mix_ref,
    qkv_ref, sel_ref, d_qkv_ref, keep_ref, send_ref, qs, ds, dq_acc, dk_acc, dv_acc,
):
    tensor, low = info[0], info[2]
    own = g0.shape[0]
    cols = heads * width
    total = k_ref.shape[0]
    lane = lanes(own, PAD)
    zero = jnp.zeros((own, PAD), BF)
    for r, grad in enumerate((g0, g1, g2, g3)):
        at = pl.multiple_of(jnp.bitwise_xor(tensor, r) * own, own)
        span = pl.ds(at, own)
        d_mixed = dot_nt(grad[...], mix_ref[...]).astype(BF)
        inner = d_mixed.astype(F32) * mixed_ref[span, :].astype(F32)
        q = q_ref[span, :]
        lse = lse_ref[span, :]
        for h in range(heads):
            here = (lane >= h * width) & (lane < (h + 1) * width)
            delta = -jnp.sum(jnp.where(here, inner, 0.0), axis=-1, keepdims=True)
            row_lse = -jnp.sum(jnp.where(lanes(own, 128) == h, lse, 0.0), axis=-1, keepdims=True)
            left = jnp.where(here | (lane == cols + 3), q, zero)
            right = jnp.where(here, d_mixed, zero)
            for p, (a, b) in enumerate(zip(three_pieces(row_lse), three_pieces(delta))):
                left = jnp.where(lane == cols + p, a, left)
                right = jnp.where(lane == cols + p, b, right)
            qs[h, span, :] = left
            ds[h, span, :] = right
    dq_acc[...] = jnp.zeros_like(dq_acc)
    lane_k = lanes(block, PAD)
    allowed = subs(block, block) <= lanes(block, block)
    for j in range(total // block):
        first = j * block
        k, v = k_ref[first : first + block, :], v_ref[first : first + block, :]
        dk_acc[...] = jnp.zeros_like(dk_acc)
        dv_acc[...] = jnp.zeros_like(dv_acc)

        def one_head(h, carry):
            qh, dh = qs[h, first:, :], ds[h, first:, :]
            scores = dot_nt(k, qh)
            d_probs = dot_nt(v, dh)
            head = jnp.where(allowed, scores[:, :block], NEGATIVE)
            probs = jnp.exp(head)
            if first + block < total:
                probs = jnp.concatenate([probs, jnp.exp(scores[:, block:])], 1)
            d_scores = (probs * d_probs).astype(BF)
            dv_acc[...] += dot(probs.astype(BF), dh)
            dk_acc[...] += dot(d_scores, qh)
            kh = jnp.where(
                (lane_k >= h * width) & (lane_k < (h + 1) * width), k, jnp.zeros_like(k)
            )
            dq_acc[first:, :] += dot_tn(d_scores, kh)
            return carry

        lax.fori_loop(0, heads, one_head, 0)
        d_qkv_ref[1, first : first + block, :] = dk_acc[:, :cols].astype(BF)
        d_qkv_ref[2, first : first + block, :] = dv_acc[:, :cols].astype(BF)
    d_qkv_ref[0] = (dq_acc[:, :cols] * width ** (-0.5)).astype(BF)
    pick = sel_ref.shape[0]
    table = (sel_ref[...] == lanes(pick, total)).astype(F32).astype(BF)
    part = jnp.zeros((pick, qkv_ref.shape[1]), F32)
    for i in range(3):
        part = part + dot_nt(dot(table, d_qkv_ref[i]).astype(BF), qkv_ref[i][:, :cols])
    half = pick // 2
    keep_ref[...] = jnp.where(low == 0, part[:half], part[half:]).astype(BF)
    send_ref[...] = jnp.where(low == 0, part[half:], part[:half]).astype(BF)


def attention_back(info, grads, q, k, v, mixed, lse, mix_w, qkv_w, sel_col, heads, width, block=256):
    own, d = grads[0].shape
    total = k.shape[0] * k.shape[1]
    flat = lambda a: a.reshape(total, PAD)
    half = shape((sel_col.shape[0] // 2, d), BF)
    return pl.pallas_call(
        functools.partial(attention_back_kernel, heads, width, block),
        out_shape=(shape((3, total, heads * width), BF), half, half),
        in_specs=[SM] + [VM] * 12,
        out_specs=(VM,) * 3,
        scratch_shapes=[
            pltpu.VMEM((heads, total, PAD), BF),
            pltpu.VMEM((heads, total, PAD), BF),
            pltpu.VMEM((total, PAD), F32),
            pltpu.VMEM((block, PAD), F32),
            pltpu.VMEM((block, PAD), F32),
        ],
        compiler_params=params(60),
        name="attention_back",
    )(info, *grads, flat(q), flat(k), flat(v), mixed, lse, mix_w, qkv_w, sel_col)


def spread_back_kernel(cols, info, d_ref, qkv_ref, out_ref):
    total = dot_nt(d_ref[0, 0], qkv_ref[0][:, :cols])
    for i in (1, 2):
        total = total + dot_nt(d_ref[i, 0], qkv_ref[i][:, :cols])
    out_ref[0] = total.astype(BF)


def spread_back(info, d_qkv, qkv_w, count):
    _, total, cols = d_qkv.shape
    own = total // count
    d = qkv_w.shape[1]
    return pl.pallas_call(
        functools.partial(spread_back_kernel, cols),
        out_shape=shape((count, own, d), BF),
        grid_spec=pltpu.PrefetchScalarGridSpec(
            num_scalar_prefetch=1,
            grid=(count,),
            in_specs=[
                pl.BlockSpec((3, 1, own, cols), lambda a, info: (0, a, 0, 0)),
                pl.BlockSpec(qkv_w.shape, lambda a, info: (0, 0, 0)),
            ],
            out_specs=pl.BlockSpec(
                (1, own, d), lambda a, info: (jnp.bitwise_xor(a, info[0]), 0, 0)
            ),
        ),
        compiler_params=params(grid=1),
        name="spread_back",
    )(info, d_qkv.reshape(3, count, own, cols), qkv_w)


def rows_back_kernel(near_ref, far_ref, rows_ref, d_mid_ref, gains_ref, d_rows_ref, vec_ref):
    d_normed = near_ref[...].astype(F32) + far_ref[...].astype(F32)
    unit, scale = unit_rows(rows_ref[...].astype(F32))
    vec_ref[...] = jnp.sum(d_normed * unit, axis=0, keepdims=True)
    d_rows = d_mid_ref[...] + norm_back(unit, scale, gains_ref[0:1, :], d_normed)
    d_rows_ref[...] = d_rows.astype(BF)


def rows_back(near, far, rows, d_mid, gains):
    own, d = rows.shape
    return pl.pallas_call(
        rows_back_kernel,
        out_shape=(shape((own, d), BF), shape((1, d), F32)),
        in_specs=[VM] * 5,
        out_specs=(VM, VM),
        compiler_params=params(),
        name="rows_back",
    )(near, far, rows, d_mid, gains)


def sel_back_kernel(
    near_ref, far_ref, picked_ref, upd_ref, mid_near, mid_far, gains_ref, out_ref
):
    d_normed = near_ref[...].astype(F32) + far_ref[...].astype(F32)
    rows = (picked_ref[...].astype(F32) + upd_ref[...].astype(F32)).astype(BF).astype(F32)
    unit, scale = unit_rows(rows)
    d_mid = mid_near[...].astype(F32) + mid_far[...].astype(F32)
    out_ref[...] = (d_mid + norm_back(unit, scale, gains_ref[0:1, :], d_normed)).astype(BF)


def sel_back(near, far, picked, upd, mid_near, mid_far, gains):
    return pl.pallas_call(
        sel_back_kernel,
        out_shape=shape(near.shape, BF),
        in_specs=[VM] * 7,
        out_specs=VM,
        compiler_params=params(),
        name="sel_back",
    )(near, far, picked, upd, mid_near, mid_far, gains)


def mid_pick_kernel(info, rows_ref, sel_ref, keep_ref, send_ref):
    tensor, low = info[0], info[2]
    own = rows_ref.shape[0]
    pick = sel_ref.shape[0]
    table = (sel_ref[...] == lanes(pick, own) + tensor * own).astype(F32).astype(BF)
    part = dot(table, rows_ref[...])
    half = pick // 2
    keep_ref[...] = jnp.where(low == 0, part[:half], part[half:]).astype(BF)
    send_ref[...] = jnp.where(low == 0, part[half:], part[:half]).astype(BF)


def mid_pick(info, rows, sel_col):
    out = shape((sel_col.shape[0] // 2, rows.shape[1]), BF)
    return pl.pallas_call(
        mid_pick_kernel,
        out_shape=(out, out),
        in_specs=[SM, VM, VM],
        out_specs=(VM, VM),
        compiler_params=params(),
        name="mid_pick",
    )(info, rows, sel_col)


def add(a, b):
    return (a.astype(F32) + b.astype(F32)).astype(BF)


def core_sum(keep, send):
    return add(keep, swap(send, "tensor", 1))


def whole_sum(keep, send):
    near = core_sum(keep, send)
    return add(near, swap(near, "tensor", 2))


def owner_sum(parts):
    sent = swap(jnp.stack([parts[1], parts[3]]), "tensor", 1)
    far = add(parts[2], sent[1])
    near = add(parts[0], sent[0])
    return near, swap(far, "tensor", 2)


def body(
    tokens, qkv_weight, out_weight, up_weight, down_weight, vectors, lengths, selected, cotangent
):
    section = lax.axis_index("section")
    tensor = lax.axis_index("tensor")
    group = lax.axis_size("dp")
    heads = HEADS // lax.axis_size("tensor")
    low = tensor & 1
    info = jnp.stack([tensor, section, low, lengths[section]]).astype(jnp.int32)
    is_dense = section == 1
    gains = vectors[0]
    qkv_w, mix_w, up_w, down_w = qkv_weight[0], out_weight[0], up_weight[0], down_weight[0]
    cols = qkv_w.shape[2]
    width = cols // heads
    sel_col = selected[:, :, None]
    sel_row = selected[:, None, :]
    my_sel = lax.dynamic_index_in_dim(selected, section, 0, keepdims=False)
    my_col, my_row = my_sel[:, None], my_sel[None, :]

    picked_half = whole_sum(*pick_rows(info, tokens, sel_col))
    picked_other = swap(picked_half, "tensor", 1)

    def dense(own):
        return jnp.where(is_dense, own, hop(own, 1, 0))

    d_gains = dense(gains)
    d_qkv_w = jnp.pad(dense(qkv_w), ((0, 0), (0, 0), (0, PAD - cols)))
    d_mix_w = jnp.pad(dense(mix_w), ((0, PAD - cols), (0, 0)))

    def everywhere(block):
        far = swap(block, "tensor", 2)
        return [block, swap(block, "tensor", 1), far, swap(far, "tensor", 1)]

    my_tokens = lax.dynamic_index_in_dim(tokens, section, 0, keepdims=False)
    toks = everywhere(my_tokens)
    ups = everywhere(dense(up_w))
    downs = everywhere(dense(down_w))

    picked, normed, q, k, v, mixed, keep, send = routed_attn(
        info, picked_half, picked_other, gains, qkv_w, mix_w, heads
    )
    attn_half = whole_sum(keep, send)
    attn_other = swap(attn_half, "tensor", 1)
    attn, normed2, act, slope, keep, send = routed_mlp(
        info, picked, attn_half, attn_other, gains, up_w, down_w
    )
    near = core_sum(keep, send)
    both_half, update_half = make_update(
        picked_half, attn_half, near, swap(near, "tensor", 2), gains
    )
    both_other = swap(both_half, "tensor", 1)
    arrived = hop(update_half[1], 0, 1)
    my_update = jnp.where(is_dense, arrived, update_half[0])
    my_update_other = swap(my_update, "tensor", 1)

    rows, d_normed_rows, dq_in, dk_in, dv_in = project(
        info, toks, my_update, my_update_other, my_row, d_gains, d_qkv_w, heads, width
    )
    parts, d_mixed_rows, lse = attention(info, dq_in, dk_in, dv_in, d_mix_w, heads, width)
    near, far = owner_sum(parts)
    my_cot = lax.dynamic_index_in_dim(cotangent, section, 0, keepdims=False)
    result, d_mid, d_mid_low, m_normed, m_grad, m_act, m_pre, m_vec = mlp_pass(
        rows, near, far, my_cot, d_gains, ups, downs
    )
    grads = everywhere(d_mid_low)
    mid_keep, mid_send = mid_pick(info, d_mid_low, my_col)
    mid_near = core_sum(mid_keep, mid_send)
    mid_far = swap(mid_near, "tensor", 2)
    sent_result = hop(result.astype(BF), 0, 1)

    up_parts = jnp.einsum("rd,frc->fdc", m_normed, m_pre, preferred_element_type=F32).astype(BF)
    down_parts = jnp.einsum("frc,rd->fcd", m_act, m_grad, preferred_element_type=F32).astype(BF)

    d_qkv, keep, send = attention_back(
        info, grads, dq_in, dk_in, dv_in, d_mixed_rows, lse, d_mix_w, d_qkv_w, my_col, heads, width
    )
    near = core_sum(keep, send)
    far = swap(near, "tensor", 2)
    my_picked = lax.dynamic_index_in_dim(picked_half, section, 0, keepdims=False)
    my_d_sel = sel_back(near, far, my_picked, my_update, mid_near, mid_far, d_gains)
    d_sel_half = jnp.stack([my_d_sel, hop(my_d_sel, 1, 0)])
    d_sel_other = swap(d_sel_half, "tensor", 1)

    row_parts = spread_back(info, d_qkv, d_qkv_w, 4)
    near, far = owner_sum(row_parts)
    d_rows, row_vec = rows_back(near, far, rows, d_mid, d_gains)
    flat_normed = d_normed_rows.reshape(-1, d_normed_rows.shape[2])
    qkv_part = jnp.einsum("rd,krc->kdc", flat_normed, d_qkv, preferred_element_type=F32).astype(BF)
    own_count = rows.shape[0]
    mix_part = jnp.zeros((PAD, rows.shape[1]), F32)
    for r in range(4):
        block = lax.dynamic_slice_in_dim(d_mixed_rows, (tensor ^ r) * own_count, own_count, 0)
        mix_part = mix_part + jnp.einsum("rc,rd->cd", block, grads[r], preferred_element_type=F32)
    mix_part = mix_part[:cols].astype(BF)
    near, far = owner_sum(up_parts)
    up_part = add(near, far)
    near, far = owner_sum(down_parts)
    down_part = add(near, far)

    def over_groups(parts):
        qkv_g, mix_g, up_g, down_g = parts
        return (
            lax.psum_scatter(qkv_g, "dp", scatter_dimension=1, tiled=True),
            lax.psum_scatter(mix_g, "dp", scatter_dimension=1, tiled=True),
            lax.psum_scatter(up_g, "dp", scatter_dimension=0, tiled=True),
            lax.psum_scatter(down_g, "dp", scatter_dimension=1, tiled=True),
        )

    dense_sums = over_groups((qkv_part, mix_part, up_part, down_part))
    dense_far = [hop(part, 0, 1) for part in dense_sums]

    d_sel, r_d_mlp, r_d_pre, gain_two, keep, send = routed_back_mlp(
        info, d_sel_half, d_sel_other, picked, attn, gains, slope, up_w, down_w
    )
    half = whole_sum(keep, send)
    other = swap(half, "tensor", 1)
    r_d_mid, r_d_low, r_d_qkv, r_vec, keep, send = routed_back_attn(
        info, half, other, d_sel, picked, attn, both_half, both_other, gains, q, k, v,
        qkv_w, mix_w, heads,
    )
    half = whole_sum(keep, send)
    other = swap(half, "tensor", 1)
    r_up = jnp.einsum("rd,rc->dc", normed2, r_d_pre, preferred_element_type=F32).astype(BF)
    r_down = jnp.einsum("rc,rd->cd", act, r_d_mlp, preferred_element_type=F32).astype(BF)
    r_qkv = jnp.einsum("rd,krc->kdc", normed, r_d_qkv, preferred_element_type=F32).astype(BF)
    r_mix = jnp.einsum("rc,rd->cd", mixed, r_d_low, preferred_element_type=F32).astype(BF)
    routed_sums = over_groups((r_qkv, r_mix, r_up, r_down))

    far_rows = jnp.where(is_dense, sent_result, hop(d_rows, 1, 0))
    combined = finish(
        info, half, other, r_d_mid, picked, gains, sel_row, d_rows, far_rows, result
    )
    final_grads = [
        jnp.where(is_dense, own.astype(F32) + far.astype(F32), routed.astype(F32))
        for own, far, routed in zip(dense_sums, dense_far, routed_sums)
    ]

    vecs = jnp.concatenate([r_vec[0:1], gain_two, r_vec[1:2], row_vec, m_vec], 0)
    for axis in ("tensor", "dp"):
        bit = 1
        while bit < lax.axis_size(axis):
            vecs = vecs + swap(vecs, axis, bit)
            bit *= 2
    dense_vecs = vecs[3:] + hop(vecs[3:], 0, 1)
    vecs = jnp.where(is_dense, dense_vecs, vecs[:3])
    share = vecs.shape[1] // group
    vecs = lax.dynamic_slice_in_dim(vecs, lax.axis_index("dp") * share, share, 1)
    return (
        combined[None],
        final_grads[0][None],
        final_grads[1][None],
        final_grads[2][None],
        final_grads[3][None],
        vecs[None],
    )


def solution(mesh):
    placed = (
        P("dp", "tensor", None),
        P("section", None, None, "tensor"),
        P("section", "tensor", None),
        P("section", None, "tensor"),
        P("section", "tensor", None),
        P("section", None, None),
        P("dp"),
        P("dp", None),
        P("dp", "tensor", None),
    )
    return jax.shard_map(
        body,
        mesh=mesh,
        in_specs=placed,
        out_specs=(
            P("section", "dp", "tensor", None),
            P("section", None, "dp", "tensor"),
            P("section", "tensor", "dp"),
            P("section", "dp", "tensor"),
            P("section", "tensor", "dp"),
            P("section", None, "dp"),
        ),
        check_vma=False,
    )
```

```python
import functools

import jax
import jax.numpy as jnp
from jax import lax
from jax.experimental import pallas as pl
from jax.experimental.pallas import tpu as pltpu
from jax.sharding import PartitionSpec as P

HEADS = 12
EPSILON = 1e-06
NEGATIVE = -1e30
BF = jnp.bfloat16
F32 = jnp.float32
PAD = 256
MIB = 1 << 20


def swap(block, axis, bit):
    count = lax.axis_size(axis)
    return lax.ppermute(block, axis, [(i, i ^ bit) for i in range(count)])


def hop(block, source, target):
    return lax.ppermute(block, "section", [(source, target)])


def dot(left, right):
    return lax.dot_general(left, right, (((1,), (0,)), ((), ())), preferred_element_type=F32)


def dot_nt(left, right):
    return lax.dot_general(left, right, (((1,), (1,)), ((), ())), preferred_element_type=F32)


def dot_tn(left, right):
    return lax.dot_general(left, right, (((0,), (0,)), ((), ())), preferred_element_type=F32)


def unit_rows(values):
    scale = lax.rsqrt(jnp.mean(values * values, axis=-1, keepdims=True) + EPSILON)
    return values * scale, scale


def norm_back(unit, scale, gain, grad):
    e = grad * gain
    return scale * (e - unit * jnp.mean(e * unit, axis=-1, keepdims=True))


def gelu_pair(x):
    c = 0.7978845608028654
    a = 0.044715
    xx = x * x
    th = jnp.tanh(c * (x + a * (x * xx)))
    half = 0.5 * (1.0 + th)
    slope = half + (0.5 * x) * (1.0 - th * th) * (c * (1.0 + (3.0 * a) * xx))
    return x * half, slope


def lanes(rows, width):
    return lax.broadcasted_iota(jnp.int32, (rows, width), 1)


def subs(rows, width):
    return lax.broadcasted_iota(jnp.int32, (rows, width), 0)


def head_of(values, lane, head, width):
    zero = jnp.zeros_like(values)
    return jnp.where((lane >= head * width) & (lane < (head + 1) * width), values, zero)


def three_pieces(column):
    first = column.astype(BF)
    rest = column - first.astype(F32)
    second = rest.astype(BF)
    third = (rest - second.astype(F32)).astype(BF)
    return first, second, third


def params(limit=56, grid=None):
    if grid is None:
        return pltpu.CompilerParams(vmem_limit_bytes=limit * MIB)
    return pltpu.CompilerParams(
        vmem_limit_bytes=limit * MIB, dimension_semantics=("arbitrary",) * grid
    )


def cost(us):
    return pl.CostEstimate(
        flops=int(us * 1e8), bytes_accessed=int(us * 3.3e6), transcendentals=0
    )


def after(value, *others):
    return lax.optimization_barrier((value,) + others)[0]


VM = pl.BlockSpec(memory_space=pltpu.VMEM)
SM = pl.BlockSpec(memory_space=pltpu.SMEM)
HB = pl.BlockSpec(memory_space=pl.ANY)


def shape(dims, dtype):
    return jax.ShapeDtypeStruct(dims, dtype)


def halves_out(partial, low, keep_ref, send_ref):
    pick = partial.shape[0] // 2
    half = pick // 2
    for s in range(2):
        first = partial[s * pick : s * pick + half]
        second = partial[s * pick + half : (s + 1) * pick]
        keep_ref[s] = jnp.where(low == 0, first, second).astype(BF)
        send_ref[s] = jnp.where(low == 0, second, first).astype(BF)


def halves_in(own_ref, other_ref, low):
    parts = []
    for s in range(2):
        own, other = own_ref[s].astype(F32), other_ref[s].astype(F32)
        parts.append(jnp.where(low == 0, own, other))
        parts.append(jnp.where(low == 0, other, own))
    return jnp.concatenate(parts, 0)


def pick_kernel(rows_ref, sel_ref, keep_ref, send_ref):
    tensor = lax.axis_index("tensor")
    own = rows_ref.shape[1]
    pick = sel_ref.shape[1]
    parts = []
    for s in range(2):
        table = (sel_ref[s : s + 1, :] == subs(own, pick) + tensor * own).astype(F32).astype(BF)
        parts.append(dot_tn(table, rows_ref[s]))
    halves_out(jnp.concatenate(parts, 0), tensor & 1, keep_ref, send_ref)


def pick_rows(rows, selected):
    _, _, d = rows.shape
    out = shape((2, selected.shape[1] // 2, d), BF)
    return pl.pallas_call(
        pick_kernel,
        out_shape=(out, out),
        in_specs=[VM, VM],
        out_specs=(VM, VM),
        compiler_params=params(),
        cost_estimate=cost(3),
        name="pick",
    )(rows, selected)


def routed_attn_kernel(
    heads, info, own_ref, other_ref, gains_ref, qkv_ref, mix_ref,
    picked_ref, normed_ref, q_ref, k_ref, v_ref, mixed_ref, keep_ref, send_ref,
):
    low = info[2]
    picked = halves_in(own_ref, other_ref, low)
    picked_ref[...] = picked.astype(BF)
    unit, _ = unit_rows(picked)
    normed = (unit * gains_ref[0:1, :]).astype(BF)
    normed_ref[...] = normed
    width = qkv_ref.shape[1] // heads
    q = dot_nt(normed, qkv_ref[0]).astype(BF)
    k = dot_nt(normed, qkv_ref[1]).astype(BF)
    v = dot_nt(normed, qkv_ref[2]).astype(BF)
    q = (q.astype(F32) * width ** (-0.5)).astype(BF)
    q_ref[...] = q
    k_ref[...] = k
    v_ref[...] = v
    pick = picked.shape[0] // 2
    lane = lanes(pick, heads * width)
    allowed = lanes(pick, pick) <= subs(pick, pick)
    parts = []
    for s in range(2):
        span = slice(s * pick, (s + 1) * pick)
        total = jnp.zeros((pick, heads * width), F32)
        for h in range(heads):
            scores = dot_nt(head_of(q[span], lane, h, width), k[span])
            scores = jnp.where(allowed, scores, NEGATIVE)
            expos = jnp.exp(scores - jnp.max(scores, axis=-1, keepdims=True))
            probs = expos / jnp.sum(expos, axis=-1, keepdims=True)
            total = total + dot(probs.astype(BF), head_of(v[span], lane, h, width))
        parts.append(total.astype(BF))
    mixed = jnp.concatenate(parts, 0)
    mixed_ref[...] = mixed
    halves_out(dot(mixed, mix_ref[...]), low, keep_ref, send_ref)


def routed_attn(info, own, other, gains, qkv_w, mix_w, heads):
    _, half, d = own.shape
    rows = 4 * half
    cols = qkv_w.shape[1]
    part = shape((2, half, d), BF)
    wide, narrow = shape((rows, d), BF), shape((rows, cols), BF)
    return pl.pallas_call(
        functools.partial(routed_attn_kernel, heads),
        out_shape=(wide, wide, narrow, narrow, narrow, narrow, part, part),
        in_specs=[SM] + [VM] * 5,
        out_specs=(VM,) * 8,
        compiler_params=params(),
        cost_estimate=cost(5),
        name="routed_attn",
    )(info, own, other, gains, qkv_w, mix_w)


def routed_mlp_kernel(
    info, picked_ref, own_ref, other_ref, gains_ref, up_ref, down_ref,
    attn_ref, normed_ref, act_ref, slope_ref, keep_ref, send_ref,
):
    low = info[2]
    attn = halves_in(own_ref, other_ref, low)
    attn_ref[...] = attn.astype(BF)
    unit, _ = unit_rows(picked_ref[...].astype(F32) + attn)
    normed = (unit * gains_ref[1:2, :]).astype(BF)
    normed_ref[...] = normed
    act, slope = gelu_pair(dot(normed, up_ref[...]))
    act = act.astype(BF)
    act_ref[...] = act
    slope_ref[...] = slope
    halves_out(dot(act, down_ref[...]), low, keep_ref, send_ref)


def routed_mlp(info, picked, own, other, gains, up_w, down_w):
    rows, d = picked.shape
    hidden = up_w.shape[1]
    part = shape((2, rows // 4, d), BF)
    return pl.pallas_call(
        routed_mlp_kernel,
        out_shape=(
            shape((rows, d), BF), shape((rows, d), BF), shape((rows, hidden), BF),
            shape((rows, hidden), F32), part, part,
        ),
        in_specs=[SM] + [VM] * 6,
        out_specs=(VM,) * 6,
        compiler_params=params(),
        cost_estimate=cost(6),
        name="routed_mlp",
    )(info, picked, own, other, gains, up_w, down_w)


def update_kernel(picked_ref, attn_ref, mlp_ref, mlp2_ref, gains_ref, both_ref, update_ref):
    d = picked_ref.shape[2]
    weight = gains_ref[2:3, :] * d ** (-0.5)
    for s in range(2):
        router = jnp.sum(picked_ref[s].astype(F32) * weight, axis=-1, keepdims=True)
        both = attn_ref[s].astype(F32) + (mlp_ref[s].astype(F32) + mlp2_ref[s].astype(F32))
        both_ref[s] = both.astype(BF)
        update_ref[s] = (router * both).astype(BF)


def make_update(picked_half, attn_half, mlp_half, mlp_far, gains):
    out = shape(picked_half.shape, BF)
    return pl.pallas_call(
        update_kernel,
        out_shape=(out, out),
        in_specs=[VM] * 5,
        out_specs=(VM, VM),
        compiler_params=params(),
        cost_estimate=cost(2.5),
        name="update",
    )(picked_half, attn_half, mlp_half, mlp_far, gains)


def routed_back_mlp_kernel(
    info, sel_own, sel_back, sel_other, picked_ref, attn_ref, gains_ref, slope_ref, up_ref, down_ref,
    d_sel_ref, d_mlp_ref, d_pre_ref, gain_ref, keep_ref, send_ref,
):
    low = info[2]
    d = picked_ref.shape[1]
    parts = []
    for s, own in enumerate((sel_own[...], sel_back[...])):
        other = sel_other[s]
        parts += [jnp.where(low == 0, own, other), jnp.where(low == 0, other, own)]
    d_sel = jnp.concatenate(parts, 0).astype(F32)
    d_sel_ref[...] = d_sel
    picked = picked_ref[...].astype(F32)
    router = jnp.sum(picked * (gains_ref[2:3, :] * d ** (-0.5)), axis=-1, keepdims=True)
    d_mlp = (router * d_sel).astype(BF)
    d_mlp_ref[...] = d_mlp
    d_pre = (dot_nt(d_mlp, down_ref[...]) * slope_ref[...]).astype(BF)
    d_pre_ref[...] = d_pre
    d_normed = dot_nt(d_pre, up_ref[...])
    unit, _ = unit_rows(picked + attn_ref[...].astype(F32))
    gain_ref[...] = jnp.sum(d_normed * unit, axis=0, keepdims=True)
    halves_out(d_normed, low, keep_ref, send_ref)


def routed_back_mlp(info, sel_own, sel_back, sel_other, picked, attn, gains, slope, up_w, down_w):
    rows, d = picked.shape
    hidden = up_w.shape[1]
    part = shape((2, rows // 4, d), BF)
    return pl.pallas_call(
        routed_back_mlp_kernel,
        out_shape=(
            shape((rows, d), F32), shape((rows, d), BF), shape((rows, hidden), BF),
            shape((1, d), F32), part, part,
        ),
        in_specs=[SM] + [VM] * 9,
        out_specs=(VM,) * 6,
        compiler_params=params(),
        cost_estimate=cost(6),
        name="routed_back_mlp",
    )(info, sel_own, sel_back, sel_other, picked, attn, gains, slope, up_w, down_w)


def routed_back_attn_kernel(
    heads, info, own_ref, other_ref, d_sel_ref, picked_ref, attn_ref, both_own, both_other,
    gains_ref, q_ref, k_ref, v_ref, qkv_ref, mix_ref,
    d_mid_ref, d_low_ref, d_qkv_ref, vec_ref, keep_ref, send_ref,
):
    low = info[2]
    rows, d = picked_ref.shape
    d_normed2 = halves_in(own_ref, other_ref, low)
    picked = picked_ref[...].astype(F32)
    d_sel = d_sel_ref[...]
    router_row = gains_ref[2:3, :] * d ** (-0.5)
    router = jnp.sum(picked * router_row, axis=-1, keepdims=True)
    unit2, scale2 = unit_rows(picked + attn_ref[...].astype(F32))
    d_mid = norm_back(unit2, scale2, gains_ref[1:2, :], d_normed2)
    both = halves_in(both_own, both_other.at[2:], low)
    d_router = jnp.sum(d_sel * both, axis=-1, keepdims=True)
    d_mid_ref[...] = d_mid + d_router * router_row
    d_weight = jnp.sum(picked * d_router, axis=0, keepdims=True) * d ** (-0.5)
    vec_ref[1:2, :] = jnp.where(info[0] == 0, d_weight, jnp.zeros_like(d_weight))
    d_low = (router * d_sel + d_mid).astype(BF)
    d_low_ref[...] = d_low
    d_mixed = dot_nt(d_low, mix_ref[...]).astype(BF)
    width = qkv_ref.shape[1] // heads
    pick = rows // 2
    lane = lanes(pick, heads * width)
    allowed = subs(pick, pick) <= lanes(pick, pick)
    dq_parts, dk_parts, dv_parts = [], [], []
    for s in range(2):
        span = slice(s * pick, (s + 1) * pick)
        q, k, v, dm = q_ref[span, :], k_ref[span, :], v_ref[span, :], d_mixed[span]
        dq = jnp.zeros((pick, heads * width), F32)
        dk, dv = dq, dq
        for h in range(heads):
            qh, kh = head_of(q, lane, h, width), head_of(k, lane, h, width)
            dh = head_of(dm, lane, h, width)
            scores = jnp.where(allowed, dot_nt(k, qh), NEGATIVE)
            expos = jnp.exp(scores - jnp.max(scores, axis=0, keepdims=True))
            probs = expos / jnp.sum(expos, axis=0, keepdims=True)
            d_probs = dot_nt(v, dh)
            inner = jnp.sum(probs * d_probs, axis=0, keepdims=True)
            d_scores = (probs * (d_probs - inner)).astype(BF)
            dv = dv + dot(probs.astype(BF), dh)
            dk = dk + dot(d_scores, qh)
            dq = dq + dot_tn(d_scores, kh)
        dq_parts.append(dq * width ** (-0.5))
        dk_parts.append(dk)
        dv_parts.append(dv)
    d_normed = jnp.zeros((rows, d), F32)
    for i, parts in enumerate((dq_parts, dk_parts, dv_parts)):
        whole = jnp.concatenate(parts, 0).astype(BF)
        d_qkv_ref[i] = whole
        d_normed = d_normed + dot(whole, qkv_ref[i])
    unit, _ = unit_rows(picked)
    vec_ref[0:1, :] = jnp.sum(d_normed * unit, axis=0, keepdims=True)
    halves_out(d_normed, low, keep_ref, send_ref)


def routed_back_attn(
    info, own, other, d_sel, picked, attn, both_own, both_other, gains, q, k, v, qkv_w, mix_w, heads
):
    rows, d = picked.shape
    part = shape((2, rows // 4, d), BF)
    return pl.pallas_call(
        functools.partial(routed_back_attn_kernel, heads),
        out_shape=(
            shape((rows, d), F32), shape((rows, d), BF), shape((3,) + q.shape, BF),
            shape((2, d), F32), part, part,
        ),
        in_specs=[SM] + [VM] * 13,
        out_specs=(VM,) * 6,
        compiler_params=params(),
        cost_estimate=cost(8),
        name="routed_back_attn",
    )(info, own, other, d_sel, picked, attn, both_own, both_other, gains, q, k, v, qkv_w, mix_w)


def finish_kernel(
    info, own_ref, other_ref, d_mid_ref, picked_ref, gains_ref, sel_ref,
    d_rows_ref, far_ref, sent_ref, result_ref, out_ref,
):
    tensor, section, low = info[0], info[1], info[2]
    own = d_rows_ref.shape[0]
    pick = sel_ref.shape[1]

    @pl.when(section == 0)
    def _():
        d_normed = halves_in(own_ref, other_ref, low)
        unit, scale = unit_rows(picked_ref[...].astype(F32))
        d_picked = d_mid_ref[...] + norm_back(unit, scale, gains_ref[0:1, :], d_normed)
        d_picked = d_picked.astype(BF)
        for s in range(2):
            table = (sel_ref[s : s + 1, :] == subs(own, pick) + tensor * own).astype(F32).astype(BF)
            base = (d_rows_ref if s == 0 else far_ref)[...].astype(F32)
            out_ref[s] = base + dot(table, d_picked[s * pick : (s + 1) * pick])

    @pl.when(section != 0)
    def _():
        out_ref[0] = sent_ref[...].astype(F32)
        out_ref[1] = result_ref[...]


def finish(info, own, other, d_mid, picked, gains, sel_row, d_rows, far, sent, result):
    rows, d = d_rows.shape
    return pl.pallas_call(
        finish_kernel,
        out_shape=shape((2, rows, d), F32),
        in_specs=[SM] + [VM] * 10,
        out_specs=VM,
        compiler_params=params(),
        cost_estimate=cost(6),
        name="finish",
    )(info, own, other, d_mid, picked, gains, sel_row, d_rows, far, sent, result)


def pack_kernel(gains_ref, qkv_ref, mix_ref, out_ref):
    cols, d = mix_ref.shape
    for n in range(3):
        out_ref[n * cols : (n + 1) * cols, :] = qkv_ref[n]
    out_ref[3 * cols : 4 * cols, :] = mix_ref[...]
    rows = subs(16, d)
    extra = jnp.zeros((16, d), F32)
    for n in range(3):
        for p, piece in enumerate(three_pieces(gains_ref[n : n + 1, :])):
            extra = jnp.where(rows == 3 * n + p, piece.astype(F32), extra)
    out_ref[4 * cols :, :] = extra.astype(BF)


def pack_weights(gains, qkv_w, mix_w):
    cols, d = mix_w.shape
    return pl.pallas_call(
        pack_kernel,
        out_shape=shape((4 * cols + 16, d), BF),
        in_specs=[VM] * 3,
        out_specs=VM,
        compiler_params=params(),
        cost_estimate=cost(2),
        name="pack",
    )(gains, qkv_w, mix_w)


def prepare_kernel(info, g0, q0, m0, far_ref, gains_ref, qkv_ref, mix_ref):
    cols = m0.shape[0]
    own = info[1] == 1
    extra = far_ref[4 * cols :, :].astype(F32)
    for n in range(3):
        far = (extra[3 * n : 3 * n + 1] + extra[3 * n + 1 : 3 * n + 2]) + extra[3 * n + 2 : 3 * n + 3]
        gains_ref[n : n + 1, :] = jnp.where(own, g0[n : n + 1, :], far)
    qkv_ref[...] = jnp.zeros_like(qkv_ref)
    for n in range(3):
        qkv_ref[n, :cols, :] = jnp.where(own, q0[n], far_ref[n * cols : (n + 1) * cols, :])
    mix_ref[...] = jnp.zeros_like(mix_ref)
    mix_ref[:cols, :] = jnp.where(own, m0[...], far_ref[3 * cols : 4 * cols, :])


def prepare(info, gains, qkv_w, mix_w, far):
    d = mix_w.shape[1]
    return pl.pallas_call(
        prepare_kernel,
        out_shape=(shape(gains.shape, F32), shape((3, PAD, d), BF), shape((PAD, d), BF)),
        in_specs=[SM] + [VM] * 4,
        out_specs=(VM,) * 3,
        compiler_params=params(),
        cost_estimate=cost(2),
        name="prepare",
    )(info, gains, qkv_w, mix_w, far)


def project_kernel(
    heads, width, info, tok0, tok1, tok2a, tok2b, tok3a, tok3b, upd_own, upd_other, sel_ref,
    gains_ref, qkv_ref, rows_ref, normed_ref, q_ref, k_ref, v_ref, buf,
):
    tensor, low, length = info[0], info[2], info[3]
    r = pl.program_id(0)
    own, d = buf.shape
    for i, tok in enumerate((tok0, tok1)):
        @pl.when(r == i)
        def _():
            buf[...] = tok[...]

    for i, tok_a, tok_b in ((2, tok2a, tok2b), (3, tok3a, tok3b)):
        @pl.when(r == i)
        def _():
            buf[: own // 2] = tok_a[...]
            buf[own // 2 :] = tok_b[...]

    place = jnp.bitwise_xor(r, tensor) * own
    pick = sel_ref.shape[1]
    first, second = upd_own[...], upd_other[...]
    update = jnp.concatenate(
        [jnp.where(low == 0, first, second), jnp.where(low == 0, second, first)], 0
    )
    sel = jnp.where(info[1] == 0, sel_ref[0:1, :], sel_ref[1:2, :])
    table = (sel == subs(own, pick) + place).astype(F32).astype(BF)
    rows = (buf[...].astype(F32) + dot(table, update)).astype(BF)

    @pl.when(r == 0)
    def _():
        rows_ref[...] = rows

    unit, _ = unit_rows(rows.astype(F32))
    normed = (unit * gains_ref[0:1, :]).astype(BF)
    normed_ref[0] = normed
    lane = lanes(own, PAD)
    cols = heads * width
    one, zero = jnp.float32(1), jnp.float32(0)
    q = dot_nt(normed, qkv_ref[0]).astype(BF).astype(F32) * width ** (-0.5)
    q_ref[0] = jnp.where(lane == cols + 3, one, q).astype(BF)
    key_at = subs(own, PAD) + place
    extra = jnp.where(lane < cols + 3, one, jnp.where(key_at < length, zero, NEGATIVE))
    k = dot_nt(normed, qkv_ref[1])
    k_ref[0] = jnp.where((lane >= cols) & (lane < cols + 4), extra, k).astype(BF)
    v = dot_nt(normed, qkv_ref[2])
    v_ref[0] = jnp.where((lane >= cols) & (lane < cols + 3), one, v).astype(BF)


def project(info, toks, upd_own, upd_other, sel, gains, qkv_w, heads, width, count):
    own, d = toks[0].shape
    full = lambda dims: pl.BlockSpec(dims, lambda r, info: (0,) * len(dims))
    placed = lambda w: pl.BlockSpec((1, own, w), lambda r, info: (jnp.bitwise_xor(r, info[0]), 0, 0))
    padded = shape((count, own, PAD), BF)
    return pl.pallas_call(
        functools.partial(project_kernel, heads, width),
        out_shape=(shape((own, d), BF), shape((count, own, d), BF), padded, padded, padded),
        grid_spec=pltpu.PrefetchScalarGridSpec(
            num_scalar_prefetch=1,
            grid=(count,),
            in_specs=[full(tok.shape) for tok in toks]
            + [full(upd_own.shape)] * 2
            + [full(sel.shape), full(gains.shape), full(qkv_w.shape)],
            out_specs=(full((own, d)), placed(d), placed(PAD), placed(PAD), placed(PAD)),
            scratch_shapes=[pltpu.VMEM((own, d), BF)],
        ),
        compiler_params=params(grid=1),
        cost_estimate=cost(9),
        name="project",
    )(info, *toks, upd_own, upd_other, sel, gains, qkv_w)


def attention_kernel(
    heads, width, base, per, info, q_ref, k_ref, v_ref, mix_ref,
    send_ref, keep_ref, mixed_ref, lse_ref,
):
    i = pl.program_id(0)
    block = q_ref.shape[1]
    cols = heads * width
    steps = k_ref.shape[0] // block
    place = jnp.bitwise_xor(base + 1 - i // per, info[0]) * per + i % per

    def run(step):
        span = (step + 1) * block
        q = q_ref[0]
        lane = lanes(block, PAD)
        total = jnp.zeros((block, PAD), F32)
        lse = jnp.zeros((block, 128), F32)
        zero = jnp.zeros_like(q)
        for h in range(heads):
            here = (lane >= h * width) & (lane < (h + 1) * width)
            qh = jnp.where(here | (lane == cols + 3), q, zero)
            scores = dot_nt(qh, k_ref[0:span, :])
            causal = lanes(block, block) <= subs(block, block)
            tail = jnp.where(causal, scores[:, span - block :], NEGATIVE)
            high = jnp.max(tail, axis=-1, keepdims=True)
            if step:
                high = jnp.maximum(high, jnp.max(scores[:, : span - block], axis=-1, keepdims=True))
            probs = jnp.exp(tail - high).astype(BF)
            if step:
                probs = jnp.concatenate(
                    [jnp.exp(scores[:, : span - block] - high).astype(BF), probs], 1
                )
            out = dot(probs, v_ref[0:span, :])
            norm = jnp.sum(jnp.where(lane == cols, out, 0.0), axis=-1, keepdims=True)
            total = jnp.where(here, out / norm, total)
            lse = jnp.where(lanes(block, 128) == h, high + jnp.log(norm), lse)
        lse_ref[0] = lse
        mixed = total.astype(BF)
        mixed_ref[0] = mixed
        part = dot(mixed, mix_ref[...]).astype(BF)

        @pl.when(i < per)
        def _():
            send_ref[...] = part

        @pl.when(i >= per)
        def _():
            keep_ref[...] = part

    for step in range(steps):
        @pl.when(place == step)
        def _():
            run(step)


def attention(info, q, k, v, mix_w, heads, width, base, block=256):
    count, own, _ = q.shape
    total = count * own
    d = mix_w.shape[1]
    per = own // block
    k, v = k.reshape(total, PAD), v.reshape(total, PAD)
    full = lambda dims: pl.BlockSpec(dims, lambda i, info: (0,) * len(dims))
    rel = lambda w: pl.BlockSpec((1, block, w), lambda i, info: (1 - i // per, i % per, 0))
    out = shape((own, d), BF)
    return pl.pallas_call(
        functools.partial(attention_kernel, heads, width, base, per),
        out_shape=(out, out, shape((2, own, PAD), BF), shape((2, own, 128), F32)),
        grid_spec=pltpu.PrefetchScalarGridSpec(
            num_scalar_prefetch=1,
            grid=(2 * per,),
            in_specs=[
                pl.BlockSpec(
                    (1, block, PAD),
                    lambda i, info: (
                        jnp.bitwise_xor(base + 1 - i // per, info[0]), i % per, 0,
                    ),
                ),
                full(k.shape), full(v.shape), full(mix_w.shape),
            ],
            out_specs=(
                pl.BlockSpec((block, d), lambda i, info: (jnp.minimum(i, per - 1), 0)),
                pl.BlockSpec((block, d), lambda i, info: (jnp.maximum(i - per, 0), 0)),
                rel(PAD), rel(128),
            ),
        ),
        compiler_params=params(grid=1),
        cost_estimate=cost(0.3),
        name="attention",
    )(info, q, k, v, mix_w)


def mlp_kernel(
    half, rows_ref, keep_ref, near_ref, far_ref, cot_ref, gains_ref,
    p0a, p0b, p1a, p1b, p2a, p2b, p3a, p3b,
    result_ref, low_ref, d_mid_ref, d_mid_low_ref, keep_out, send_out,
    vec_ref, up_v, down_v, slope_v, act_v, pre_v, rows_v, result_v, low_v, sems, out_sems,
):
    leaving = []

    def leave(src, dst):
        copy = pltpu.make_async_copy(src, dst, out_sems.at[len(leaving)])
        copy.start()
        leaving.append(copy)

    parity = lax.axis_index("dp") & 1
    first = pl.ds(pl.multiple_of(parity * half, half), half)
    second = pl.ds(pl.multiple_of((1 - parity) * half, half), half)
    copies = {}
    count = 0
    for i in range(4):
        for n, (name, dest) in enumerate((("up", up_v), ("down", down_v))):
            a, b = ((p0a, p0b), (p1a, p1b), (p2a, p2b), (p3a, p3b))[i]
            moves = [(a.at[n], dest.at[i, first, :]), (b.at[n], dest.at[i, second, :])]
            some = []
            for src, dst in moves:
                copy = pltpu.make_async_copy(src, dst, sems.at[count])
                copy.start()
                some.append(copy)
                count += 1
            copies[name, i] = some
    attn = keep_ref[...].astype(F32) + near_ref[...].astype(F32) + far_ref[...].astype(F32)
    middle = rows_ref[...].astype(F32) + attn
    unit2, scale2 = unit_rows(middle)
    normed = (unit2 * gains_ref[1:2, :]).astype(BF)
    rows_v[0] = normed
    leave(rows_v.at[0], send_out.at[4])
    mlp = jnp.zeros_like(middle)
    for i in range(4):
        for copy in copies["up", i]:
            copy.wait()
        act, slope = gelu_pair(dot(normed, up_v[i]))
        act = act.astype(BF)
        act_v[i] = act
        leave(act_v.at[i], (keep_out if i % 2 == 0 else send_out).at[i // 2])
        slope_v[i] = slope
        for copy in copies["down", i]:
            copy.wait()
        mlp = mlp + dot(act, down_v[i])
    unit3, scale3 = unit_rows(middle + mlp)
    gain3 = gains_ref[2:3, :]
    result = unit3 * gain3
    result_v[...] = result
    leave(result_v, result_ref)
    low_v[...] = result.astype(BF)
    leave(low_v, low_ref)
    cot = cot_ref[0].astype(F32)
    vec_ref[1:2, :] = jnp.sum(cot * unit3, axis=0, keepdims=True)
    d_final = norm_back(unit3, scale3, gain3, cot)
    d_mlp = d_final.astype(BF)
    rows_v[1] = d_mlp
    leave(rows_v.at[1], send_out.at[5])
    d_normed = jnp.zeros_like(middle)
    for i in range(4):
        d_pre = (dot_nt(d_mlp, down_v[i]) * slope_v[i]).astype(BF)
        pre_v[i] = d_pre
        leave(pre_v.at[i], (keep_out if i % 2 == 0 else send_out).at[2 + i // 2])
        d_normed = d_normed + dot_nt(d_pre, up_v[i])
    vec_ref[0:1, :] = jnp.sum(d_normed * unit2, axis=0, keepdims=True)
    d_mid = d_final + norm_back(unit2, scale2, gains_ref[1:2, :], d_normed)
    d_mid_ref[...] = d_mid
    low = d_mid.astype(BF)
    d_mid_low_ref[...] = low
    rows_v[2] = low
    leave(rows_v.at[2], send_out.at[6])
    for copy in leaving:
        copy.wait()


def mlp_pass(rows, keep, near, far, cot, gains, pieces):
    own, d = rows.shape
    hidden = pieces[0].shape[2]
    half = d // 2
    wide, low = shape((own, d), F32), shape((own, d), BF)
    return pl.pallas_call(
        functools.partial(mlp_kernel, half),
        out_shape=(
            wide, low, wide, low, shape((4, own, d), BF), shape((7, own, d), BF), shape((2, d), F32)
        ),
        in_specs=[VM] * 6 + [HB] * 8,
        out_specs=(HB, HB, VM, VM, HB, HB, VM),
        scratch_shapes=[
            pltpu.VMEM((4, d, hidden), BF),
            pltpu.VMEM((4, hidden, d), BF),
            pltpu.VMEM((4, own, hidden), F32),
            pltpu.VMEM((4, own, hidden), BF),
            pltpu.VMEM((4, own, hidden), BF),
            pltpu.VMEM((3, own, d), BF),
            pltpu.VMEM((own, d), F32),
            pltpu.VMEM((own, d), BF),
            pltpu.SemaphoreType.DMA((16,)),
            pltpu.SemaphoreType.DMA((13,)),
        ],
        compiler_params=params(60),
        cost_estimate=cost(21),
        name="dense_mlp",
    )(rows, keep, near, far, cot, gains, *pieces)


def mlp_grads_kernel(
    act_ref, pre_ref, own_ref, act2_ref, pre2_ref, rows2_ref, out_ref
):
    i = pl.program_id(0)

    @pl.when(i == 0)
    def _():
        out_ref[0] = (dot_tn(own_ref[0], pre_ref[0]) + dot_tn(rows2_ref[0], pre2_ref[0])).astype(BF)

    @pl.when(i == 1)
    def _():
        out_ref[0] = (dot_tn(own_ref[0], act_ref[0]) + dot_tn(rows2_ref[0], act2_ref[0])).astype(BF)


def mlp_grads(keep, send, other, which):
    _, own, d = keep.shape
    at = lambda n: pl.BlockSpec((1, own, d), lambda i: (n, 0, 0))
    pair = pl.BlockSpec((1, own, d), lambda i: (4 + i, 0, 0))
    return pl.pallas_call(
        mlp_grads_kernel,
        out_shape=shape((2, d, d), BF),
        grid=(2,),
        in_specs=[at(which), at(2 + which), pair, at(which), at(2 + which), pair],
        out_specs=pl.BlockSpec((1, d, d), lambda i: (i, 0, 0)),
        compiler_params=params(56, grid=1),
        cost_estimate=cost(5),
        name="mlp_grads",
    )(keep, keep, send, other, other, other)


def attention_back_kernel(
    heads, width, block, info, g0, g1, g2, g3, q_ref, k_ref, v_ref, mixed_n, mixed_f, lse_n, lse_f,
    mix_ref, qkv_ref, sel_ref, d_qkv_ref, keep_ref, send_ref, mid_ref,
    qs, ds, dq_acc, dk_acc, dv_acc,
):
    tensor, low = info[0], info[2]
    own = g0.shape[0]
    cols = heads * width
    total = k_ref.shape[0]
    lane = lanes(own, PAD)
    zero = jnp.zeros((own, PAD), BF)
    grads = (g0[...], g1[0], g2[...], g3[...])
    for r, grad in enumerate(grads):
        at = pl.multiple_of(jnp.bitwise_xor(tensor, r) * own, own)
        span = pl.ds(at, own)
        d_mixed = dot_nt(grad, mix_ref[...]).astype(BF)
        inner = d_mixed.astype(F32) * (mixed_n if r < 2 else mixed_f)[r % 2].astype(F32)
        q = q_ref[span, :]
        lse = (lse_n if r < 2 else lse_f)[r % 2]
        for h in range(heads):
            here = (lane >= h * width) & (lane < (h + 1) * width)
            delta = -jnp.sum(jnp.where(here, inner, 0.0), axis=-1, keepdims=True)
            row_lse = -jnp.sum(jnp.where(lanes(own, 128) == h, lse, 0.0), axis=-1, keepdims=True)
            left = jnp.where(here | (lane == cols + 3), q, zero)
            right = jnp.where(here, d_mixed, zero)
            for p, (a, b) in enumerate(zip(three_pieces(row_lse), three_pieces(delta))):
                left = jnp.where(lane == cols + p, a, left)
                right = jnp.where(lane == cols + p, b, right)
            qs[h, span, :] = left
            ds[h, span, :] = right
    dq_acc[...] = jnp.zeros_like(dq_acc)
    lane_k = lanes(block, PAD)
    allowed = subs(block, block) <= lanes(block, block)
    for j in range(total // block):
        first = j * block
        k, v = k_ref[first : first + block, :], v_ref[first : first + block, :]
        dk = jnp.zeros((block, PAD), F32)
        dv = jnp.zeros((block, PAD), F32)
        stacked, keys = [], []
        for h in range(heads):
            qh, dh = qs[h, first:, :], ds[h, first:, :]
            scores = dot_nt(k, qh)
            d_probs = dot_nt(v, dh)
            head = jnp.where(allowed, scores[:, :block], NEGATIVE)
            probs = jnp.exp(head)
            if first + block < total:
                probs = jnp.concatenate([probs, jnp.exp(scores[:, block:])], 1)
            d_scores = (probs * d_probs).astype(BF)
            dv = dv + dot(probs.astype(BF), dh)
            dk = dk + dot(d_scores, qh)
            stacked.append(d_scores)
            keys.append(
                jnp.where((lane_k >= h * width) & (lane_k < (h + 1) * width), k, jnp.zeros_like(k))
            )
        dq_acc[first:, :] += dot_tn(jnp.concatenate(stacked, 0), jnp.concatenate(keys, 0))
        dk_acc[...] = dk
        dv_acc[...] = dv
        d_qkv_ref[1, first : first + block, :] = dk_acc[:, :cols].astype(BF)
        d_qkv_ref[2, first : first + block, :] = dv_acc[:, :cols].astype(BF)
    d_qkv_ref[0] = (dq_acc[:, :cols] * width ** (-0.5)).astype(BF)
    pick = sel_ref.shape[1]
    sel = jnp.where(info[1] == 0, sel_ref[0:1, :], sel_ref[1:2, :])
    table = (sel == subs(total, pick)).astype(F32).astype(BF)
    part = jnp.zeros((pick, qkv_ref.shape[2]), F32)
    for i in range(3):
        part = part + dot(dot_tn(table, d_qkv_ref[i]).astype(BF), qkv_ref[i][:cols, :])
    half = pick // 2
    keep_ref[...] = jnp.where(low == 0, part[:half], part[half:]).astype(BF)
    send_ref[...] = jnp.where(low == 0, part[half:], part[:half]).astype(BF)
    mine = jnp.where(low == 0, sel[:, :half], sel[:, half:])
    mid = jnp.zeros((half, qkv_ref.shape[2]), F32)
    for r, grad in enumerate(grads):
        table = (mine == subs(own, half) + jnp.bitwise_xor(tensor, r) * own).astype(F32).astype(BF)
        mid = mid + dot_tn(table, grad)
    mid_ref[...] = mid.astype(BF)


def attention_back(
    info, grads, q, k, v, mixed, lse, mix_w, qkv_w, selected, heads, width, block=256
):
    keep, other, far, far_other = grads
    own, d = keep.shape
    total = k.shape[0] * k.shape[1]
    flat = lambda a: a.reshape(total, PAD)
    half = shape((selected.shape[1] // 2, d), BF)
    at = lambda n: pl.BlockSpec((1, own, d), lambda i: (n, 0, 0))
    full = lambda a: pl.BlockSpec(a.shape, lambda i: (0,) * a.ndim)
    rest = (flat(q), flat(k), flat(v), *mixed, *lse, mix_w, qkv_w, selected)
    return pl.pallas_call(
        functools.partial(attention_back_kernel, heads, width, block),
        out_shape=(shape((3, total, heads * width), BF), half, half, half),
        grid=(1,),
        in_specs=[SM, full(keep), at(6), full(far), full(far_other)] + [full(a) for a in rest],
        out_specs=(
            pl.BlockSpec((3, total, heads * width), lambda i: (0, 0, 0)),
        ) + (pl.BlockSpec(half.shape, lambda i: (0, 0)),) * 3,
        scratch_shapes=[
            pltpu.VMEM((heads, total, PAD), BF),
            pltpu.VMEM((heads, total, PAD), BF),
            pltpu.VMEM((total, PAD), F32),
            pltpu.VMEM((block, PAD), F32),
            pltpu.VMEM((block, PAD), F32),
        ],
        compiler_params=params(60, grid=1),
        cost_estimate=cost(35),
        name="attention_back",
    )(info, keep, other, far, far_other, *rest)


def spread_back_kernel(cols, info, d_ref, qkv_ref, send_ref, keep_ref):
    i = pl.program_id(0)
    total = dot(d_ref[0, 0], qkv_ref[0][:cols, :])
    for n in (1, 2):
        total = total + dot(d_ref[n, 0], qkv_ref[n][:cols, :])
    total = total.astype(BF)

    @pl.when(i < 2)
    def _():
        send_ref[0] = total

    @pl.when(i >= 2)
    def _():
        keep_ref[0] = total


def spread_back(info, d_qkv, qkv_w, count):
    _, total, cols = d_qkv.shape
    own = total // count
    d = qkv_w.shape[2]
    pos = lambda i: jnp.where(i < 2, 3 - 2 * i, 6 - 2 * i)
    out = shape((2, own, d), BF)
    return pl.pallas_call(
        functools.partial(spread_back_kernel, cols),
        out_shape=(out, out),
        grid_spec=pltpu.PrefetchScalarGridSpec(
            num_scalar_prefetch=1,
            grid=(count,),
            in_specs=[
                pl.BlockSpec(
                    (3, 1, own, cols), lambda i, info: (0, jnp.bitwise_xor(pos(i), info[0]), 0, 0)
                ),
                pl.BlockSpec(qkv_w.shape, lambda i, info: (0, 0, 0)),
            ],
            out_specs=(
                pl.BlockSpec((1, own, d), lambda i, info: (1 - jnp.minimum(i, 1), 0, 0)),
                pl.BlockSpec((1, own, d), lambda i, info: (1 - jnp.maximum(i - 2, 0), 0, 0)),
            ),
        ),
        compiler_params=params(grid=1),
        cost_estimate=cost(5),
        name="spread_back",
    )(info, d_qkv.reshape(3, count, own, cols), qkv_w)


def attn_grads_kernel(
    cols, info, d_ref, normed_ref, g0, g1, g2, g3, mixed_n, mixed_f, pack_ref, acc,
):
    i = pl.program_id(0)

    @pl.when(i == 0)
    def _():
        acc[...] = jnp.zeros_like(acc)

    for n in range(3):
        acc[n * cols : (n + 1) * cols, :] += dot_tn(d_ref[n, 0], normed_ref[0])
    for r, grad in enumerate((g0, g1, g2, g3)):
        @pl.when(i == r)
        def _():
            mixed = (mixed_n if r < 2 else mixed_f)[r % 2]
            rows = grad[0] if r == 1 else grad[...]
            acc[3 * cols :, :] += dot_tn(mixed[:, :cols], rows)

    @pl.when(i == 3)
    def _():
        pack_ref[...] = jnp.transpose(acc[...]).astype(BF)


def attn_grads(info, d_qkv, normed, grads, mixed):
    _, total, cols = d_qkv.shape
    count, own, d = normed.shape
    full = lambda dims: pl.BlockSpec(dims, lambda i, info: (0,) * len(dims))
    return pl.pallas_call(
        functools.partial(attn_grads_kernel, cols),
        out_shape=shape((d, 4 * cols), BF),
        grid_spec=pltpu.PrefetchScalarGridSpec(
            num_scalar_prefetch=1,
            grid=(count,),
            in_specs=[
                pl.BlockSpec(
                    (3, 1, own, cols), lambda i, info: (0, jnp.bitwise_xor(i, info[0]), 0, 0)
                ),
                pl.BlockSpec((1, own, d), lambda i, info: (jnp.bitwise_xor(i, info[0]), 0, 0)),
            ]
            + [
                full((own, d)), pl.BlockSpec((1, own, d), lambda i, info: (6, 0, 0)),
                full((own, d)), full((own, d)),
            ]
            + [full(mixed[0].shape)] * 2,
            out_specs=full((d, 4 * cols)),
            scratch_shapes=[pltpu.VMEM((4 * cols, d), F32)],
        ),
        compiler_params=params(grid=1),
        cost_estimate=cost(8),
        name="attn_grads",
    )(info, d_qkv.reshape(3, count, own, cols), normed, *grads, *mixed)


def routed_mlp_grads_kernel(
    info, normed_ref, pre_ref, act_ref, grad_ref, part_ref, far_ref, pack_ref,
):
    hidden = pre_ref.shape[1]

    @pl.when(info[1] == 0)
    def _():
        pack_ref[:, :hidden] = dot_tn(normed_ref[...], pre_ref[...]).astype(BF)
        pack_ref[:, hidden:] = dot_tn(grad_ref[...], act_ref[...]).astype(BF)

    @pl.when(info[1] != 0)
    def _():
        for n in range(2):
            total = part_ref[n].astype(F32) + far_ref[n].astype(F32)
            pack_ref[:, n * hidden : (n + 1) * hidden] = total.astype(BF)


def routed_mlp_grads(info, normed, pre, act, grad, *dense):
    return pl.pallas_call(
        routed_mlp_grads_kernel,
        out_shape=shape((normed.shape[1], 2 * pre.shape[1]), BF),
        in_specs=[SM] + [VM] * 6,
        out_specs=VM,
        compiler_params=params(),
        cost_estimate=cost(5),
        name="routed_mlp_grads",
    )(info, normed, pre, act, grad, *dense)


def routed_attn_grads_kernel(
    info, normed_ref, d_ref, low_ref, mixed_ref, part_ref, hop_ref, vec_ref, pack_ref
):
    cols = mixed_ref.shape[1]
    wide = 4 * cols
    vecs = jnp.concatenate(
        [vec_ref[...], jnp.zeros((128 - vec_ref.shape[0], vec_ref.shape[1]), F32)], 0
    )
    pack_ref[:, wide:] = jnp.transpose(vecs).astype(BF)

    @pl.when(info[1] == 0)
    def _():
        rows = [dot_tn(d_ref[n], normed_ref[...]) for n in range(3)]
        rows.append(dot_tn(mixed_ref[...], low_ref[...]))
        pack_ref[:, :wide] = jnp.transpose(jnp.concatenate(rows, 0)).astype(BF)

    @pl.when(info[1] != 0)
    def _():
        pack_ref[:, :wide] = (part_ref[...].astype(F32) + hop_ref[...].astype(F32)).astype(BF)


def routed_attn_grads(info, normed, d_qkv, d_low, mixed, part, far, vecs):
    return pl.pallas_call(
        routed_attn_grads_kernel,
        out_shape=shape((normed.shape[1], 4 * mixed.shape[1] + 128), BF),
        in_specs=[SM] + [VM] * 7,
        out_specs=VM,
        compiler_params=params(),
        cost_estimate=cost(3),
        name="routed_attn_grads",
    )(info, normed, d_qkv, d_low, mixed, part, far, vecs)


def rows_back_kernel(keep_ref, near_ref, far_ref, rows_ref, d_mid_ref, gains_ref, d_rows_ref, vec_ref):
    d_normed = keep_ref[0].astype(F32) + near_ref[0].astype(F32) + far_ref[...].astype(F32)
    unit, scale = unit_rows(rows_ref[...].astype(F32))
    vec_ref[...] = jnp.sum(d_normed * unit, axis=0, keepdims=True)
    d_rows = d_mid_ref[...] + norm_back(unit, scale, gains_ref[0:1, :], d_normed)
    d_rows_ref[...] = d_rows.astype(BF)


def rows_back(keep, near, far, rows, d_mid, gains):
    own, d = rows.shape
    return pl.pallas_call(
        rows_back_kernel,
        out_shape=(shape((own, d), BF), shape((1, d), F32)),
        in_specs=[VM] * 6,
        out_specs=(VM, VM),
        compiler_params=params(),
        cost_estimate=cost(4),
        name="rows_back",
    )(keep, near, far, rows, d_mid, gains)


def sel_back_kernel(near_ref, far_ref, picked_ref, upd_ref, mid_ref, gains_ref, out_ref):
    d_normed = near_ref[...].astype(F32) + far_ref[...].astype(F32)
    rows = (picked_ref[...].astype(F32) + upd_ref[...].astype(F32)).astype(BF).astype(F32)
    unit, scale = unit_rows(rows)
    d_rows = mid_ref[...].astype(F32) + norm_back(unit, scale, gains_ref[0:1, :], d_normed)
    out_ref[...] = d_rows.astype(BF)


def sel_back(near, far, picked, upd, mid, gains):
    return pl.pallas_call(
        sel_back_kernel,
        out_shape=shape(near.shape, BF),
        in_specs=[VM] * 6,
        out_specs=VM,
        compiler_params=params(),
        cost_estimate=cost(2.3),
        name="sel_back",
    )(near, far, picked, upd, mid, gains)


def add(a, b):
    return (a.astype(F32) + b.astype(F32)).astype(BF)


def core_sum(keep, send):
    return add(keep, swap(send, "tensor", 1))


def whole_sum(keep, send):
    near = core_sum(keep, send)
    return add(near, swap(near, "tensor", 2))


def scatter_groups(pack):
    count, me = lax.axis_size("dp"), lax.axis_index("dp")
    if count != 4:
        return lax.psum_scatter(pack, "dp", scatter_dimension=0, tiled=True)
    for bit in (1, 2):
        rows = pack.shape[0] // 2
        side = (me // bit) % 2
        if bit == 1:
            quarters = pack.reshape(2, 2, rows // 2, pack.shape[1])
            take = lambda at: lax.dynamic_index_in_dim(quarters, at, 1, keepdims=False)
            keep, send = take(side), take(1 - side)
        else:
            keep = lax.dynamic_index_in_dim(pack, side, 0, keepdims=False)
            send = lax.dynamic_index_in_dim(pack, 1 - side, 0, keepdims=False)
        pack = add(keep, swap(send, "dp", bit))
    return pack


def body(
    tokens, qkv_weight, out_weight, up_weight, down_weight, vectors, lengths, selected, cotangent
):
    section = lax.axis_index("section")
    tensor = lax.axis_index("tensor")
    group = lax.axis_size("dp")
    heads = HEADS // lax.axis_size("tensor")
    low = tensor & 1
    is_dense = section == 1
    gains = vectors[0]
    qkv_w = jnp.swapaxes(qkv_weight[0], 1, 2)
    mix_w, up_w, down_w = out_weight[0], up_weight[0], down_weight[0]
    cols = qkv_w.shape[1]
    width = cols // heads
    d = mix_w.shape[1]

    barrier = lax.optimization_barrier
    core = lambda block: swap(block, "tensor", 1)
    cross = lambda block: swap(block, "tensor", 2)

    halves = up_w.shape[0] // 2
    parity = lax.axis_index("dp") & 1
    take = lambda w, at: lax.dynamic_slice_in_dim(w, at * halves, halves, 0)
    mine = (take(up_w, parity), take(down_w, parity))
    up_far = hop(mine[0], 1, 0)
    down_far = hop(after(mine[1], up_far), 1, 0)

    near = core_sum(*pick_rows(tokens, selected))
    far = cross(near)
    info = jnp.stack([tensor, section, low, lengths[section]]).astype(jnp.int32)
    my_tokens = lax.dynamic_index_in_dim(tokens, section, 0, keepdims=False)
    part = my_tokens.shape[0] // 2
    tok_a, tok_b = my_tokens[:part], my_tokens[part:]
    far, my_tokens, info, tok_a, tok_b = barrier((far, my_tokens, info, tok_a, tok_b))
    tok2a = cross(after(tok_a, far))
    packed = pack_weights(gains, qkv_w, mix_w)
    picked_half = add(near, far)
    picked_other = core(picked_half)

    picked, normed, q, k, v, mixed, keep, send = routed_attn(
        info, picked_half, picked_other, gains, qkv_w, mix_w, heads
    )
    send, tok2a, up_far = barrier((send, tok2a, up_far))
    near = core_sum(keep, send)
    far = cross(near)
    far, packed, down_far = barrier((far, packed, down_far))
    attn_half = add(near, far)
    tok2b = cross(after(tok_b, far))
    tok1 = core(my_tokens)
    attn_other = core(attn_half)
    packed_far = hop(after(packed, down_far), 1, 0)
    attn, normed2, act, slope, keep, send = routed_mlp(
        info, picked, attn_half, attn_other, gains, up_w, down_w
    )
    piece0a = jnp.stack(
        [jnp.where(is_dense, own, far) for own, far in zip(mine, (up_far, down_far))]
    )
    send, tok2b = barrier((send, tok2b))
    near = core_sum(keep, send)
    far = cross(near)
    far, piece0a = barrier((far, piece0a))
    piece0b = swap(piece0a, "dp", 1)
    both_half, update_half = make_update(picked_half, attn_half, near, far, gains)
    piece2a = cross(after(piece0a, far))
    piece1a = core(piece0a)
    tok3a, tok3b = core(tok2a), core(tok2b)
    arrived = hop(update_half[1], 0, 1)
    my_update = jnp.where(is_dense, arrived, update_half[0])
    my_update, piece1a, packed_far = barrier((my_update, piece1a, packed_far))
    d_gains, d_qkv_w, d_mix_w = prepare(info, gains, qkv_w, mix_w, packed_far)
    my_update_other = core(my_update)
    my_update_other, d_gains = barrier((my_update_other, d_gains))
    toks = (my_tokens, tok1, tok2a, tok2b, tok3a, tok3b)

    piece2b = swap(after(piece2a, my_update_other), "dp", 1)

    rows, d_normed_rows, dq_in, dk_in, dv_in = project(
        info, toks, my_update, my_update_other, selected, d_gains, d_qkv_w, heads, width,
        lax.axis_size("tensor"),
    )
    dq_in, piece0b = barrier((dq_in, piece0b))
    send, keep, mixed_f, lse_f = attention(info, dq_in, dk_in, dv_in, d_mix_w, heads, width, 2)
    send, piece2b = barrier((send, piece2b))
    near = core_sum(keep, send)
    far = cross(near)
    piece1b = core(after(piece0b, near))
    send, keep, mixed_n, lse_n = attention(info, dq_in, dk_in, dv_in, d_mix_w, heads, width, 0)
    piece3a = core(after(piece2a, send))
    piece3b = core(after(piece2b, send))
    send, far = barrier((send, far))
    near = core(send)
    my_cot = lax.dynamic_slice_in_dim(cotangent, section, 1, 0)
    result, result_low, d_mid, d_mid_low, mlp_keep, mlp_send, m_vec = mlp_pass(
        rows, keep, near, far, my_cot, d_gains,
        (piece0a, piece0b, piece1a, piece1b, piece2a, piece2b, piece3a, piece3b),
    )
    grad_f = cross(d_mid_low)
    mlp_other = core(mlp_send)
    mlp_f = mlp_grads(mlp_keep, mlp_send, mlp_other, 1)
    grad_f, mlp_f = barrier((grad_f, mlp_f))
    grads = (d_mid_low, mlp_other, grad_f, core(grad_f))
    mlp_f2 = cross(mlp_f)
    sent_result = hop(result_low, 0, 1)

    d_qkv, keep, send, mid_sel = attention_back(
        info, grads, dq_in, dk_in, dv_in, (mixed_n, mixed_f), (lse_n, lse_f),
        d_mix_w, d_qkv_w, selected, heads, width,
    )
    send, sent_result = barrier((send, sent_result))
    mlp_n = mlp_grads(mlp_keep, mlp_send, after(mlp_other, send), 0)
    near = core_sum(keep, send)
    near, mlp_f2, mlp_n = barrier((near, mlp_f2, mlp_n))
    far = cross(near)
    mlp_part = add(mlp_n, mlp_f2)
    far, mlp_part = barrier((far, mlp_part))
    mlp_hop = hop(mlp_part, 0, 1)
    my_picked = lax.dynamic_index_in_dim(picked_half, section, 0, keepdims=False)
    my_d_sel = sel_back(near, far, my_picked, my_update, mid_sel, d_gains)
    back = hop(my_d_sel, 1, 0)
    attn_part = attn_grads(
        info, after(d_qkv, my_d_sel), d_normed_rows, grads, (mixed_n, mixed_f)
    )
    back, attn_part = barrier((back, attn_part))
    sel_other = core(jnp.concatenate([my_d_sel[None], back[None], both_half], 0))

    d_sel, r_d_mlp, r_d_pre, gain_two, keep2, send2 = routed_back_mlp(
        info, my_d_sel, back, sel_other, picked, attn, gains, slope, up_w, down_w
    )
    near = core_sum(keep2, send2)
    far = cross(near)
    row_send, row_keep = spread_back(info, after(d_qkv, near), d_qkv_w, 4)
    far, row_send, mlp_hop = barrier((far, row_send, mlp_hop))
    row_core = core(row_send)
    half = add(near, far)
    other = core(half)
    r_mlp = routed_mlp_grads(info, normed2, r_d_pre, act, r_d_mlp, mlp_part, mlp_hop)
    other, r_mlp = barrier((other, r_mlp))
    row_far = cross(add(row_keep[1], row_core[1]))
    attn_hop = hop(attn_part, 0, 1)
    hidden = up_w.shape[1]
    r_d_mid, r_d_low, r_d_qkv, r_vec, keep2, send2 = routed_back_attn(
        info, half, other, d_sel, picked, attn, both_half, sel_other, gains, q, k, v,
        qkv_w, mix_w, heads,
    )
    near = core_sum(keep2, send2)
    mlp_sum = lax.psum_scatter(r_mlp, "dp", scatter_dimension=0, tiled=True)
    near, row_far = barrier((near, row_far))
    far = cross(near)
    d_rows, row_vec = rows_back(row_keep, row_core, row_far, rows, d_mid, d_gains)
    d_rows_far = hop(d_rows, 1, 0)
    far, d_rows, attn_hop = barrier((far, d_rows, attn_hop))
    half = add(near, far)
    other = core(half)
    vecs = jnp.concatenate([r_vec[0:1], gain_two, r_vec[1:2], row_vec, m_vec], 0)
    vecs = vecs + swap(vecs, "tensor", 1)
    vecs = vecs + swap(vecs, "tensor", 2)
    r_attn = routed_attn_grads(
        info, normed, r_d_qkv, r_d_low, mixed, after(attn_part, half), attn_hop, vecs
    )
    attn_sum = scatter_groups(r_attn)

    combined = finish(
        info, half, other, r_d_mid, picked, gains, selected, d_rows, d_rows_far, sent_result, result
    )
    share = d // group
    up_grad = mlp_sum[:, :hidden].astype(F32)
    down_grad = jnp.swapaxes(mlp_sum[:, hidden:], 0, 1).astype(F32)
    qkv_grad = jnp.swapaxes(attn_sum[:, : 3 * cols].reshape(share, 3, cols), 0, 1).astype(F32)
    mix_grad = jnp.swapaxes(attn_sum[:, 3 * cols : 4 * cols], 0, 1).astype(F32)

    vecs = jnp.transpose(attn_sum[:, 4 * cols : 4 * cols + 8].astype(F32))
    dense_vec = vecs[3:6] + hop(vecs[3:6], 0, 1)
    vecs = jnp.where(is_dense, dense_vec, vecs[:3])
    return (
        combined[None],
        qkv_grad[None],
        mix_grad[None],
        up_grad[None],
        down_grad[None],
        vecs[None],
    )


def solution(mesh):
    placed = (
        P("dp", "tensor", None),
        P("section", None, None, "tensor"),
        P("section", "tensor", None),
        P("section", None, "tensor"),
        P("section", "tensor", None),
        P("section", None, None),
        P("dp"),
        P("dp", None),
        P("dp", "tensor", None),
    )
    return jax.shard_map(
        body,
        mesh=mesh,
        in_specs=placed,
        out_specs=(
            P("section", "dp", "tensor", None),
            P("section", None, "dp", "tensor"),
            P("section", "tensor", "dp"),
            P("section", "dp", "tensor"),
            P("section", "tensor", "dp"),
            P("section", None, "dp"),
        ),
        check_vma=False,
    )
```

```python
import functools

import jax
import jax.numpy as jnp
from jax import lax
from jax.experimental import pallas as pl
from jax.experimental.pallas import tpu as pltpu
from jax.sharding import PartitionSpec as P

HEADS = 12
EPSILON = 1e-06
NEGATIVE = -1e30
BF = jnp.bfloat16
F32 = jnp.float32
PAD = 256
MIB = 1 << 20


def swap(block, axis, bit):
    count = lax.axis_size(axis)
    return lax.ppermute(block, axis, [(i, i ^ bit) for i in range(count)])


def hop(block, source, target):
    return lax.ppermute(block, "section", [(source, target)])


def dot(left, right):
    return lax.dot_general(left, right, (((1,), (0,)), ((), ())), preferred_element_type=F32)


def dot_nt(left, right):
    return lax.dot_general(left, right, (((1,), (1,)), ((), ())), preferred_element_type=F32)


def dot_tn(left, right):
    return lax.dot_general(left, right, (((0,), (0,)), ((), ())), preferred_element_type=F32)


def unit_rows(values):
    scale = lax.rsqrt(jnp.mean(values * values, axis=-1, keepdims=True) + EPSILON)
    return values * scale, scale


def norm_back(unit, scale, gain, grad):
    e = grad * gain
    return scale * (e - unit * jnp.mean(e * unit, axis=-1, keepdims=True))


def gelu_pair(x):
    c = 0.7978845608028654
    a = 0.044715
    xx = x * x
    th = jnp.tanh(c * (x + a * (x * xx)))
    half = 0.5 * (1.0 + th)
    slope = half + (0.5 * x) * (1.0 - th * th) * (c * (1.0 + (3.0 * a) * xx))
    return x * half, slope


def lanes(rows, width):
    return lax.broadcasted_iota(jnp.int32, (rows, width), 1)


def subs(rows, width):
    return lax.broadcasted_iota(jnp.int32, (rows, width), 0)


def head_of(values, lane, head, width):
    zero = jnp.zeros_like(values)
    return jnp.where((lane >= head * width) & (lane < (head + 1) * width), values, zero)


def three_pieces(column):
    first = column.astype(BF)
    rest = column - first.astype(F32)
    second = rest.astype(BF)
    third = (rest - second.astype(F32)).astype(BF)
    return first, second, third


def params(limit=56, grid=None):
    if grid is None:
        return pltpu.CompilerParams(vmem_limit_bytes=limit * MIB)
    return pltpu.CompilerParams(
        vmem_limit_bytes=limit * MIB, dimension_semantics=("arbitrary",) * grid
    )


def cost(us):
    return pl.CostEstimate(
        flops=int(us * 1e8), bytes_accessed=int(us * 3.3e6), transcendentals=0
    )


def after(value, *others):
    return lax.optimization_barrier((value,) + others)[0]


VM = pl.BlockSpec(memory_space=pltpu.VMEM)
SM = pl.BlockSpec(memory_space=pltpu.SMEM)
HB = pl.BlockSpec(memory_space=pl.ANY)


def shape(dims, dtype):
    return jax.ShapeDtypeStruct(dims, dtype)


def halves_out(partial, low, keep_ref, send_ref):
    pick = partial.shape[0] // 2
    half = pick // 2
    for s in range(2):
        first = partial[s * pick : s * pick + half]
        second = partial[s * pick + half : (s + 1) * pick]
        keep_ref[s] = jnp.where(low == 0, first, second).astype(BF)
        send_ref[s] = jnp.where(low == 0, second, first).astype(BF)


def halves_in(own_ref, other_ref, low):
    parts = []
    for s in range(2):
        own, other = own_ref[s].astype(F32), other_ref[s].astype(F32)
        parts.append(jnp.where(low == 0, own, other))
        parts.append(jnp.where(low == 0, other, own))
    return jnp.concatenate(parts, 0)


def pick_kernel(rows_ref, sel_ref, keep_ref, send_ref):
    tensor = lax.axis_index("tensor")
    own = rows_ref.shape[1]
    pick = sel_ref.shape[1]
    parts = []
    for s in range(2):
        table = (sel_ref[s : s + 1, :] == subs(own, pick) + tensor * own).astype(F32).astype(BF)
        parts.append(dot_tn(table, rows_ref[s]))
    halves_out(jnp.concatenate(parts, 0), tensor & 1, keep_ref, send_ref)


def pick_rows(rows, selected):
    _, _, d = rows.shape
    out = shape((2, selected.shape[1] // 2, d), BF)
    return pl.pallas_call(
        pick_kernel,
        out_shape=(out, out),
        in_specs=[VM, VM],
        out_specs=(VM, VM),
        compiler_params=params(),
        cost_estimate=cost(3),
        name="pick",
    )(rows, selected)


def routed_attn_kernel(
    heads, info, own_ref, other_ref, gains_ref, qkv_ref, mix_ref,
    picked_ref, normed_ref, q_ref, k_ref, v_ref, mixed_ref, keep_ref, send_ref,
):
    low = info[2]
    picked = halves_in(own_ref, other_ref, low)
    picked_ref[...] = picked.astype(BF)
    unit, _ = unit_rows(picked)
    normed = (unit * gains_ref[0:1, :]).astype(BF)
    normed_ref[...] = normed
    width = qkv_ref.shape[1] // heads
    q = dot_nt(normed, qkv_ref[0]).astype(BF)
    k = dot_nt(normed, qkv_ref[1]).astype(BF)
    v = dot_nt(normed, qkv_ref[2]).astype(BF)
    q = (q.astype(F32) * width ** (-0.5)).astype(BF)
    q_ref[...] = q
    k_ref[...] = k
    v_ref[...] = v
    pick = picked.shape[0] // 2
    lane = lanes(pick, heads * width)
    allowed = lanes(pick, pick) <= subs(pick, pick)
    parts = []
    for s in range(2):
        span = slice(s * pick, (s + 1) * pick)
        total = jnp.zeros((pick, heads * width), F32)
        for h in range(heads):
            scores = dot_nt(head_of(q[span], lane, h, width), k[span])
            scores = jnp.where(allowed, scores, NEGATIVE)
            expos = jnp.exp(scores - jnp.max(scores, axis=-1, keepdims=True))
            probs = expos / jnp.sum(expos, axis=-1, keepdims=True)
            total = total + dot(probs.astype(BF), head_of(v[span], lane, h, width))
        parts.append(total.astype(BF))
    mixed = jnp.concatenate(parts, 0)
    mixed_ref[...] = mixed
    halves_out(dot(mixed, mix_ref[...]), low, keep_ref, send_ref)


def routed_attn(info, own, other, gains, qkv_w, mix_w, heads):
    _, half, d = own.shape
    rows = 4 * half
    cols = qkv_w.shape[1]
    part = shape((2, half, d), BF)
    wide, narrow = shape((rows, d), BF), shape((rows, cols), BF)
    return pl.pallas_call(
        functools.partial(routed_attn_kernel, heads),
        out_shape=(wide, wide, narrow, narrow, narrow, narrow, part, part),
        in_specs=[SM] + [VM] * 5,
        out_specs=(VM,) * 8,
        compiler_params=params(),
        cost_estimate=cost(5),
        name="routed_attn",
    )(info, own, other, gains, qkv_w, mix_w)


def routed_mlp_kernel(
    info, picked_ref, own_ref, other_ref, gains_ref, up_ref, down_ref,
    attn_ref, normed_ref, act_ref, slope_ref, keep_ref, send_ref,
):
    low = info[2]
    attn = halves_in(own_ref, other_ref, low)
    attn_ref[...] = attn.astype(BF)
    unit, _ = unit_rows(picked_ref[...].astype(F32) + attn)
    normed = (unit * gains_ref[1:2, :]).astype(BF)
    normed_ref[...] = normed
    act, slope = gelu_pair(dot(normed, up_ref[...]))
    act = act.astype(BF)
    act_ref[...] = act
    slope_ref[...] = slope
    halves_out(dot(act, down_ref[...]), low, keep_ref, send_ref)


def routed_mlp(info, picked, own, other, gains, up_w, down_w):
    rows, d = picked.shape
    hidden = up_w.shape[1]
    part = shape((2, rows // 4, d), BF)
    return pl.pallas_call(
        routed_mlp_kernel,
        out_shape=(
            shape((rows, d), BF), shape((rows, d), BF), shape((rows, hidden), BF),
            shape((rows, hidden), F32), part, part,
        ),
        in_specs=[SM] + [VM] * 6,
        out_specs=(VM,) * 6,
        compiler_params=params(),
        cost_estimate=cost(6),
        name="routed_mlp",
    )(info, picked, own, other, gains, up_w, down_w)


def update_kernel(picked_ref, attn_ref, mlp_ref, mlp2_ref, gains_ref, both_ref, update_ref):
    d = picked_ref.shape[2]
    weight = gains_ref[2:3, :] * d ** (-0.5)
    for s in range(2):
        router = jnp.sum(picked_ref[s].astype(F32) * weight, axis=-1, keepdims=True)
        both = attn_ref[s].astype(F32) + (mlp_ref[s].astype(F32) + mlp2_ref[s].astype(F32))
        both_ref[s] = both.astype(BF)
        update_ref[s] = (router * both).astype(BF)


def make_update(picked_half, attn_half, mlp_half, mlp_far, gains):
    out = shape(picked_half.shape, BF)
    return pl.pallas_call(
        update_kernel,
        out_shape=(out, out),
        in_specs=[VM] * 5,
        out_specs=(VM, VM),
        compiler_params=params(),
        cost_estimate=cost(2.5),
        name="update",
    )(picked_half, attn_half, mlp_half, mlp_far, gains)


def routed_back_mlp_kernel(
    info, sel_own, sel_back, sel_other, picked_ref, attn_ref, gains_ref, slope_ref, up_ref, down_ref,
    d_sel_ref, d_mlp_ref, d_pre_ref, gain_ref, keep_ref, send_ref,
):
    low = info[2]
    d = picked_ref.shape[1]
    parts = []
    for s, own in enumerate((sel_own[...], sel_back[...])):
        other = sel_other[s]
        parts += [jnp.where(low == 0, own, other), jnp.where(low == 0, other, own)]
    d_sel = jnp.concatenate(parts, 0).astype(F32)
    d_sel_ref[...] = d_sel
    picked = picked_ref[...].astype(F32)
    router = jnp.sum(picked * (gains_ref[2:3, :] * d ** (-0.5)), axis=-1, keepdims=True)
    d_mlp = (router * d_sel).astype(BF)
    d_mlp_ref[...] = d_mlp
    d_pre = (dot_nt(d_mlp, down_ref[...]) * slope_ref[...]).astype(BF)
    d_pre_ref[...] = d_pre
    d_normed = dot_nt(d_pre, up_ref[...])
    unit, _ = unit_rows(picked + attn_ref[...].astype(F32))
    gain_ref[...] = jnp.sum(d_normed * unit, axis=0, keepdims=True)
    halves_out(d_normed, low, keep_ref, send_ref)


def routed_back_mlp(info, sel_own, sel_back, sel_other, picked, attn, gains, slope, up_w, down_w):
    rows, d = picked.shape
    hidden = up_w.shape[1]
    part = shape((2, rows // 4, d), BF)
    return pl.pallas_call(
        routed_back_mlp_kernel,
        out_shape=(
            shape((rows, d), F32), shape((rows, d), BF), shape((rows, hidden), BF),
            shape((1, d), F32), part, part,
        ),
        in_specs=[SM] + [VM] * 9,
        out_specs=(VM,) * 6,
        compiler_params=params(),
        cost_estimate=cost(6),
        name="routed_back_mlp",
    )(info, sel_own, sel_back, sel_other, picked, attn, gains, slope, up_w, down_w)


def routed_back_attn_kernel(
    heads, info, own_ref, other_ref, d_sel_ref, picked_ref, attn_ref, both_own, both_other,
    gains_ref, q_ref, k_ref, v_ref, qkv_ref, mix_ref,
    d_mid_ref, d_low_ref, d_qkv_ref, vec_ref, keep_ref, send_ref,
):
    low = info[2]
    rows, d = picked_ref.shape
    d_normed2 = halves_in(own_ref, other_ref, low)
    picked = picked_ref[...].astype(F32)
    d_sel = d_sel_ref[...]
    router_row = gains_ref[2:3, :] * d ** (-0.5)
    router = jnp.sum(picked * router_row, axis=-1, keepdims=True)
    unit2, scale2 = unit_rows(picked + attn_ref[...].astype(F32))
    d_mid = norm_back(unit2, scale2, gains_ref[1:2, :], d_normed2)
    both = halves_in(both_own, both_other.at[2:], low)
    d_router = jnp.sum(d_sel * both, axis=-1, keepdims=True)
    d_mid_ref[...] = d_mid + d_router * router_row
    d_weight = jnp.sum(picked * d_router, axis=0, keepdims=True) * d ** (-0.5)
    vec_ref[1:2, :] = jnp.where(info[0] == 0, d_weight, jnp.zeros_like(d_weight))
    d_low = (router * d_sel + d_mid).astype(BF)
    d_low_ref[...] = d_low
    d_mixed = dot_nt(d_low, mix_ref[...]).astype(BF)
    width = qkv_ref.shape[1] // heads
    pick = rows // 2
    lane = lanes(pick, heads * width)
    allowed = subs(pick, pick) <= lanes(pick, pick)
    dq_parts, dk_parts, dv_parts = [], [], []
    for s in range(2):
        span = slice(s * pick, (s + 1) * pick)
        q, k, v, dm = q_ref[span, :], k_ref[span, :], v_ref[span, :], d_mixed[span]
        dq = jnp.zeros((pick, heads * width), F32)
        dk, dv = dq, dq
        for h in range(heads):
            qh, kh = head_of(q, lane, h, width), head_of(k, lane, h, width)
            dh = head_of(dm, lane, h, width)
            scores = jnp.where(allowed, dot_nt(k, qh), NEGATIVE)
            expos = jnp.exp(scores - jnp.max(scores, axis=0, keepdims=True))
            probs = expos / jnp.sum(expos, axis=0, keepdims=True)
            d_probs = dot_nt(v, dh)
            inner = jnp.sum(probs * d_probs, axis=0, keepdims=True)
            d_scores = (probs * (d_probs - inner)).astype(BF)
            dv = dv + dot(probs.astype(BF), dh)
            dk = dk + dot(d_scores, qh)
            dq = dq + dot_tn(d_scores, kh)
        dq_parts.append(dq * width ** (-0.5))
        dk_parts.append(dk)
        dv_parts.append(dv)
    d_normed = jnp.zeros((rows, d), F32)
    for i, parts in enumerate((dq_parts, dk_parts, dv_parts)):
        whole = jnp.concatenate(parts, 0).astype(BF)
        d_qkv_ref[i] = whole
        d_normed = d_normed + dot(whole, qkv_ref[i])
    unit, _ = unit_rows(picked)
    vec_ref[0:1, :] = jnp.sum(d_normed * unit, axis=0, keepdims=True)
    halves_out(d_normed, low, keep_ref, send_ref)


def routed_back_attn(
    info, own, other, d_sel, picked, attn, both_own, both_other, gains, q, k, v, qkv_w, mix_w, heads
):
    rows, d = picked.shape
    part = shape((2, rows // 4, d), BF)
    return pl.pallas_call(
        functools.partial(routed_back_attn_kernel, heads),
        out_shape=(
            shape((rows, d), F32), shape((rows, d), BF), shape((3,) + q.shape, BF),
            shape((2, d), F32), part, part,
        ),
        in_specs=[SM] + [VM] * 13,
        out_specs=(VM,) * 6,
        compiler_params=params(),
        cost_estimate=cost(8),
        name="routed_back_attn",
    )(info, own, other, d_sel, picked, attn, both_own, both_other, gains, q, k, v, qkv_w, mix_w)


def finish_kernel(
    info, own_ref, other_ref, d_mid_ref, picked_ref, gains_ref, sel_ref,
    d_rows_ref, far_ref, sent_ref, result_ref, out_ref,
):
    tensor, section, low = info[0], info[1], info[2]
    own = d_rows_ref.shape[0]
    pick = sel_ref.shape[1]

    @pl.when(section == 0)
    def _():
        d_normed = halves_in(own_ref, other_ref, low)
        unit, scale = unit_rows(picked_ref[...].astype(F32))
        d_picked = d_mid_ref[...] + norm_back(unit, scale, gains_ref[0:1, :], d_normed)
        d_picked = d_picked.astype(BF)
        for s in range(2):
            table = (sel_ref[s : s + 1, :] == subs(own, pick) + tensor * own).astype(F32).astype(BF)
            base = (d_rows_ref if s == 0 else far_ref)[...].astype(F32)
            out_ref[s] = base + dot(table, d_picked[s * pick : (s + 1) * pick])

    @pl.when(section != 0)
    def _():
        out_ref[0] = sent_ref[...].astype(F32)
        out_ref[1] = result_ref[...]


def finish(info, own, other, d_mid, picked, gains, sel_row, d_rows, far, sent, result):
    rows, d = d_rows.shape
    return pl.pallas_call(
        finish_kernel,
        out_shape=shape((2, rows, d), F32),
        in_specs=[SM] + [VM] * 10,
        out_specs=VM,
        compiler_params=params(),
        cost_estimate=cost(6),
        name="finish",
    )(info, own, other, d_mid, picked, gains, sel_row, d_rows, far, sent, result)


def pack_kernel(gains_ref, qkv_ref, mix_ref, out_ref):
    cols, d = mix_ref.shape
    for n in range(3):
        out_ref[n * cols : (n + 1) * cols, :] = qkv_ref[n]
    out_ref[3 * cols : 4 * cols, :] = mix_ref[...]
    rows = subs(16, d)
    extra = jnp.zeros((16, d), F32)
    for n in range(3):
        for p, piece in enumerate(three_pieces(gains_ref[n : n + 1, :])):
            extra = jnp.where(rows == 3 * n + p, piece.astype(F32), extra)
    out_ref[4 * cols :, :] = extra.astype(BF)


def pack_weights(gains, qkv_w, mix_w):
    cols, d = mix_w.shape
    return pl.pallas_call(
        pack_kernel,
        out_shape=shape((4 * cols + 16, d), BF),
        in_specs=[VM] * 3,
        out_specs=VM,
        compiler_params=params(),
        cost_estimate=cost(2),
        name="pack",
    )(gains, qkv_w, mix_w)


def prepare_kernel(info, g0, q0, m0, far_ref, gains_ref, qkv_ref, mix_ref):
    cols = m0.shape[0]
    own = info[1] == 1
    extra = far_ref[4 * cols :, :].astype(F32)
    for n in range(3):
        far = (extra[3 * n : 3 * n + 1] + extra[3 * n + 1 : 3 * n + 2]) + extra[3 * n + 2 : 3 * n + 3]
        gains_ref[n : n + 1, :] = jnp.where(own, g0[n : n + 1, :], far)
    qkv_ref[...] = jnp.zeros_like(qkv_ref)
    for n in range(3):
        qkv_ref[n, :cols, :] = jnp.where(own, q0[n], far_ref[n * cols : (n + 1) * cols, :])
    mix_ref[...] = jnp.zeros_like(mix_ref)
    mix_ref[:cols, :] = jnp.where(own, m0[...], far_ref[3 * cols : 4 * cols, :])


def prepare(info, gains, qkv_w, mix_w, far):
    d = mix_w.shape[1]
    return pl.pallas_call(
        prepare_kernel,
        out_shape=(shape(gains.shape, F32), shape((3, PAD, d), BF), shape((PAD, d), BF)),
        in_specs=[SM] + [VM] * 4,
        out_specs=(VM,) * 3,
        compiler_params=params(),
        cost_estimate=cost(2),
        name="prepare",
    )(info, gains, qkv_w, mix_w, far)


def project_kernel(
    heads, width, info, tok0, tok1, tok2a, tok2b, tok3a, tok3b, upd_own, upd_other, sel_ref,
    gains_ref, qkv_ref, rows_ref, normed_ref, q_ref, k_ref, v_ref, buf,
):
    tensor, low, length = info[0], info[2], info[3]
    r = pl.program_id(0)
    own, d = buf.shape
    for i, tok in enumerate((tok0, tok1)):
        @pl.when(r == i)
        def _():
            buf[...] = tok[...]

    for i, tok_a, tok_b in ((2, tok2a, tok2b), (3, tok3a, tok3b)):
        @pl.when(r == i)
        def _():
            buf[: own // 2] = tok_a[...]
            buf[own // 2 :] = tok_b[...]

    place = jnp.bitwise_xor(r, tensor) * own
    pick = sel_ref.shape[1]
    first, second = upd_own[...], upd_other[...]
    update = jnp.concatenate(
        [jnp.where(low == 0, first, second), jnp.where(low == 0, second, first)], 0
    )
    sel = jnp.where(info[1] == 0, sel_ref[0:1, :], sel_ref[1:2, :])
    table = (sel == subs(own, pick) + place).astype(F32).astype(BF)
    rows = (buf[...].astype(F32) + dot(table, update)).astype(BF)

    @pl.when(r == 0)
    def _():
        rows_ref[...] = rows

    unit, _ = unit_rows(rows.astype(F32))
    normed = (unit * gains_ref[0:1, :]).astype(BF)
    normed_ref[0] = normed
    lane = lanes(own, PAD)
    cols = heads * width
    one, zero = jnp.float32(1), jnp.float32(0)
    q = dot_nt(normed, qkv_ref[0]).astype(BF).astype(F32) * width ** (-0.5)
    q_ref[0] = jnp.where(lane == cols + 3, one, q).astype(BF)
    key_at = subs(own, PAD) + place
    extra = jnp.where(lane < cols + 3, one, jnp.where(key_at < length, zero, NEGATIVE))
    k = dot_nt(normed, qkv_ref[1])
    k_ref[0] = jnp.where((lane >= cols) & (lane < cols + 4), extra, k).astype(BF)
    v = dot_nt(normed, qkv_ref[2])
    v_ref[0] = jnp.where((lane >= cols) & (lane < cols + 3), one, v).astype(BF)


def project(info, toks, upd_own, upd_other, sel, gains, qkv_w, heads, width, count):
    own, d = toks[0].shape
    full = lambda dims: pl.BlockSpec(dims, lambda r, info: (0,) * len(dims))
    placed = lambda w: pl.BlockSpec((1, own, w), lambda r, info: (jnp.bitwise_xor(r, info[0]), 0, 0))
    padded = shape((count, own, PAD), BF)
    return pl.pallas_call(
        functools.partial(project_kernel, heads, width),
        out_shape=(shape((own, d), BF), shape((count, own, d), BF), padded, padded, padded),
        grid_spec=pltpu.PrefetchScalarGridSpec(
            num_scalar_prefetch=1,
            grid=(count,),
            in_specs=[full(tok.shape) for tok in toks]
            + [full(upd_own.shape)] * 2
            + [full(sel.shape), full(gains.shape), full(qkv_w.shape)],
            out_specs=(full((own, d)), placed(d), placed(PAD), placed(PAD), placed(PAD)),
            scratch_shapes=[pltpu.VMEM((own, d), BF)],
        ),
        compiler_params=params(grid=1),
        cost_estimate=cost(9),
        name="project",
    )(info, *toks, upd_own, upd_other, sel, gains, qkv_w)


def attention_kernel(
    heads, width, base, per, info, q_ref, k_ref, v_ref, mix_ref,
    send_ref, keep_ref, mixed_ref, lse_ref,
):
    i = pl.program_id(0)
    block = q_ref.shape[1]
    cols = heads * width
    steps = k_ref.shape[0] // block
    place = jnp.bitwise_xor(base + 1 - i // per, info[0]) * per + i % per

    def run(step):
        span = (step + 1) * block
        q = q_ref[0]
        lane = lanes(block, PAD)
        total = jnp.zeros((block, PAD), F32)
        lse = jnp.zeros((block, 128), F32)
        zero = jnp.zeros_like(q)
        for h in range(heads):
            here = (lane >= h * width) & (lane < (h + 1) * width)
            qh = jnp.where(here | (lane == cols + 3), q, zero)
            scores = dot_nt(qh, k_ref[0:span, :])
            causal = lanes(block, block) <= subs(block, block)
            tail = jnp.where(causal, scores[:, span - block :], NEGATIVE)
            high = jnp.max(tail, axis=-1, keepdims=True)
            if step:
                high = jnp.maximum(high, jnp.max(scores[:, : span - block], axis=-1, keepdims=True))
            probs = jnp.exp(tail - high).astype(BF)
            if step:
                probs = jnp.concatenate(
                    [jnp.exp(scores[:, : span - block] - high).astype(BF), probs], 1
                )
            out = dot(probs, v_ref[0:span, :])
            norm = jnp.sum(jnp.where(lane == cols, out, 0.0), axis=-1, keepdims=True)
            total = jnp.where(here, out / norm, total)
            lse = jnp.where(lanes(block, 128) == h, high + jnp.log(norm), lse)
        lse_ref[0] = lse
        mixed = total.astype(BF)
        mixed_ref[0] = mixed
        part = dot(mixed, mix_ref[...]).astype(BF)

        @pl.when(i < per)
        def _():
            send_ref[...] = part

        @pl.when(i >= per)
        def _():
            keep_ref[...] = part

    for step in range(steps):
        @pl.when(place == step)
        def _():
            run(step)


def attention(info, q, k, v, mix_w, heads, width, base, block=256):
    count, own, _ = q.shape
    total = count * own
    d = mix_w.shape[1]
    per = own // block
    k, v = k.reshape(total, PAD), v.reshape(total, PAD)
    full = lambda dims: pl.BlockSpec(dims, lambda i, info: (0,) * len(dims))
    rel = lambda w: pl.BlockSpec((1, block, w), lambda i, info: (1 - i // per, i % per, 0))
    out = shape((own, d), BF)
    return pl.pallas_call(
        functools.partial(attention_kernel, heads, width, base, per),
        out_shape=(out, out, shape((2, own, PAD), BF), shape((2, own, 128), F32)),
        grid_spec=pltpu.PrefetchScalarGridSpec(
            num_scalar_prefetch=1,
            grid=(2 * per,),
            in_specs=[
                pl.BlockSpec(
                    (1, block, PAD),
                    lambda i, info: (
                        jnp.bitwise_xor(base + 1 - i // per, info[0]), i % per, 0,
                    ),
                ),
                full(k.shape), full(v.shape), full(mix_w.shape),
            ],
            out_specs=(
                pl.BlockSpec((block, d), lambda i, info: (jnp.minimum(i, per - 1), 0)),
                pl.BlockSpec((block, d), lambda i, info: (jnp.maximum(i - per, 0), 0)),
                rel(PAD), rel(128),
            ),
        ),
        compiler_params=params(grid=1),
        cost_estimate=cost(0.3),
        name="attention",
    )(info, q, k, v, mix_w)


def mlp_kernel(
    half, rows_ref, keep_ref, near_ref, far_ref, cot_ref, gains_ref,
    p0a, p0b, p1a, p1b, p2a, p2b, p3a, p3b,
    result_ref, low_ref, d_mid_ref, d_mid_low_ref, keep_out, send_out,
    vec_ref, up_v, down_v, slope_v, act_v, pre_v, rows_v, result_v, low_v, sems, out_sems,
):
    leaving = []

    def leave(src, dst):
        copy = pltpu.make_async_copy(src, dst, out_sems.at[len(leaving)])
        copy.start()
        leaving.append(copy)

    parity = lax.axis_index("dp") & 1
    first = pl.ds(pl.multiple_of(parity * half, half), half)
    second = pl.ds(pl.multiple_of((1 - parity) * half, half), half)
    copies = {}
    count = 0
    for i in range(4):
        for n, (name, dest) in enumerate((("up", up_v), ("down", down_v))):
            a, b = ((p0a, p0b), (p1a, p1b), (p2a, p2b), (p3a, p3b))[i]
            moves = [(a.at[n], dest.at[i, first, :]), (b.at[n], dest.at[i, second, :])]
            some = []
            for src, dst in moves:
                copy = pltpu.make_async_copy(src, dst, sems.at[count])
                copy.start()
                some.append(copy)
                count += 1
            copies[name, i] = some
    attn = keep_ref[...].astype(F32) + near_ref[...].astype(F32) + far_ref[...].astype(F32)
    middle = rows_ref[...].astype(F32) + attn
    unit2, scale2 = unit_rows(middle)
    normed = (unit2 * gains_ref[1:2, :]).astype(BF)
    rows_v[0] = normed
    leave(rows_v.at[0], send_out.at[4])
    mlp = jnp.zeros_like(middle)
    for i in range(4):
        for copy in copies["up", i]:
            copy.wait()
        act, slope = gelu_pair(dot(normed, up_v[i]))
        act = act.astype(BF)
        act_v[i] = act
        leave(act_v.at[i], (keep_out if i % 2 == 0 else send_out).at[i // 2])
        slope_v[i] = slope
        for copy in copies["down", i]:
            copy.wait()
        mlp = mlp + dot(act, down_v[i])
    unit3, scale3 = unit_rows(middle + mlp)
    gain3 = gains_ref[2:3, :]
    result = unit3 * gain3
    result_v[...] = result
    leave(result_v, result_ref)
    low_v[...] = result.astype(BF)
    leave(low_v, low_ref)
    cot = cot_ref[0].astype(F32)
    vec_ref[1:2, :] = jnp.sum(cot * unit3, axis=0, keepdims=True)
    d_final = norm_back(unit3, scale3, gain3, cot)
    d_mlp = d_final.astype(BF)
    rows_v[1] = d_mlp
    leave(rows_v.at[1], send_out.at[5])
    d_normed = jnp.zeros_like(middle)
    for i in range(4):
        d_pre = (dot_nt(d_mlp, down_v[i]) * slope_v[i]).astype(BF)
        pre_v[i] = d_pre
        leave(pre_v.at[i], (keep_out if i % 2 == 0 else send_out).at[2 + i // 2])
        d_normed = d_normed + dot_nt(d_pre, up_v[i])
    vec_ref[0:1, :] = jnp.sum(d_normed * unit2, axis=0, keepdims=True)
    d_mid = d_final + norm_back(unit2, scale2, gains_ref[1:2, :], d_normed)
    d_mid_ref[...] = d_mid
    low = d_mid.astype(BF)
    d_mid_low_ref[...] = low
    rows_v[2] = low
    leave(rows_v.at[2], send_out.at[6])
    for copy in leaving:
        copy.wait()


def mlp_pass(rows, keep, near, far, cot, gains, pieces):
    own, d = rows.shape
    hidden = pieces[0].shape[2]
    half = d // 2
    wide, low = shape((own, d), F32), shape((own, d), BF)
    return pl.pallas_call(
        functools.partial(mlp_kernel, half),
        out_shape=(
            wide, low, wide, low, shape((4, own, d), BF), shape((7, own, d), BF), shape((2, d), F32)
        ),
        in_specs=[VM] * 6 + [HB] * 8,
        out_specs=(HB, HB, VM, VM, HB, HB, VM),
        scratch_shapes=[
            pltpu.VMEM((4, d, hidden), BF),
            pltpu.VMEM((4, hidden, d), BF),
            pltpu.VMEM((4, own, hidden), F32),
            pltpu.VMEM((4, own, hidden), BF),
            pltpu.VMEM((4, own, hidden), BF),
            pltpu.VMEM((3, own, d), BF),
            pltpu.VMEM((own, d), F32),
            pltpu.VMEM((own, d), BF),
            pltpu.SemaphoreType.DMA((16,)),
            pltpu.SemaphoreType.DMA((13,)),
        ],
        compiler_params=params(60),
        cost_estimate=cost(21),
        name="dense_mlp",
    )(rows, keep, near, far, cot, gains, *pieces)


FIRST = 8


def far_grads_kernel(
    act_ref, pre_ref, near_ref, own_ref, act2_ref, pre2_ref, near2_ref, rows2_ref,
    cross_ref, hop_ref, first_ref,
):
    i = pl.program_id(0)
    d = own_ref.shape[2]
    part = first_ref.shape[0]

    @pl.when(i == 0)
    def _():
        up = dot_tn(own_ref[0], pre_ref[0]) + dot_tn(rows2_ref[0], pre2_ref[0])
        cross_ref[:d] = up.astype(BF)

    @pl.when(i == 1)
    def _():
        rows, rows2 = own_ref[0], rows2_ref[0]
        down = (dot_tn(rows, act_ref[0]) + dot_tn(rows2, act2_ref[0])).astype(BF)
        cross_ref[d:] = down[:part]
        hop_ref[0] = down[part:]
        near = (dot_tn(rows, near_ref[0]) + dot_tn(rows2, near2_ref[0])).astype(BF)
        first_ref[...] = near[:part]
        hop_ref[1] = near[part:]


def near_grads_kernel(pre_ref, own_ref, pre2_ref, rows2_ref, first_ref, crossed_ref, out_ref):
    d = own_ref.shape[2]
    up = dot_tn(own_ref[0], pre_ref[0]) + dot_tn(rows2_ref[0], pre2_ref[0])
    out_ref[:d] = (up + crossed_ref[:d].astype(F32)).astype(BF)
    out_ref[d:] = (first_ref[...].astype(F32) + crossed_ref[d:].astype(F32)).astype(BF)


def far_grads(keep, send, other):
    _, own, d = keep.shape
    part = d // FIRST
    at = lambda n: pl.BlockSpec((1, own, d), lambda i: (n, 0, 0))
    pair = pl.BlockSpec((1, own, d), lambda i: (4 + i, 0, 0))
    return pl.pallas_call(
        far_grads_kernel,
        out_shape=(
            shape((d + part, d), BF), shape((2, d - part, d), BF), shape((part, d), BF)
        ),
        grid=(2,),
        in_specs=[at(1), at(3), at(0), pair, at(1), at(3), at(0), pair],
        out_specs=(
            pl.BlockSpec((d + part, d), lambda i: (0, 0)),
            pl.BlockSpec((2, d - part, d), lambda i: (0, 0, 0)),
            pl.BlockSpec((part, d), lambda i: (0, 0)),
        ),
        compiler_params=params(56, grid=1),
        cost_estimate=cost(5),
        name="far_grads",
    )(keep, keep, keep, send, other, other, other, other)


def near_grads(keep, send, other, first, crossed):
    _, own, d = keep.shape
    at = lambda n: pl.BlockSpec((1, own, d), lambda i: (n, 0, 0))
    full = lambda a: pl.BlockSpec(a.shape, lambda i: (0, 0))
    return pl.pallas_call(
        near_grads_kernel,
        out_shape=shape(crossed.shape, BF),
        grid=(1,),
        in_specs=[at(2), at(4), at(2), at(4), full(first), full(crossed)],
        out_specs=full(crossed),
        compiler_params=params(56, grid=1),
        cost_estimate=cost(5),
        name="near_grads",
    )(keep, send, other, other, first, crossed)


def attention_back_kernel(
    heads, width, block, info, g0, g1, g2, g3, q_ref, k_ref, v_ref, mixed_n, mixed_f, lse_n, lse_f,
    mix_ref, qkv_ref, sel_ref, d_qkv_ref, keep_ref, send_ref, mid_ref,
    qs, ds, dq_acc, dk_acc, dv_acc,
):
    tensor, low = info[0], info[2]
    own = g0.shape[0]
    cols = heads * width
    total = k_ref.shape[0]
    lane = lanes(own, PAD)
    zero = jnp.zeros((own, PAD), BF)
    grads = (g0[...], g1[0], g2[...], g3[...])
    for r, grad in enumerate(grads):
        at = pl.multiple_of(jnp.bitwise_xor(tensor, r) * own, own)
        span = pl.ds(at, own)
        d_mixed = dot_nt(grad, mix_ref[...]).astype(BF)
        inner = d_mixed.astype(F32) * (mixed_n if r < 2 else mixed_f)[r % 2].astype(F32)
        q = q_ref[span, :]
        lse = (lse_n if r < 2 else lse_f)[r % 2]
        for h in range(heads):
            here = (lane >= h * width) & (lane < (h + 1) * width)
            delta = -jnp.sum(jnp.where(here, inner, 0.0), axis=-1, keepdims=True)
            row_lse = -jnp.sum(jnp.where(lanes(own, 128) == h, lse, 0.0), axis=-1, keepdims=True)
            left = jnp.where(here | (lane == cols + 3), q, zero)
            right = jnp.where(here, d_mixed, zero)
            for p, (a, b) in enumerate(zip(three_pieces(row_lse), three_pieces(delta))):
                left = jnp.where(lane == cols + p, a, left)
                right = jnp.where(lane == cols + p, b, right)
            qs[h, span, :] = left
            ds[h, span, :] = right
    dq_acc[...] = jnp.zeros_like(dq_acc)
    lane_k = lanes(block, PAD)
    allowed = subs(block, block) <= lanes(block, block)
    for j in range(total // block):
        first = j * block
        k, v = k_ref[first : first + block, :], v_ref[first : first + block, :]
        dk = jnp.zeros((block, PAD), F32)
        dv = jnp.zeros((block, PAD), F32)
        stacked, keys = [], []
        for h in range(heads):
            qh, dh = qs[h, first:, :], ds[h, first:, :]
            scores = dot_nt(k, qh)
            d_probs = dot_nt(v, dh)
            head = jnp.where(allowed, scores[:, :block], NEGATIVE)
            probs = jnp.exp(head)
            if first + block < total:
                probs = jnp.concatenate([probs, jnp.exp(scores[:, block:])], 1)
            d_scores = (probs * d_probs).astype(BF)
            dv = dv + dot(probs.astype(BF), dh)
            dk = dk + dot(d_scores, qh)
            stacked.append(d_scores)
            keys.append(
                jnp.where((lane_k >= h * width) & (lane_k < (h + 1) * width), k, jnp.zeros_like(k))
            )
        dq_acc[first:, :] += dot_tn(jnp.concatenate(stacked, 0), jnp.concatenate(keys, 0))
        dk_acc[...] = dk
        dv_acc[...] = dv
        d_qkv_ref[1, first : first + block, :] = dk_acc[:, :cols].astype(BF)
        d_qkv_ref[2, first : first + block, :] = dv_acc[:, :cols].astype(BF)
    d_qkv_ref[0] = (dq_acc[:, :cols] * width ** (-0.5)).astype(BF)
    pick = sel_ref.shape[1]
    sel = jnp.where(info[1] == 0, sel_ref[0:1, :], sel_ref[1:2, :])
    table = (sel == subs(total, pick)).astype(F32).astype(BF)
    part = jnp.zeros((pick, qkv_ref.shape[2]), F32)
    for i in range(3):
        part = part + dot(dot_tn(table, d_qkv_ref[i]).astype(BF), qkv_ref[i][:cols, :])
    half = pick // 2
    keep_ref[...] = jnp.where(low == 0, part[:half], part[half:]).astype(BF)
    send_ref[...] = jnp.where(low == 0, part[half:], part[:half]).astype(BF)
    mine = jnp.where(low == 0, sel[:, :half], sel[:, half:])
    mid = jnp.zeros((half, qkv_ref.shape[2]), F32)
    for r, grad in enumerate(grads):
        table = (mine == subs(own, half) + jnp.bitwise_xor(tensor, r) * own).astype(F32).astype(BF)
        mid = mid + dot_tn(table, grad)
    mid_ref[...] = mid.astype(BF)


def attention_back(
    info, grads, q, k, v, mixed, lse, mix_w, qkv_w, selected, heads, width, block=256
):
    keep, other, far, far_other = grads
    own, d = keep.shape
    total = k.shape[0] * k.shape[1]
    flat = lambda a: a.reshape(total, PAD)
    half = shape((selected.shape[1] // 2, d), BF)
    at = lambda n: pl.BlockSpec((1, own, d), lambda i: (n, 0, 0))
    full = lambda a: pl.BlockSpec(a.shape, lambda i: (0,) * a.ndim)
    rest = (flat(q), flat(k), flat(v), *mixed, *lse, mix_w, qkv_w, selected)
    return pl.pallas_call(
        functools.partial(attention_back_kernel, heads, width, block),
        out_shape=(shape((3, total, heads * width), BF), half, half, half),
        grid=(1,),
        in_specs=[SM, full(keep), at(6), full(far), full(far_other)] + [full(a) for a in rest],
        out_specs=(
            pl.BlockSpec((3, total, heads * width), lambda i: (0, 0, 0)),
        ) + (pl.BlockSpec(half.shape, lambda i: (0, 0)),) * 3,
        scratch_shapes=[
            pltpu.VMEM((heads, total, PAD), BF),
            pltpu.VMEM((heads, total, PAD), BF),
            pltpu.VMEM((total, PAD), F32),
            pltpu.VMEM((block, PAD), F32),
            pltpu.VMEM((block, PAD), F32),
        ],
        compiler_params=params(60, grid=1),
        cost_estimate=cost(35),
        name="attention_back",
    )(info, keep, other, far, far_other, *rest)


def spread_back_kernel(cols, info, d_ref, qkv_ref, send_ref, keep_ref):
    i = pl.program_id(0)
    total = dot(d_ref[0, 0], qkv_ref[0][:cols, :])
    for n in (1, 2):
        total = total + dot(d_ref[n, 0], qkv_ref[n][:cols, :])
    total = total.astype(BF)

    @pl.when(i < 2)
    def _():
        send_ref[0] = total

    @pl.when(i >= 2)
    def _():
        keep_ref[0] = total


def spread_back(info, d_qkv, qkv_w, count):
    _, total, cols = d_qkv.shape
    own = total // count
    d = qkv_w.shape[2]
    pos = lambda i: jnp.where(i < 2, 3 - 2 * i, 6 - 2 * i)
    out = shape((2, own, d), BF)
    return pl.pallas_call(
        functools.partial(spread_back_kernel, cols),
        out_shape=(out, out),
        grid_spec=pltpu.PrefetchScalarGridSpec(
            num_scalar_prefetch=1,
            grid=(count,),
            in_specs=[
                pl.BlockSpec(
                    (3, 1, own, cols), lambda i, info: (0, jnp.bitwise_xor(pos(i), info[0]), 0, 0)
                ),
                pl.BlockSpec(qkv_w.shape, lambda i, info: (0, 0, 0)),
            ],
            out_specs=(
                pl.BlockSpec((1, own, d), lambda i, info: (1 - jnp.minimum(i, 1), 0, 0)),
                pl.BlockSpec((1, own, d), lambda i, info: (1 - jnp.maximum(i - 2, 0), 0, 0)),
            ),
        ),
        compiler_params=params(grid=1),
        cost_estimate=cost(5),
        name="spread_back",
    )(info, d_qkv.reshape(3, count, own, cols), qkv_w)


def attn_grads_kernel(
    cols, info, d_ref, normed_ref, g0, g1, g2, g3, mixed_n, mixed_f, pack_ref, acc,
):
    i = pl.program_id(0)

    @pl.when(i == 0)
    def _():
        acc[...] = jnp.zeros_like(acc)

    for n in range(3):
        acc[n * cols : (n + 1) * cols, :] += dot_tn(d_ref[n, 0], normed_ref[0])
    for r, grad in enumerate((g0, g1, g2, g3)):
        @pl.when(i == r)
        def _():
            mixed = (mixed_n if r < 2 else mixed_f)[r % 2]
            rows = grad[0] if r == 1 else grad[...]
            acc[3 * cols :, :] += dot_tn(mixed[:, :cols], rows)

    @pl.when(i == 3)
    def _():
        pack_ref[...] = jnp.transpose(acc[...]).astype(BF)


def attn_grads(info, d_qkv, normed, grads, mixed):
    _, total, cols = d_qkv.shape
    count, own, d = normed.shape
    full = lambda dims: pl.BlockSpec(dims, lambda i, info: (0,) * len(dims))
    return pl.pallas_call(
        functools.partial(attn_grads_kernel, cols),
        out_shape=shape((d, 4 * cols), BF),
        grid_spec=pltpu.PrefetchScalarGridSpec(
            num_scalar_prefetch=1,
            grid=(count,),
            in_specs=[
                pl.BlockSpec(
                    (3, 1, own, cols), lambda i, info: (0, jnp.bitwise_xor(i, info[0]), 0, 0)
                ),
                pl.BlockSpec((1, own, d), lambda i, info: (jnp.bitwise_xor(i, info[0]), 0, 0)),
            ]
            + [
                full((own, d)), pl.BlockSpec((1, own, d), lambda i, info: (6, 0, 0)),
                full((own, d)), full((own, d)),
            ]
            + [full(mixed[0].shape)] * 2,
            out_specs=full((d, 4 * cols)),
            scratch_shapes=[pltpu.VMEM((4 * cols, d), F32)],
        ),
        compiler_params=params(grid=1),
        cost_estimate=cost(8),
        name="attn_grads",
    )(info, d_qkv.reshape(3, count, own, cols), normed, *grads, *mixed)


def routed_mlp_grads_kernel(
    info, normed_ref, pre_ref, act_ref, grad_ref, part_ref, far_ref, last_ref, last_far, last_cross,
    pack_ref,
):
    hidden = pre_ref.shape[1]

    @pl.when(info[1] == 0)
    def _():
        pack_ref[:, :hidden] = dot_tn(normed_ref[...], pre_ref[...]).astype(BF)
        pack_ref[:, hidden:] = dot_tn(grad_ref[...], act_ref[...]).astype(BF)

    @pl.when(info[1] != 0)
    def _():
        d = normed_ref.shape[1]
        total = (part_ref[...].astype(F32) + far_ref[...].astype(F32)).astype(BF)
        part = part_ref.shape[0] - d
        pack_ref[:, :hidden] = total[:d]
        pack_ref[:part, hidden:] = total[d:]
        total = last_ref[1].astype(F32) + last_far[1].astype(F32) + last_cross[...].astype(F32)
        pack_ref[part:, hidden:] = total.astype(BF)


def routed_mlp_grads(info, normed, pre, act, grad, *dense):
    return pl.pallas_call(
        routed_mlp_grads_kernel,
        out_shape=shape((normed.shape[1], 2 * pre.shape[1]), BF),
        in_specs=[SM] + [VM] * 9,
        out_specs=VM,
        compiler_params=params(),
        cost_estimate=cost(5),
        name="routed_mlp_grads",
    )(info, normed, pre, act, grad, *dense)


def routed_attn_grads_kernel(
    info, normed_ref, d_ref, low_ref, mixed_ref, part_ref, hop_ref, vec_ref, pack_ref
):
    cols = mixed_ref.shape[1]
    wide = 4 * cols
    vecs = jnp.concatenate(
        [vec_ref[...], jnp.zeros((128 - vec_ref.shape[0], vec_ref.shape[1]), F32)], 0
    )
    pack_ref[:, wide:] = jnp.transpose(vecs).astype(BF)

    @pl.when(info[1] == 0)
    def _():
        rows = [dot_tn(d_ref[n], normed_ref[...]) for n in range(3)]
        rows.append(dot_tn(mixed_ref[...], low_ref[...]))
        pack_ref[:, :wide] = jnp.transpose(jnp.concatenate(rows, 0)).astype(BF)

    @pl.when(info[1] != 0)
    def _():
        pack_ref[:, :wide] = (part_ref[...].astype(F32) + hop_ref[...].astype(F32)).astype(BF)


def routed_attn_grads(info, normed, d_qkv, d_low, mixed, part, far, vecs):
    return pl.pallas_call(
        routed_attn_grads_kernel,
        out_shape=shape((normed.shape[1], 4 * mixed.shape[1] + 128), BF),
        in_specs=[SM] + [VM] * 7,
        out_specs=VM,
        compiler_params=params(),
        cost_estimate=cost(3),
        name="routed_attn_grads",
    )(info, normed, d_qkv, d_low, mixed, part, far, vecs)


def rows_back_kernel(keep_ref, near_ref, far_ref, rows_ref, d_mid_ref, gains_ref, d_rows_ref, vec_ref):
    d_normed = keep_ref[0].astype(F32) + near_ref[0].astype(F32) + far_ref[...].astype(F32)
    unit, scale = unit_rows(rows_ref[...].astype(F32))
    vec_ref[...] = jnp.sum(d_normed * unit, axis=0, keepdims=True)
    d_rows = d_mid_ref[...] + norm_back(unit, scale, gains_ref[0:1, :], d_normed)
    d_rows_ref[...] = d_rows.astype(BF)


def rows_back(keep, near, far, rows, d_mid, gains):
    own, d = rows.shape
    return pl.pallas_call(
        rows_back_kernel,
        out_shape=(shape((own, d), BF), shape((1, d), F32)),
        in_specs=[VM] * 6,
        out_specs=(VM, VM),
        compiler_params=params(),
        cost_estimate=cost(4),
        name="rows_back",
    )(keep, near, far, rows, d_mid, gains)


def sel_back_kernel(near_ref, far_ref, picked_ref, upd_ref, mid_ref, gains_ref, out_ref):
    d_normed = near_ref[...].astype(F32) + far_ref[...].astype(F32)
    rows = (picked_ref[...].astype(F32) + upd_ref[...].astype(F32)).astype(BF).astype(F32)
    unit, scale = unit_rows(rows)
    d_rows = mid_ref[...].astype(F32) + norm_back(unit, scale, gains_ref[0:1, :], d_normed)
    out_ref[...] = d_rows.astype(BF)


def sel_back(near, far, picked, upd, mid, gains):
    return pl.pallas_call(
        sel_back_kernel,
        out_shape=shape(near.shape, BF),
        in_specs=[VM] * 6,
        out_specs=VM,
        compiler_params=params(),
        cost_estimate=cost(2.3),
        name="sel_back",
    )(near, far, picked, upd, mid, gains)


def add(a, b):
    return (a.astype(F32) + b.astype(F32)).astype(BF)


def core_sum(keep, send):
    return add(keep, swap(send, "tensor", 1))


def whole_sum(keep, send):
    near = core_sum(keep, send)
    return add(near, swap(near, "tensor", 2))


def scatter_groups(pack):
    count, me = lax.axis_size("dp"), lax.axis_index("dp")
    if count != 4:
        return lax.psum_scatter(pack, "dp", scatter_dimension=0, tiled=True)
    for bit in (1, 2):
        rows = pack.shape[0] // 2
        side = (me // bit) % 2
        if bit == 1:
            quarters = pack.reshape(2, 2, rows // 2, pack.shape[1])
            take = lambda at: lax.dynamic_index_in_dim(quarters, at, 1, keepdims=False)
            keep, send = take(side), take(1 - side)
        else:
            keep = lax.dynamic_index_in_dim(pack, side, 0, keepdims=False)
            send = lax.dynamic_index_in_dim(pack, 1 - side, 0, keepdims=False)
        pack = add(keep, swap(send, "dp", bit))
    return pack


def body(
    tokens, qkv_weight, out_weight, up_weight, down_weight, vectors, lengths, selected, cotangent
):
    section = lax.axis_index("section")
    tensor = lax.axis_index("tensor")
    group = lax.axis_size("dp")
    heads = HEADS // lax.axis_size("tensor")
    low = tensor & 1
    is_dense = section == 1
    gains = vectors[0]
    qkv_w = jnp.swapaxes(qkv_weight[0], 1, 2)
    mix_w, up_w, down_w = out_weight[0], up_weight[0], down_weight[0]
    cols = qkv_w.shape[1]
    width = cols // heads
    d = mix_w.shape[1]

    barrier = lax.optimization_barrier
    core = lambda block: swap(block, "tensor", 1)
    cross = lambda block: swap(block, "tensor", 2)

    halves = up_w.shape[0] // 2
    parity = lax.axis_index("dp") & 1
    take = lambda w, at: lax.dynamic_slice_in_dim(w, at * halves, halves, 0)
    mine = (take(up_w, parity), take(down_w, parity))
    up_far = hop(mine[0], 1, 0)
    down_far = hop(after(mine[1], up_far), 1, 0)

    near = core_sum(*pick_rows(tokens, selected))
    far = cross(near)
    info = jnp.stack([tensor, section, low, lengths[section]]).astype(jnp.int32)
    my_tokens = lax.dynamic_index_in_dim(tokens, section, 0, keepdims=False)
    part = my_tokens.shape[0] // 2
    tok_a, tok_b = my_tokens[:part], my_tokens[part:]
    far, my_tokens, info, tok_a, tok_b = barrier((far, my_tokens, info, tok_a, tok_b))
    tok2a = cross(after(tok_a, far))
    packed = pack_weights(gains, qkv_w, mix_w)
    picked_half = add(near, far)
    picked_other = core(picked_half)

    picked, normed, q, k, v, mixed, keep, send = routed_attn(
        info, picked_half, picked_other, gains, qkv_w, mix_w, heads
    )
    send, tok2a, up_far = barrier((send, tok2a, up_far))
    near = core_sum(keep, send)
    far = cross(near)
    far, packed, down_far = barrier((far, packed, down_far))
    attn_half = add(near, far)
    tok2b = cross(after(tok_b, far))
    tok1 = core(my_tokens)
    attn_other = core(attn_half)
    packed_far = hop(after(packed, down_far), 1, 0)
    attn, normed2, act, slope, keep, send = routed_mlp(
        info, picked, attn_half, attn_other, gains, up_w, down_w
    )
    piece0a = jnp.stack(
        [jnp.where(is_dense, own, far) for own, far in zip(mine, (up_far, down_far))]
    )
    send, tok2b = barrier((send, tok2b))
    near = core_sum(keep, send)
    far = cross(near)
    far, piece0a = barrier((far, piece0a))
    both_half, update_half = make_update(picked_half, attn_half, near, far, gains)
    piece2a = cross(after(piece0a, far))
    piece1a = core(piece0a)
    tok3a, tok3b = core(tok2a), core(tok2b)
    arrived = hop(update_half[1], 0, 1)
    my_update = jnp.where(is_dense, arrived, update_half[0])
    my_update, piece1a, packed_far = barrier((my_update, piece1a, packed_far))
    d_gains, d_qkv_w, d_mix_w = prepare(info, gains, qkv_w, mix_w, packed_far)
    my_update_other = core(my_update)
    my_update_other, d_gains = barrier((my_update_other, d_gains))
    toks = (my_tokens, tok1, tok2a, tok2b, tok3a, tok3b)

    piece0b = swap(piece0a, "dp", 1)
    piece2a, piece0b = barrier((after(piece2a, my_update_other), piece0b))
    piece2b = swap(piece2a, "dp", 1)

    rows, d_normed_rows, dq_in, dk_in, dv_in = project(
        info, toks, my_update, my_update_other, selected, d_gains, d_qkv_w, heads, width,
        lax.axis_size("tensor"),
    )
    send, keep, mixed_f, lse_f = attention(info, dq_in, dk_in, dv_in, d_mix_w, heads, width, 2)
    send, piece2b = barrier((send, piece2b))
    near = core_sum(keep, send)
    far = cross(near)
    send, keep, mixed_n, lse_n = attention(info, dq_in, dk_in, dv_in, d_mix_w, heads, width, 0)
    piece3a = core(after(piece2a, send))
    piece3b = core(after(piece2b, send))
    piece1b = core(after(piece0b, send))
    send, far = barrier((send, far))
    near = core(send)
    my_cot = lax.dynamic_slice_in_dim(cotangent, section, 1, 0)
    result, result_low, d_mid, d_mid_low, mlp_keep, mlp_send, m_vec = mlp_pass(
        rows, keep, near, far, my_cot, d_gains,
        (piece0a, piece0b, piece1a, piece1b, piece2a, piece2b, piece3a, piece3b),
    )
    grad_f = cross(d_mid_low)
    mlp_other = core(mlp_send)
    mlp_f, last, first = far_grads(mlp_keep, mlp_send, mlp_other)
    grad_f, mlp_f, last = barrier((grad_f, mlp_f, last))
    grads = (d_mid_low, mlp_other, grad_f, core(grad_f))
    mlp_f2 = cross(mlp_f)
    last_h = hop(last, 0, 1)

    d_qkv, keep, send, mid_sel = attention_back(
        info, grads, dq_in, dk_in, dv_in, (mixed_n, mixed_f), (lse_n, lse_f),
        d_mix_w, d_qkv_w, selected, heads, width,
    )
    near = core_sum(keep, send)
    far = cross(near)
    mlp_part = near_grads(mlp_keep, mlp_send, after(mlp_other, near), first, mlp_f2)
    last_f = add(last[0], after(last_h[0], mlp_part))
    far, mlp_part, last_f = barrier((far, mlp_part, last_f))
    last_f2 = cross(last_f)
    mlp_hop = hop(mlp_part, 0, 1)
    my_picked = lax.dynamic_index_in_dim(picked_half, section, 0, keepdims=False)
    my_d_sel = sel_back(near, far, my_picked, my_update, mid_sel, d_gains)
    back = hop(my_d_sel, 1, 0)
    attn_part = attn_grads(
        info, after(d_qkv, my_d_sel), d_normed_rows, grads, (mixed_n, mixed_f)
    )
    back, attn_part, last_f2 = barrier((back, attn_part, last_f2))
    sel_other = core(jnp.concatenate([my_d_sel[None], back[None], both_half], 0))

    d_sel, r_d_mlp, r_d_pre, gain_two, keep2, send2 = routed_back_mlp(
        info, my_d_sel, back, sel_other, picked, attn, gains, slope, up_w, down_w
    )
    send2, mlp_hop = barrier((send2, mlp_hop))
    near = core_sum(keep2, send2)
    far = cross(near)
    r_mlp = routed_mlp_grads(
        info, normed2, r_d_pre, act, r_d_mlp, mlp_part, mlp_hop, last, last_h, last_f2
    )
    row_send, row_keep = spread_back(info, after(d_qkv, r_mlp), d_qkv_w, 4)
    far, row_send = barrier((far, row_send))
    row_core = core(row_send)
    half = add(near, far)
    other = core(half)
    row_far = cross(add(row_keep[1], row_core[1]))
    attn_hop = hop(attn_part, 0, 1)
    hidden = up_w.shape[1]
    r_d_mid, r_d_low, r_d_qkv, r_vec, keep2, send2 = routed_back_attn(
        info, half, other, d_sel, picked, attn, both_half, sel_other, gains, q, k, v,
        qkv_w, mix_w, heads,
    )
    near = core_sum(keep2, send2)
    mlp_sum = lax.psum_scatter(r_mlp, "dp", scatter_dimension=0, tiled=True)
    near, row_far, attn_hop = barrier((near, row_far, attn_hop))
    far = cross(near)
    d_rows, row_vec = rows_back(row_keep, row_core, row_far, rows, d_mid, d_gains)
    d_rows_far = hop(d_rows, 1, 0)
    far, d_rows = barrier((far, d_rows))
    sent_result = hop(after(result_low, attn_hop), 0, 1)
    half = add(near, far)
    other = core(half)
    vecs = jnp.concatenate([r_vec[0:1], gain_two, r_vec[1:2], row_vec, m_vec], 0)
    vecs = vecs + swap(vecs, "tensor", 1)
    vecs = vecs + swap(vecs, "tensor", 2)
    r_attn = routed_attn_grads(
        info, normed, r_d_qkv, r_d_low, mixed, after(attn_part, half), attn_hop, vecs
    )
    attn_sum = scatter_groups(r_attn)

    combined = finish(
        info, half, other, r_d_mid, picked, gains, selected, d_rows, d_rows_far, sent_result, result
    )
    share = d // group
    up_grad = mlp_sum[:, :hidden].astype(F32)
    down_grad = jnp.swapaxes(mlp_sum[:, hidden:], 0, 1).astype(F32)
    qkv_grad = jnp.swapaxes(attn_sum[:, : 3 * cols].reshape(share, 3, cols), 0, 1).astype(F32)
    mix_grad = jnp.swapaxes(attn_sum[:, 3 * cols : 4 * cols], 0, 1).astype(F32)

    vecs = jnp.transpose(attn_sum[:, 4 * cols : 4 * cols + 8].astype(F32))
    dense_vec = vecs[3:6] + hop(vecs[3:6], 0, 1)
    vecs = jnp.where(is_dense, dense_vec, vecs[:3])
    return (
        combined[None],
        qkv_grad[None],
        mix_grad[None],
        up_grad[None],
        down_grad[None],
        vecs[None],
    )


def solution(mesh):
    placed = (
        P("dp", "tensor", None),
        P("section", None, None, "tensor"),
        P("section", "tensor", None),
        P("section", None, "tensor"),
        P("section", "tensor", None),
        P("section", None, None),
        P("dp"),
        P("dp", None),
        P("dp", "tensor", None),
    )
    return jax.shard_map(
        body,
        mesh=mesh,
        in_specs=placed,
        out_specs=(
            P("section", "dp", "tensor", None),
            P("section", None, "dp", "tensor"),
            P("section", "tensor", "dp"),
            P("section", "dp", "tensor"),
            P("section", "tensor", "dp"),
            P("section", None, "dp"),
        ),
        check_vma=False,
    )
```

```python
import functools

import jax
import jax.numpy as jnp
from jax import lax
from jax.experimental import pallas as pl
from jax.experimental.pallas import tpu as pltpu
from jax.sharding import PartitionSpec as P

HEADS = 12
EPSILON = 1e-06
NEGATIVE = -1e30
BF = jnp.bfloat16
F32 = jnp.float32
PAD = 256
MIB = 1 << 20


def swap(block, axis, bit):
    count = lax.axis_size(axis)
    return lax.ppermute(block, axis, [(i, i ^ bit) for i in range(count)])


def hop(block, source, target):
    return lax.ppermute(block, "section", [(source, target)])


def dot(left, right):
    return lax.dot_general(left, right, (((1,), (0,)), ((), ())), preferred_element_type=F32)


def dot_nt(left, right):
    return lax.dot_general(left, right, (((1,), (1,)), ((), ())), preferred_element_type=F32)


def dot_tn(left, right):
    return lax.dot_general(left, right, (((0,), (0,)), ((), ())), preferred_element_type=F32)


def unit_rows(values):
    scale = lax.rsqrt(jnp.mean(values * values, axis=-1, keepdims=True) + EPSILON)
    return values * scale, scale


def norm_back(unit, scale, gain, grad):
    e = grad * gain
    return scale * (e - unit * jnp.mean(e * unit, axis=-1, keepdims=True))


def gelu_pair(x):
    c = 0.7978845608028654
    a = 0.044715
    xx = x * x
    th = jnp.tanh(c * (x + a * (x * xx)))
    half = 0.5 * (1.0 + th)
    slope = half + (0.5 * x) * (1.0 - th * th) * (c * (1.0 + (3.0 * a) * xx))
    return x * half, slope


def lanes(rows, width):
    return lax.broadcasted_iota(jnp.int32, (rows, width), 1)


def subs(rows, width):
    return lax.broadcasted_iota(jnp.int32, (rows, width), 0)


def head_of(values, lane, head, width):
    zero = jnp.zeros_like(values)
    return jnp.where((lane >= head * width) & (lane < (head + 1) * width), values, zero)


def three_pieces(column):
    first = column.astype(BF)
    rest = column - first.astype(F32)
    second = rest.astype(BF)
    third = (rest - second.astype(F32)).astype(BF)
    return first, second, third


def params(limit=56, grid=None):
    if grid is None:
        return pltpu.CompilerParams(vmem_limit_bytes=limit * MIB)
    return pltpu.CompilerParams(
        vmem_limit_bytes=limit * MIB, dimension_semantics=("arbitrary",) * grid
    )


def cost(us):
    return pl.CostEstimate(
        flops=int(us * 1e8), bytes_accessed=int(us * 3.3e6), transcendentals=0
    )


def after(value, *others):
    return lax.optimization_barrier((value,) + others)[0]


VM = pl.BlockSpec(memory_space=pltpu.VMEM)
SM = pl.BlockSpec(memory_space=pltpu.SMEM)
HB = pl.BlockSpec(memory_space=pl.ANY)


def shape(dims, dtype):
    return jax.ShapeDtypeStruct(dims, dtype)


def halves_out(partial, low, keep_ref, send_ref):
    pick = partial.shape[0] // 2
    half = pick // 2
    for s in range(2):
        first = partial[s * pick : s * pick + half]
        second = partial[s * pick + half : (s + 1) * pick]
        keep_ref[s] = jnp.where(low == 0, first, second).astype(BF)
        send_ref[s] = jnp.where(low == 0, second, first).astype(BF)


def halves_in(own_ref, other_ref, low):
    parts = []
    for s in range(2):
        own, other = own_ref[s].astype(F32), other_ref[s].astype(F32)
        parts.append(jnp.where(low == 0, own, other))
        parts.append(jnp.where(low == 0, other, own))
    return jnp.concatenate(parts, 0)


def pick_kernel(rows_ref, sel_ref, keep_ref, send_ref):
    tensor = lax.axis_index("tensor")
    own = rows_ref.shape[1]
    pick = sel_ref.shape[1]
    parts = []
    for s in range(2):
        table = (sel_ref[s : s + 1, :] == subs(own, pick) + tensor * own).astype(F32).astype(BF)
        parts.append(dot_tn(table, rows_ref[s]))
    halves_out(jnp.concatenate(parts, 0), tensor & 1, keep_ref, send_ref)


def pick_rows(rows, selected):
    _, _, d = rows.shape
    out = shape((2, selected.shape[1] // 2, d), BF)
    return pl.pallas_call(
        pick_kernel,
        out_shape=(out, out),
        in_specs=[VM, VM],
        out_specs=(VM, VM),
        compiler_params=params(),
        cost_estimate=cost(3),
        name="pick",
    )(rows, selected)


def routed_attn_kernel(
    heads, info, own_ref, other_ref, gains_ref, qkv_ref, mix_ref,
    picked_ref, normed_ref, q_ref, k_ref, v_ref, mixed_ref, keep_ref, send_ref,
):
    low = info[2]
    picked = halves_in(own_ref, other_ref, low)
    picked_ref[...] = picked.astype(BF)
    unit, _ = unit_rows(picked)
    normed = (unit * gains_ref[0:1, :]).astype(BF)
    normed_ref[...] = normed
    width = qkv_ref.shape[1] // heads
    q = dot_nt(normed, qkv_ref[0]).astype(BF)
    k = dot_nt(normed, qkv_ref[1]).astype(BF)
    v = dot_nt(normed, qkv_ref[2]).astype(BF)
    q = (q.astype(F32) * width ** (-0.5)).astype(BF)
    q_ref[...] = q
    k_ref[...] = k
    v_ref[...] = v
    pick = picked.shape[0] // 2
    lane = lanes(pick, heads * width)
    allowed = lanes(pick, pick) <= subs(pick, pick)
    parts = []
    for s in range(2):
        span = slice(s * pick, (s + 1) * pick)
        total = jnp.zeros((pick, heads * width), F32)
        for h in range(heads):
            scores = dot_nt(head_of(q[span], lane, h, width), k[span])
            scores = jnp.where(allowed, scores, NEGATIVE)
            expos = jnp.exp(scores - jnp.max(scores, axis=-1, keepdims=True))
            probs = expos / jnp.sum(expos, axis=-1, keepdims=True)
            total = total + dot(probs.astype(BF), head_of(v[span], lane, h, width))
        parts.append(total.astype(BF))
    mixed = jnp.concatenate(parts, 0)
    mixed_ref[...] = mixed
    halves_out(dot(mixed, mix_ref[...]), low, keep_ref, send_ref)


def routed_attn(info, own, other, gains, qkv_w, mix_w, heads):
    _, half, d = own.shape
    rows = 4 * half
    cols = qkv_w.shape[1]
    part = shape((2, half, d), BF)
    wide, narrow = shape((rows, d), BF), shape((rows, cols), BF)
    return pl.pallas_call(
        functools.partial(routed_attn_kernel, heads),
        out_shape=(wide, wide, narrow, narrow, narrow, narrow, part, part),
        in_specs=[SM] + [VM] * 5,
        out_specs=(VM,) * 8,
        compiler_params=params(),
        cost_estimate=cost(5),
        name="routed_attn",
    )(info, own, other, gains, qkv_w, mix_w)


def routed_mlp_kernel(
    info, picked_ref, own_ref, other_ref, gains_ref, up_ref, down_ref,
    attn_ref, normed_ref, act_ref, slope_ref, keep_ref, send_ref,
):
    low = info[2]
    attn = halves_in(own_ref, other_ref, low)
    attn_ref[...] = attn.astype(BF)
    unit, _ = unit_rows(picked_ref[...].astype(F32) + attn)
    normed = (unit * gains_ref[1:2, :]).astype(BF)
    normed_ref[...] = normed
    act, slope = gelu_pair(dot(normed, up_ref[...]))
    act = act.astype(BF)
    act_ref[...] = act
    slope_ref[...] = slope
    halves_out(dot(act, down_ref[...]), low, keep_ref, send_ref)


def routed_mlp(info, picked, own, other, gains, up_w, down_w):
    rows, d = picked.shape
    hidden = up_w.shape[1]
    part = shape((2, rows // 4, d), BF)
    return pl.pallas_call(
        routed_mlp_kernel,
        out_shape=(
            shape((rows, d), BF), shape((rows, d), BF), shape((rows, hidden), BF),
            shape((rows, hidden), F32), part, part,
        ),
        in_specs=[SM] + [VM] * 6,
        out_specs=(VM,) * 6,
        compiler_params=params(),
        cost_estimate=cost(6),
        name="routed_mlp",
    )(info, picked, own, other, gains, up_w, down_w)


def update_kernel(picked_ref, attn_ref, mlp_ref, mlp2_ref, gains_ref, both_ref, update_ref):
    d = picked_ref.shape[2]
    weight = gains_ref[2:3, :] * d ** (-0.5)
    for s in range(2):
        router = jnp.sum(picked_ref[s].astype(F32) * weight, axis=-1, keepdims=True)
        both = attn_ref[s].astype(F32) + (mlp_ref[s].astype(F32) + mlp2_ref[s].astype(F32))
        both_ref[s] = both.astype(BF)
        update_ref[s] = (router * both).astype(BF)


def make_update(picked_half, attn_half, mlp_half, mlp_far, gains):
    out = shape(picked_half.shape, BF)
    return pl.pallas_call(
        update_kernel,
        out_shape=(out, out),
        in_specs=[VM] * 5,
        out_specs=(VM, VM),
        compiler_params=params(),
        cost_estimate=cost(2.5),
        name="update",
    )(picked_half, attn_half, mlp_half, mlp_far, gains)


def routed_back_mlp_kernel(
    info, sel_own, sel_back, sel_other, picked_ref, attn_ref, gains_ref, slope_ref, up_ref, down_ref,
    d_sel_ref, d_mlp_ref, d_pre_ref, gain_ref, keep_ref, send_ref,
):
    low = info[2]
    d = picked_ref.shape[1]
    parts = []
    for s, own in enumerate((sel_own[...], sel_back[...])):
        other = sel_other[s]
        parts += [jnp.where(low == 0, own, other), jnp.where(low == 0, other, own)]
    d_sel = jnp.concatenate(parts, 0).astype(F32)
    d_sel_ref[...] = d_sel
    picked = picked_ref[...].astype(F32)
    router = jnp.sum(picked * (gains_ref[2:3, :] * d ** (-0.5)), axis=-1, keepdims=True)
    d_mlp = (router * d_sel).astype(BF)
    d_mlp_ref[...] = d_mlp
    d_pre = (dot_nt(d_mlp, down_ref[...]) * slope_ref[...]).astype(BF)
    d_pre_ref[...] = d_pre
    d_normed = dot_nt(d_pre, up_ref[...])
    unit, _ = unit_rows(picked + attn_ref[...].astype(F32))
    gain_ref[...] = jnp.sum(d_normed * unit, axis=0, keepdims=True)
    halves_out(d_normed, low, keep_ref, send_ref)


def routed_back_mlp(info, sel_own, sel_back, sel_other, picked, attn, gains, slope, up_w, down_w):
    rows, d = picked.shape
    hidden = up_w.shape[1]
    part = shape((2, rows // 4, d), BF)
    return pl.pallas_call(
        routed_back_mlp_kernel,
        out_shape=(
            shape((rows, d), F32), shape((rows, d), BF), shape((rows, hidden), BF),
            shape((1, d), F32), part, part,
        ),
        in_specs=[SM] + [VM] * 9,
        out_specs=(VM,) * 6,
        compiler_params=params(),
        cost_estimate=cost(6),
        name="routed_back_mlp",
    )(info, sel_own, sel_back, sel_other, picked, attn, gains, slope, up_w, down_w)


def routed_back_attn_kernel(
    heads, info, own_ref, other_ref, d_sel_ref, picked_ref, attn_ref, both_own, both_other,
    gains_ref, q_ref, k_ref, v_ref, qkv_ref, mix_ref,
    d_mid_ref, d_low_ref, d_qkv_ref, vec_ref, keep_ref, send_ref,
):
    low = info[2]
    rows, d = picked_ref.shape
    d_normed2 = halves_in(own_ref, other_ref, low)
    picked = picked_ref[...].astype(F32)
    d_sel = d_sel_ref[...]
    router_row = gains_ref[2:3, :] * d ** (-0.5)
    router = jnp.sum(picked * router_row, axis=-1, keepdims=True)
    unit2, scale2 = unit_rows(picked + attn_ref[...].astype(F32))
    d_mid = norm_back(unit2, scale2, gains_ref[1:2, :], d_normed2)
    both = halves_in(both_own, both_other.at[2:], low)
    d_router = jnp.sum(d_sel * both, axis=-1, keepdims=True)
    d_mid_ref[...] = d_mid + d_router * router_row
    d_weight = jnp.sum(picked * d_router, axis=0, keepdims=True) * d ** (-0.5)
    vec_ref[1:2, :] = jnp.where(info[0] == 0, d_weight, jnp.zeros_like(d_weight))
    d_low = (router * d_sel + d_mid).astype(BF)
    d_low_ref[...] = d_low
    d_mixed = dot_nt(d_low, mix_ref[...]).astype(BF)
    width = qkv_ref.shape[1] // heads
    pick = rows // 2
    lane = lanes(pick, heads * width)
    allowed = subs(pick, pick) <= lanes(pick, pick)
    dq_parts, dk_parts, dv_parts = [], [], []
    for s in range(2):
        span = slice(s * pick, (s + 1) * pick)
        q, k, v, dm = q_ref[span, :], k_ref[span, :], v_ref[span, :], d_mixed[span]
        dq = jnp.zeros((pick, heads * width), F32)
        dk, dv = dq, dq
        for h in range(heads):
            qh, kh = head_of(q, lane, h, width), head_of(k, lane, h, width)
            dh = head_of(dm, lane, h, width)
            scores = jnp.where(allowed, dot_nt(k, qh), NEGATIVE)
            expos = jnp.exp(scores - jnp.max(scores, axis=0, keepdims=True))
            probs = expos / jnp.sum(expos, axis=0, keepdims=True)
            d_probs = dot_nt(v, dh)
            inner = jnp.sum(probs * d_probs, axis=0, keepdims=True)
            d_scores = (probs * (d_probs - inner)).astype(BF)
            dv = dv + dot(probs.astype(BF), dh)
            dk = dk + dot(d_scores, qh)
            dq = dq + dot_tn(d_scores, kh)
        dq_parts.append(dq * width ** (-0.5))
        dk_parts.append(dk)
        dv_parts.append(dv)
    d_normed = jnp.zeros((rows, d), F32)
    for i, parts in enumerate((dq_parts, dk_parts, dv_parts)):
        whole = jnp.concatenate(parts, 0).astype(BF)
        d_qkv_ref[i] = whole
        d_normed = d_normed + dot(whole, qkv_ref[i])
    unit, _ = unit_rows(picked)
    vec_ref[0:1, :] = jnp.sum(d_normed * unit, axis=0, keepdims=True)
    halves_out(d_normed, low, keep_ref, send_ref)


def routed_back_attn(
    info, own, other, d_sel, picked, attn, both_own, both_other, gains, q, k, v, qkv_w, mix_w, heads
):
    rows, d = picked.shape
    part = shape((2, rows // 4, d), BF)
    return pl.pallas_call(
        functools.partial(routed_back_attn_kernel, heads),
        out_shape=(
            shape((rows, d), F32), shape((rows, d), BF), shape((3,) + q.shape, BF),
            shape((2, d), F32), part, part,
        ),
        in_specs=[SM] + [VM] * 13,
        out_specs=(VM,) * 6,
        compiler_params=params(),
        cost_estimate=cost(8),
        name="routed_back_attn",
    )(info, own, other, d_sel, picked, attn, both_own, both_other, gains, q, k, v, qkv_w, mix_w)


def finish_kernel(
    info, own_ref, other_ref, d_mid_ref, picked_ref, gains_ref, sel_ref,
    d_rows_ref, far_ref, sent_ref, result_ref, out_ref,
):
    tensor, section, low = info[0], info[1], info[2]
    own = d_rows_ref.shape[0]
    pick = sel_ref.shape[1]

    @pl.when(section == 0)
    def _():
        d_normed = halves_in(own_ref, other_ref, low)
        unit, scale = unit_rows(picked_ref[...].astype(F32))
        d_picked = d_mid_ref[...] + norm_back(unit, scale, gains_ref[0:1, :], d_normed)
        d_picked = d_picked.astype(BF)
        for s in range(2):
            table = (sel_ref[s : s + 1, :] == subs(own, pick) + tensor * own).astype(F32).astype(BF)
            base = (d_rows_ref if s == 0 else far_ref)[...].astype(F32)
            out_ref[s] = base + dot(table, d_picked[s * pick : (s + 1) * pick])

    @pl.when(section != 0)
    def _():
        out_ref[0] = sent_ref[...].astype(F32)
        out_ref[1] = result_ref[...]


def finish(info, own, other, d_mid, picked, gains, sel_row, d_rows, far, sent, result):
    rows, d = d_rows.shape
    return pl.pallas_call(
        finish_kernel,
        out_shape=shape((2, rows, d), F32),
        in_specs=[SM] + [VM] * 10,
        out_specs=VM,
        compiler_params=params(),
        cost_estimate=cost(6),
        name="finish",
    )(info, own, other, d_mid, picked, gains, sel_row, d_rows, far, sent, result)


def pack_kernel(gains_ref, qkv_ref, mix_ref, out_ref):
    cols, d = mix_ref.shape
    for n in range(3):
        out_ref[n * cols : (n + 1) * cols, :] = qkv_ref[n]
    out_ref[3 * cols : 4 * cols, :] = mix_ref[...]
    rows = subs(16, d)
    extra = jnp.zeros((16, d), F32)
    for n in range(3):
        for p, piece in enumerate(three_pieces(gains_ref[n : n + 1, :])):
            extra = jnp.where(rows == 3 * n + p, piece.astype(F32), extra)
    out_ref[4 * cols :, :] = extra.astype(BF)


def pack_weights(gains, qkv_w, mix_w):
    cols, d = mix_w.shape
    return pl.pallas_call(
        pack_kernel,
        out_shape=shape((4 * cols + 16, d), BF),
        in_specs=[VM] * 3,
        out_specs=VM,
        compiler_params=params(),
        cost_estimate=cost(2),
        name="pack",
    )(gains, qkv_w, mix_w)


def prepare_kernel(info, g0, q0, m0, far_ref, gains_ref, qkv_ref, mix_ref):
    cols = m0.shape[0]
    own = info[1] == 1
    extra = far_ref[4 * cols :, :].astype(F32)
    for n in range(3):
        far = (extra[3 * n : 3 * n + 1] + extra[3 * n + 1 : 3 * n + 2]) + extra[3 * n + 2 : 3 * n + 3]
        gains_ref[n : n + 1, :] = jnp.where(own, g0[n : n + 1, :], far)
    qkv_ref[...] = jnp.zeros_like(qkv_ref)
    for n in range(3):
        qkv_ref[n, :cols, :] = jnp.where(own, q0[n], far_ref[n * cols : (n + 1) * cols, :])
    mix_ref[...] = jnp.zeros_like(mix_ref)
    mix_ref[:cols, :] = jnp.where(own, m0[...], far_ref[3 * cols : 4 * cols, :])


def prepare(info, gains, qkv_w, mix_w, far):
    d = mix_w.shape[1]
    return pl.pallas_call(
        prepare_kernel,
        out_shape=(shape(gains.shape, F32), shape((3, PAD, d), BF), shape((PAD, d), BF)),
        in_specs=[SM] + [VM] * 4,
        out_specs=(VM,) * 3,
        compiler_params=params(),
        cost_estimate=cost(2),
        name="prepare",
    )(info, gains, qkv_w, mix_w, far)


def project_kernel(
    heads, width, info, tok0, tok1, tok2a, tok2b, tok3a, tok3b, upd_own, upd_other, sel_ref,
    gains_ref, qkv_ref, rows_ref, normed_ref, q_ref, k_ref, v_ref, buf,
):
    tensor, low, length = info[0], info[2], info[3]
    r = pl.program_id(0)
    own, d = buf.shape
    for i, tok in enumerate((tok0, tok1)):
        @pl.when(r == i)
        def _():
            buf[...] = tok[...]

    for i, tok_a, tok_b in ((2, tok2a, tok2b), (3, tok3a, tok3b)):
        @pl.when(r == i)
        def _():
            buf[: own // 2] = tok_a[...]
            buf[own // 2 :] = tok_b[...]

    place = jnp.bitwise_xor(r, tensor) * own
    pick = sel_ref.shape[1]
    first, second = upd_own[...], upd_other[...]
    update = jnp.concatenate(
        [jnp.where(low == 0, first, second), jnp.where(low == 0, second, first)], 0
    )
    sel = jnp.where(info[1] == 0, sel_ref[0:1, :], sel_ref[1:2, :])
    table = (sel == subs(own, pick) + place).astype(F32).astype(BF)
    rows = (buf[...].astype(F32) + dot(table, update)).astype(BF)

    @pl.when(r == 0)
    def _():
        rows_ref[...] = rows

    unit, _ = unit_rows(rows.astype(F32))
    normed = (unit * gains_ref[0:1, :]).astype(BF)
    normed_ref[0] = normed
    lane = lanes(own, PAD)
    cols = heads * width
    one, zero = jnp.float32(1), jnp.float32(0)
    q = dot_nt(normed, qkv_ref[0]).astype(BF).astype(F32) * width ** (-0.5)
    q_ref[0] = jnp.where(lane == cols + 3, one, q).astype(BF)
    key_at = subs(own, PAD) + place
    extra = jnp.where(lane < cols + 3, one, jnp.where(key_at < length, zero, NEGATIVE))
    k = dot_nt(normed, qkv_ref[1])
    k_ref[0] = jnp.where((lane >= cols) & (lane < cols + 4), extra, k).astype(BF)
    v = dot_nt(normed, qkv_ref[2])
    v_ref[0] = jnp.where((lane >= cols) & (lane < cols + 3), one, v).astype(BF)


def project(info, toks, upd_own, upd_other, sel, gains, qkv_w, heads, width, count):
    own, d = toks[0].shape
    full = lambda dims: pl.BlockSpec(dims, lambda r, info: (0,) * len(dims))
    placed = lambda w: pl.BlockSpec((1, own, w), lambda r, info: (jnp.bitwise_xor(r, info[0]), 0, 0))
    padded = shape((count, own, PAD), BF)
    return pl.pallas_call(
        functools.partial(project_kernel, heads, width),
        out_shape=(shape((own, d), BF), shape((count, own, d), BF), padded, padded, padded),
        grid_spec=pltpu.PrefetchScalarGridSpec(
            num_scalar_prefetch=1,
            grid=(count,),
            in_specs=[full(tok.shape) for tok in toks]
            + [full(upd_own.shape)] * 2
            + [full(sel.shape), full(gains.shape), full(qkv_w.shape)],
            out_specs=(full((own, d)), placed(d), placed(PAD), placed(PAD), placed(PAD)),
            scratch_shapes=[pltpu.VMEM((own, d), BF)],
        ),
        compiler_params=params(grid=1),
        cost_estimate=cost(9),
        name="project",
    )(info, *toks, upd_own, upd_other, sel, gains, qkv_w)


def attention_kernel(
    heads, width, base, per, info, q_ref, k_ref, v_ref, mix_ref,
    send_ref, keep_ref, mixed_ref, lse_ref,
):
    i = pl.program_id(0)
    block = q_ref.shape[1]
    cols = heads * width
    steps = k_ref.shape[0] // block
    place = jnp.bitwise_xor(base + 1 - i // per, info[0]) * per + i % per

    def run(step):
        span = (step + 1) * block
        q = q_ref[0]
        lane = lanes(block, PAD)
        total = jnp.zeros((block, PAD), F32)
        lse = jnp.zeros((block, 128), F32)
        zero = jnp.zeros_like(q)
        for h in range(heads):
            here = (lane >= h * width) & (lane < (h + 1) * width)
            qh = jnp.where(here | (lane == cols + 3), q, zero)
            scores = dot_nt(qh, k_ref[0:span, :])
            causal = lanes(block, block) <= subs(block, block)
            tail = jnp.where(causal, scores[:, span - block :], NEGATIVE)
            high = jnp.max(tail, axis=-1, keepdims=True)
            if step:
                high = jnp.maximum(high, jnp.max(scores[:, : span - block], axis=-1, keepdims=True))
            probs = jnp.exp(tail - high).astype(BF)
            if step:
                probs = jnp.concatenate(
                    [jnp.exp(scores[:, : span - block] - high).astype(BF), probs], 1
                )
            out = dot(probs, v_ref[0:span, :])
            norm = jnp.sum(jnp.where(lane == cols, out, 0.0), axis=-1, keepdims=True)
            total = jnp.where(here, out / norm, total)
            lse = jnp.where(lanes(block, 128) == h, high + jnp.log(norm), lse)
        lse_ref[0] = lse
        mixed = total.astype(BF)
        mixed_ref[0] = mixed
        part = dot(mixed, mix_ref[...]).astype(BF)

        @pl.when(i < per)
        def _():
            send_ref[...] = part

        @pl.when(i >= per)
        def _():
            keep_ref[...] = part

    for step in range(steps):
        @pl.when(place == step)
        def _():
            run(step)


def attention(info, q, k, v, mix_w, heads, width, base, block=256):
    count, own, _ = q.shape
    total = count * own
    d = mix_w.shape[1]
    per = own // block
    k, v = k.reshape(total, PAD), v.reshape(total, PAD)
    full = lambda dims: pl.BlockSpec(dims, lambda i, info: (0,) * len(dims))
    rel = lambda w: pl.BlockSpec((1, block, w), lambda i, info: (1 - i // per, i % per, 0))
    out = shape((own, d), BF)
    return pl.pallas_call(
        functools.partial(attention_kernel, heads, width, base, per),
        out_shape=(out, out, shape((2, own, PAD), BF), shape((2, own, 128), F32)),
        grid_spec=pltpu.PrefetchScalarGridSpec(
            num_scalar_prefetch=1,
            grid=(2 * per,),
            in_specs=[
                pl.BlockSpec(
                    (1, block, PAD),
                    lambda i, info: (
                        jnp.bitwise_xor(base + 1 - i // per, info[0]), i % per, 0,
                    ),
                ),
                full(k.shape), full(v.shape), full(mix_w.shape),
            ],
            out_specs=(
                pl.BlockSpec((block, d), lambda i, info: (jnp.minimum(i, per - 1), 0)),
                pl.BlockSpec((block, d), lambda i, info: (jnp.maximum(i - per, 0), 0)),
                rel(PAD), rel(128),
            ),
        ),
        compiler_params=params(grid=1),
        cost_estimate=cost(0.3),
        name="attention",
    )(info, q, k, v, mix_w)


def mlp_kernel(
    half, rows_ref, keep_ref, near_ref, far_ref, cot_ref, gains_ref,
    p0a, p0b, p1a, p1b, p2a, p2b, p3a, p3b,
    result_ref, low_ref, d_mid_ref, d_mid_low_ref, keep_out, send_out,
    vec_ref, up_v, down_v, slope_v, act_v, pre_v, rows_v, result_v, low_v, sems, out_sems,
):
    leaving = []

    def leave(src, dst):
        copy = pltpu.make_async_copy(src, dst, out_sems.at[len(leaving)])
        copy.start()
        leaving.append(copy)

    parity = lax.axis_index("dp") & 1
    first = pl.ds(pl.multiple_of(parity * half, half), half)
    second = pl.ds(pl.multiple_of((1 - parity) * half, half), half)
    copies = {}
    count = 0
    for i in range(4):
        for n, (name, dest) in enumerate((("up", up_v), ("down", down_v))):
            a, b = ((p0a, p0b), (p1a, p1b), (p2a, p2b), (p3a, p3b))[i]
            moves = [(a.at[n], dest.at[i, first, :]), (b.at[n], dest.at[i, second, :])]
            some = []
            for src, dst in moves:
                copy = pltpu.make_async_copy(src, dst, sems.at[count])
                copy.start()
                some.append(copy)
                count += 1
            copies[name, i] = some
    attn = keep_ref[...].astype(F32) + near_ref[...].astype(F32) + far_ref[...].astype(F32)
    middle = rows_ref[...].astype(F32) + attn
    unit2, scale2 = unit_rows(middle)
    normed = (unit2 * gains_ref[1:2, :]).astype(BF)
    rows_v[0] = normed
    leave(rows_v.at[0], send_out.at[4])
    mlp = jnp.zeros_like(middle)
    for i in range(4):
        for copy in copies["up", i]:
            copy.wait()
        act, slope = gelu_pair(dot(normed, up_v[i]))
        act = act.astype(BF)
        act_v[i] = act
        leave(act_v.at[i], (keep_out if i % 2 == 0 else send_out).at[i // 2])
        slope_v[i] = slope
        for copy in copies["down", i]:
            copy.wait()
        mlp = mlp + dot(act, down_v[i])
    unit3, scale3 = unit_rows(middle + mlp)
    gain3 = gains_ref[2:3, :]
    result = unit3 * gain3
    result_v[...] = result
    leave(result_v, result_ref)
    low_v[...] = result.astype(BF)
    leave(low_v, low_ref)
    cot = cot_ref[0].astype(F32)
    vec_ref[1:2, :] = jnp.sum(cot * unit3, axis=0, keepdims=True)
    d_final = norm_back(unit3, scale3, gain3, cot)
    d_mlp = d_final.astype(BF)
    rows_v[1] = d_mlp
    leave(rows_v.at[1], send_out.at[5])
    d_normed = jnp.zeros_like(middle)
    for i in range(4):
        d_pre = (dot_nt(d_mlp, down_v[i]) * slope_v[i]).astype(BF)
        pre_v[i] = d_pre
        leave(pre_v.at[i], (keep_out if i % 2 == 0 else send_out).at[2 + i // 2])
        d_normed = d_normed + dot_nt(d_pre, up_v[i])
    vec_ref[0:1, :] = jnp.sum(d_normed * unit2, axis=0, keepdims=True)
    d_mid = d_final + norm_back(unit2, scale2, gains_ref[1:2, :], d_normed)
    d_mid_ref[...] = d_mid
    low = d_mid.astype(BF)
    d_mid_low_ref[...] = low
    rows_v[2] = low
    leave(rows_v.at[2], send_out.at[6])
    for copy in leaving:
        copy.wait()


def mlp_pass(rows, keep, near, far, cot, gains, pieces):
    own, d = rows.shape
    hidden = pieces[0].shape[2]
    half = d // 2
    wide, low = shape((own, d), F32), shape((own, d), BF)
    return pl.pallas_call(
        functools.partial(mlp_kernel, half),
        out_shape=(
            wide, low, wide, low, shape((4, own, d), BF), shape((7, own, d), BF), shape((2, d), F32)
        ),
        in_specs=[VM] * 6 + [HB] * 8,
        out_specs=(HB, HB, VM, VM, HB, HB, VM),
        scratch_shapes=[
            pltpu.VMEM((4, d, hidden), BF),
            pltpu.VMEM((4, hidden, d), BF),
            pltpu.VMEM((4, own, hidden), F32),
            pltpu.VMEM((4, own, hidden), BF),
            pltpu.VMEM((4, own, hidden), BF),
            pltpu.VMEM((3, own, d), BF),
            pltpu.VMEM((own, d), F32),
            pltpu.VMEM((own, d), BF),
            pltpu.SemaphoreType.DMA((16,)),
            pltpu.SemaphoreType.DMA((13,)),
        ],
        compiler_params=params(60),
        cost_estimate=cost(21),
        name="dense_mlp",
    )(rows, keep, near, far, cot, gains, *pieces)


FIRST = 8


def far_grads_kernel(
    act_ref, pre_ref, near_ref, own_ref, act2_ref, pre2_ref, near2_ref, rows2_ref,
    cross_ref, hop_ref, first_ref,
):
    i = pl.program_id(0)
    d = own_ref.shape[2]
    part = first_ref.shape[0]

    @pl.when(i == 0)
    def _():
        up = dot_tn(own_ref[0], pre_ref[0]) + dot_tn(rows2_ref[0], pre2_ref[0])
        cross_ref[:d] = up.astype(BF)

    @pl.when(i == 1)
    def _():
        rows, rows2 = own_ref[0], rows2_ref[0]
        down = (dot_tn(rows, act_ref[0]) + dot_tn(rows2, act2_ref[0])).astype(BF)
        cross_ref[d:] = down[:part]
        hop_ref[0] = down[part:]
        near = (dot_tn(rows, near_ref[0]) + dot_tn(rows2, near2_ref[0])).astype(BF)
        first_ref[...] = near[:part]
        hop_ref[1] = near[part:]


def near_grads_kernel(pre_ref, own_ref, pre2_ref, rows2_ref, first_ref, crossed_ref, out_ref):
    d = own_ref.shape[2]
    up = dot_tn(own_ref[0], pre_ref[0]) + dot_tn(rows2_ref[0], pre2_ref[0])
    out_ref[:d] = (up + crossed_ref[:d].astype(F32)).astype(BF)
    out_ref[d:] = (first_ref[...].astype(F32) + crossed_ref[d:].astype(F32)).astype(BF)


def far_grads(keep, send, other):
    _, own, d = keep.shape
    part = d // FIRST
    at = lambda n: pl.BlockSpec((1, own, d), lambda i: (n, 0, 0))
    pair = pl.BlockSpec((1, own, d), lambda i: (4 + i, 0, 0))
    return pl.pallas_call(
        far_grads_kernel,
        out_shape=(
            shape((d + part, d), BF), shape((2, d - part, d), BF), shape((part, d), BF)
        ),
        grid=(2,),
        in_specs=[at(1), at(3), at(0), pair, at(1), at(3), at(0), pair],
        out_specs=(
            pl.BlockSpec((d + part, d), lambda i: (0, 0)),
            pl.BlockSpec((2, d - part, d), lambda i: (0, 0, 0)),
            pl.BlockSpec((part, d), lambda i: (0, 0)),
        ),
        compiler_params=params(56, grid=1),
        cost_estimate=cost(5),
        name="far_grads",
    )(keep, keep, keep, send, other, other, other, other)


def near_grads(keep, send, other, first, crossed):
    _, own, d = keep.shape
    at = lambda n: pl.BlockSpec((1, own, d), lambda i: (n, 0, 0))
    full = lambda a: pl.BlockSpec(a.shape, lambda i: (0, 0))
    return pl.pallas_call(
        near_grads_kernel,
        out_shape=shape(crossed.shape, BF),
        grid=(1,),
        in_specs=[at(2), at(4), at(2), at(4), full(first), full(crossed)],
        out_specs=full(crossed),
        compiler_params=params(56, grid=1),
        cost_estimate=cost(5),
        name="near_grads",
    )(keep, send, other, other, first, crossed)


def attention_back_kernel(
    heads, width, block, info, g0, g1, g2, g3, q_ref, k_ref, v_ref, mixed_n, mixed_f, lse_n, lse_f,
    mix_ref, qkv_ref, sel_ref, d_qkv_ref, keep_ref, send_ref, mid_ref,
    qs, ds, dq_acc, dk_acc, dv_acc,
):
    tensor, low = info[0], info[2]
    own = g0.shape[0]
    cols = heads * width
    total = k_ref.shape[0]
    lane = lanes(own, PAD)
    zero = jnp.zeros((own, PAD), BF)
    grads = (g0[...], g1[0], g2[...], g3[...])
    for r, grad in enumerate(grads):
        at = pl.multiple_of(jnp.bitwise_xor(tensor, r) * own, own)
        span = pl.ds(at, own)
        d_mixed = dot_nt(grad, mix_ref[...]).astype(BF)
        inner = d_mixed.astype(F32) * (mixed_n if r < 2 else mixed_f)[r % 2].astype(F32)
        q = q_ref[span, :]
        lse = (lse_n if r < 2 else lse_f)[r % 2]
        for h in range(heads):
            here = (lane >= h * width) & (lane < (h + 1) * width)
            delta = -jnp.sum(jnp.where(here, inner, 0.0), axis=-1, keepdims=True)
            row_lse = -jnp.sum(jnp.where(lanes(own, 128) == h, lse, 0.0), axis=-1, keepdims=True)
            left = jnp.where(here | (lane == cols + 3), q, zero)
            right = jnp.where(here, d_mixed, zero)
            for p, (a, b) in enumerate(zip(three_pieces(row_lse), three_pieces(delta))):
                left = jnp.where(lane == cols + p, a, left)
                right = jnp.where(lane == cols + p, b, right)
            qs[h, span, :] = left
            ds[h, span, :] = right
    dq_acc[...] = jnp.zeros_like(dq_acc)
    lane_k = lanes(block, PAD)
    allowed = subs(block, block) <= lanes(block, block)
    for j in range(total // block):
        first = j * block
        k, v = k_ref[first : first + block, :], v_ref[first : first + block, :]
        dk = jnp.zeros((block, PAD), F32)
        dv = jnp.zeros((block, PAD), F32)
        stacked, keys = [], []
        for h in range(heads):
            qh, dh = qs[h, first:, :], ds[h, first:, :]
            scores = dot_nt(k, qh)
            d_probs = dot_nt(v, dh)
            head = jnp.where(allowed, scores[:, :block], NEGATIVE)
            probs = jnp.exp(head)
            if first + block < total:
                probs = jnp.concatenate([probs, jnp.exp(scores[:, block:])], 1)
            d_scores = (probs * d_probs).astype(BF)
            dv = dv + dot(probs.astype(BF), dh)
            dk = dk + dot(d_scores, qh)
            stacked.append(d_scores)
            keys.append(
                jnp.where((lane_k >= h * width) & (lane_k < (h + 1) * width), k, jnp.zeros_like(k))
            )
        dq_acc[first:, :] += dot_tn(jnp.concatenate(stacked, 0), jnp.concatenate(keys, 0))
        dk_acc[...] = dk
        dv_acc[...] = dv
        d_qkv_ref[1, first : first + block, :] = dk_acc[:, :cols].astype(BF)
        d_qkv_ref[2, first : first + block, :] = dv_acc[:, :cols].astype(BF)
    d_qkv_ref[0] = (dq_acc[:, :cols] * width ** (-0.5)).astype(BF)
    pick = sel_ref.shape[1]
    sel = jnp.where(info[1] == 0, sel_ref[0:1, :], sel_ref[1:2, :])
    table = (sel == subs(total, pick)).astype(F32).astype(BF)
    part = jnp.zeros((pick, qkv_ref.shape[2]), F32)
    for i in range(3):
        part = part + dot(dot_tn(table, d_qkv_ref[i]).astype(BF), qkv_ref[i][:cols, :])
    half = pick // 2
    keep_ref[...] = jnp.where(low == 0, part[:half], part[half:]).astype(BF)
    send_ref[...] = jnp.where(low == 0, part[half:], part[:half]).astype(BF)
    mine = jnp.where(low == 0, sel[:, :half], sel[:, half:])
    mid = jnp.zeros((half, qkv_ref.shape[2]), F32)
    for r, grad in enumerate(grads):
        table = (mine == subs(own, half) + jnp.bitwise_xor(tensor, r) * own).astype(F32).astype(BF)
        mid = mid + dot_tn(table, grad)
    mid_ref[...] = mid.astype(BF)


def attention_back(
    info, grads, q, k, v, mixed, lse, mix_w, qkv_w, selected, heads, width, block=256
):
    keep, other, far, far_other = grads
    own, d = keep.shape
    total = k.shape[0] * k.shape[1]
    flat = lambda a: a.reshape(total, PAD)
    half = shape((selected.shape[1] // 2, d), BF)
    at = lambda n: pl.BlockSpec((1, own, d), lambda i: (n, 0, 0))
    full = lambda a: pl.BlockSpec(a.shape, lambda i: (0,) * a.ndim)
    rest = (flat(q), flat(k), flat(v), *mixed, *lse, mix_w, qkv_w, selected)
    return pl.pallas_call(
        functools.partial(attention_back_kernel, heads, width, block),
        out_shape=(shape((3, total, heads * width), BF), half, half, half),
        grid=(1,),
        in_specs=[SM, full(keep), at(6), full(far), full(far_other)] + [full(a) for a in rest],
        out_specs=(
            pl.BlockSpec((3, total, heads * width), lambda i: (0, 0, 0)),
        ) + (pl.BlockSpec(half.shape, lambda i: (0, 0)),) * 3,
        scratch_shapes=[
            pltpu.VMEM((heads, total, PAD), BF),
            pltpu.VMEM((heads, total, PAD), BF),
            pltpu.VMEM((total, PAD), F32),
            pltpu.VMEM((block, PAD), F32),
            pltpu.VMEM((block, PAD), F32),
        ],
        compiler_params=params(60, grid=1),
        cost_estimate=cost(35),
        name="attention_back",
    )(info, keep, other, far, far_other, *rest)


def spread_back_kernel(cols, info, d_ref, qkv_ref, send_ref, keep_ref):
    i = pl.program_id(0)
    total = dot(d_ref[0, 0], qkv_ref[0][:cols, :])
    for n in (1, 2):
        total = total + dot(d_ref[n, 0], qkv_ref[n][:cols, :])
    total = total.astype(BF)

    @pl.when(i < 2)
    def _():
        send_ref[0] = total

    @pl.when(i >= 2)
    def _():
        keep_ref[0] = total


def spread_back(info, d_qkv, qkv_w, count):
    _, total, cols = d_qkv.shape
    own = total // count
    d = qkv_w.shape[2]
    pos = lambda i: jnp.where(i < 2, 3 - 2 * i, 6 - 2 * i)
    out = shape((2, own, d), BF)
    return pl.pallas_call(
        functools.partial(spread_back_kernel, cols),
        out_shape=(out, out),
        grid_spec=pltpu.PrefetchScalarGridSpec(
            num_scalar_prefetch=1,
            grid=(count,),
            in_specs=[
                pl.BlockSpec(
                    (3, 1, own, cols), lambda i, info: (0, jnp.bitwise_xor(pos(i), info[0]), 0, 0)
                ),
                pl.BlockSpec(qkv_w.shape, lambda i, info: (0, 0, 0)),
            ],
            out_specs=(
                pl.BlockSpec((1, own, d), lambda i, info: (1 - jnp.minimum(i, 1), 0, 0)),
                pl.BlockSpec((1, own, d), lambda i, info: (1 - jnp.maximum(i - 2, 0), 0, 0)),
            ),
        ),
        compiler_params=params(grid=1),
        cost_estimate=cost(5),
        name="spread_back",
    )(info, d_qkv.reshape(3, count, own, cols), qkv_w)


def attn_grads_kernel(
    cols, info, d_ref, normed_ref, g0, g1, g2, g3, mixed_n, mixed_f, pack_ref, acc,
):
    i = pl.program_id(0)

    @pl.when(i == 0)
    def _():
        acc[...] = jnp.zeros_like(acc)

    for n in range(3):
        acc[n * cols : (n + 1) * cols, :] += dot_tn(d_ref[n, 0], normed_ref[0])
    for r, grad in enumerate((g0, g1, g2, g3)):
        @pl.when(i == r)
        def _():
            mixed = (mixed_n if r < 2 else mixed_f)[r % 2]
            rows = grad[0] if r == 1 else grad[...]
            acc[3 * cols :, :] += dot_tn(mixed[:, :cols], rows)

    @pl.when(i == 3)
    def _():
        pack_ref[...] = jnp.transpose(acc[...]).astype(BF)


def attn_grads(info, d_qkv, normed, grads, mixed):
    _, total, cols = d_qkv.shape
    count, own, d = normed.shape
    full = lambda dims: pl.BlockSpec(dims, lambda i, info: (0,) * len(dims))
    return pl.pallas_call(
        functools.partial(attn_grads_kernel, cols),
        out_shape=shape((d, 4 * cols), BF),
        grid_spec=pltpu.PrefetchScalarGridSpec(
            num_scalar_prefetch=1,
            grid=(count,),
            in_specs=[
                pl.BlockSpec(
                    (3, 1, own, cols), lambda i, info: (0, jnp.bitwise_xor(i, info[0]), 0, 0)
                ),
                pl.BlockSpec((1, own, d), lambda i, info: (jnp.bitwise_xor(i, info[0]), 0, 0)),
            ]
            + [
                full((own, d)), pl.BlockSpec((1, own, d), lambda i, info: (6, 0, 0)),
                full((own, d)), full((own, d)),
            ]
            + [full(mixed[0].shape)] * 2,
            out_specs=full((d, 4 * cols)),
            scratch_shapes=[pltpu.VMEM((4 * cols, d), F32)],
        ),
        compiler_params=params(grid=1),
        cost_estimate=cost(8),
        name="attn_grads",
    )(info, d_qkv.reshape(3, count, own, cols), normed, *grads, *mixed)


def routed_mlp_grads_kernel(
    info, normed_ref, pre_ref, act_ref, grad_ref, part_ref, far_ref, last_ref, last_far, last_cross,
    pack_ref,
):
    hidden = pre_ref.shape[1]

    @pl.when(info[1] == 0)
    def _():
        pack_ref[:, :hidden] = dot_tn(normed_ref[...], pre_ref[...]).astype(BF)
        pack_ref[:, hidden:] = dot_tn(grad_ref[...], act_ref[...]).astype(BF)

    @pl.when(info[1] != 0)
    def _():
        d = normed_ref.shape[1]
        total = (part_ref[...].astype(F32) + far_ref[...].astype(F32)).astype(BF)
        part = part_ref.shape[0] - d
        pack_ref[:, :hidden] = total[:d]
        pack_ref[:part, hidden:] = total[d:]
        total = last_ref[1].astype(F32) + last_far[1].astype(F32) + last_cross[...].astype(F32)
        pack_ref[part:, hidden:] = total.astype(BF)


def routed_mlp_grads(info, normed, pre, act, grad, *dense):
    return pl.pallas_call(
        routed_mlp_grads_kernel,
        out_shape=shape((normed.shape[1], 2 * pre.shape[1]), BF),
        in_specs=[SM] + [VM] * 9,
        out_specs=VM,
        compiler_params=params(),
        cost_estimate=cost(5),
        name="routed_mlp_grads",
    )(info, normed, pre, act, grad, *dense)


def routed_attn_grads_kernel(
    info, normed_ref, d_ref, low_ref, mixed_ref, part_ref, hop_ref, pack_ref
):
    cols = mixed_ref.shape[1]

    @pl.when(info[1] == 0)
    def _():
        rows = [dot_tn(d_ref[n], normed_ref[...]) for n in range(3)]
        rows.append(dot_tn(mixed_ref[...], low_ref[...]))
        pack_ref[...] = jnp.transpose(jnp.concatenate(rows, 0)).astype(BF)

    @pl.when(info[1] != 0)
    def _():
        pack_ref[...] = (part_ref[...].astype(F32) + hop_ref[...].astype(F32)).astype(BF)


def routed_attn_grads(info, normed, d_qkv, d_low, mixed, part, far):
    return pl.pallas_call(
        routed_attn_grads_kernel,
        out_shape=shape((normed.shape[1], 4 * mixed.shape[1]), BF),
        in_specs=[SM] + [VM] * 6,
        out_specs=VM,
        compiler_params=params(),
        cost_estimate=cost(3),
        name="routed_attn_grads",
    )(info, normed, d_qkv, d_low, mixed, part, far)


def rows_back_kernel(keep_ref, near_ref, far_ref, rows_ref, d_mid_ref, gains_ref, d_rows_ref, vec_ref):
    d_normed = keep_ref[0].astype(F32) + near_ref[0].astype(F32) + far_ref[...].astype(F32)
    unit, scale = unit_rows(rows_ref[...].astype(F32))
    vec_ref[...] = jnp.sum(d_normed * unit, axis=0, keepdims=True)
    d_rows = d_mid_ref[...] + norm_back(unit, scale, gains_ref[0:1, :], d_normed)
    d_rows_ref[...] = d_rows.astype(BF)


def rows_back(keep, near, far, rows, d_mid, gains):
    own, d = rows.shape
    return pl.pallas_call(
        rows_back_kernel,
        out_shape=(shape((own, d), BF), shape((1, d), F32)),
        in_specs=[VM] * 6,
        out_specs=(VM, VM),
        compiler_params=params(),
        cost_estimate=cost(4),
        name="rows_back",
    )(keep, near, far, rows, d_mid, gains)


def sel_back_kernel(near_ref, far_ref, picked_ref, upd_ref, mid_ref, gains_ref, out_ref):
    d_normed = near_ref[...].astype(F32) + far_ref[...].astype(F32)
    rows = (picked_ref[...].astype(F32) + upd_ref[...].astype(F32)).astype(BF).astype(F32)
    unit, scale = unit_rows(rows)
    d_rows = mid_ref[...].astype(F32) + norm_back(unit, scale, gains_ref[0:1, :], d_normed)
    out_ref[...] = d_rows.astype(BF)


def sel_back(near, far, picked, upd, mid, gains):
    return pl.pallas_call(
        sel_back_kernel,
        out_shape=shape(near.shape, BF),
        in_specs=[VM] * 6,
        out_specs=VM,
        compiler_params=params(),
        cost_estimate=cost(2.3),
        name="sel_back",
    )(near, far, picked, upd, mid, gains)


def add(a, b):
    return (a.astype(F32) + b.astype(F32)).astype(BF)


def core_sum(keep, send):
    return add(keep, swap(send, "tensor", 1))


def whole_sum(keep, send):
    near = core_sum(keep, send)
    return add(near, swap(near, "tensor", 2))


def scatter_groups(pack):
    count, me = lax.axis_size("dp"), lax.axis_index("dp")
    if count != 4:
        return lax.psum_scatter(pack, "dp", scatter_dimension=0, tiled=True)
    for bit in (1, 2):
        rows = pack.shape[0] // 2
        side = (me // bit) % 2
        if bit == 1:
            quarters = pack.reshape(2, 2, rows // 2, pack.shape[1])
            take = lambda at: lax.dynamic_index_in_dim(quarters, at, 1, keepdims=False)
            keep, send = take(side), take(1 - side)
        else:
            keep = lax.dynamic_index_in_dim(pack, side, 0, keepdims=False)
            send = lax.dynamic_index_in_dim(pack, 1 - side, 0, keepdims=False)
        pack = add(keep, swap(send, "dp", bit))
    return pack


def body(
    tokens, qkv_weight, out_weight, up_weight, down_weight, vectors, lengths, selected, cotangent
):
    section = lax.axis_index("section")
    tensor = lax.axis_index("tensor")
    group = lax.axis_size("dp")
    heads = HEADS // lax.axis_size("tensor")
    low = tensor & 1
    is_dense = section == 1
    gains = vectors[0]
    qkv_w = jnp.swapaxes(qkv_weight[0], 1, 2)
    mix_w, up_w, down_w = out_weight[0], up_weight[0], down_weight[0]
    cols = qkv_w.shape[1]
    width = cols // heads
    d = mix_w.shape[1]

    barrier = lax.optimization_barrier
    core = lambda block: swap(block, "tensor", 1)
    cross = lambda block: swap(block, "tensor", 2)

    halves = up_w.shape[0] // 2
    parity = lax.axis_index("dp") & 1
    take = lambda w, at: lax.dynamic_slice_in_dim(w, at * halves, halves, 0)
    mine = (take(up_w, parity), take(down_w, parity))
    up_far = hop(mine[0], 1, 0)
    down_far = hop(after(mine[1], up_far), 1, 0)

    near = core_sum(*pick_rows(tokens, selected))
    far = cross(near)
    info = jnp.stack([tensor, section, low, lengths[section]]).astype(jnp.int32)
    my_tokens = lax.dynamic_index_in_dim(tokens, section, 0, keepdims=False)
    part = my_tokens.shape[0] // 2
    tok_a, tok_b = my_tokens[:part], my_tokens[part:]
    far, my_tokens, info, tok_a, tok_b = barrier((far, my_tokens, info, tok_a, tok_b))
    tok2a = cross(after(tok_a, far))
    packed = pack_weights(gains, qkv_w, mix_w)
    picked_half = add(near, far)
    picked_other = core(picked_half)

    picked, normed, q, k, v, mixed, keep, send = routed_attn(
        info, picked_half, picked_other, gains, qkv_w, mix_w, heads
    )
    send, tok2a, up_far = barrier((send, tok2a, up_far))
    near = core_sum(keep, send)
    far = cross(near)
    far, packed, down_far = barrier((far, packed, down_far))
    attn_half = add(near, far)
    tok2b = cross(after(tok_b, far))
    tok1 = core(my_tokens)
    attn_other = core(attn_half)
    packed_far = hop(after(packed, down_far), 1, 0)
    attn, normed2, act, slope, keep, send = routed_mlp(
        info, picked, attn_half, attn_other, gains, up_w, down_w
    )
    piece0a = jnp.stack(
        [jnp.where(is_dense, own, far) for own, far in zip(mine, (up_far, down_far))]
    )
    send, tok2b = barrier((send, tok2b))
    near = core_sum(keep, send)
    far = cross(near)
    far, piece0a = barrier((far, piece0a))
    both_half, update_half = make_update(picked_half, attn_half, near, far, gains)
    piece2a = cross(after(piece0a, far))
    piece1a = core(piece0a)
    tok3a, tok3b = core(tok2a), core(tok2b)
    arrived = hop(update_half[1], 0, 1)
    my_update = jnp.where(is_dense, arrived, update_half[0])
    my_update, piece1a, packed_far = barrier((my_update, piece1a, packed_far))
    d_gains, d_qkv_w, d_mix_w = prepare(info, gains, qkv_w, mix_w, packed_far)
    my_update_other = core(my_update)
    my_update_other, d_gains = barrier((my_update_other, d_gains))
    toks = (my_tokens, tok1, tok2a, tok2b, tok3a, tok3b)

    piece0b = swap(piece0a, "dp", 1)
    piece2a, piece0b = barrier((after(piece2a, my_update_other), piece0b))
    piece2b = swap(piece2a, "dp", 1)

    rows, d_normed_rows, dq_in, dk_in, dv_in = project(
        info, toks, my_update, my_update_other, selected, d_gains, d_qkv_w, heads, width,
        lax.axis_size("tensor"),
    )
    send, keep, mixed_f, lse_f = attention(info, dq_in, dk_in, dv_in, d_mix_w, heads, width, 2)
    send, piece2b = barrier((send, piece2b))
    near = core_sum(keep, send)
    far = cross(near)
    send, keep, mixed_n, lse_n = attention(info, dq_in, dk_in, dv_in, d_mix_w, heads, width, 0)
    piece3a = core(after(piece2a, send))
    piece3b = core(after(piece2b, send))
    piece1b = core(after(piece0b, send))
    send, far = barrier((send, far))
    near = core(send)
    my_cot = lax.dynamic_slice_in_dim(cotangent, section, 1, 0)
    result, result_low, d_mid, d_mid_low, mlp_keep, mlp_send, m_vec = mlp_pass(
        rows, keep, near, far, my_cot, d_gains,
        (piece0a, piece0b, piece1a, piece1b, piece2a, piece2b, piece3a, piece3b),
    )
    grad_f = cross(d_mid_low)
    mlp_other = core(mlp_send)
    mlp_f, last, first = far_grads(mlp_keep, mlp_send, mlp_other)
    grad_f, mlp_f, last = barrier((grad_f, mlp_f, last))
    grads = (d_mid_low, mlp_other, grad_f, core(grad_f))
    mlp_f2 = cross(mlp_f)
    last_h = hop(last, 0, 1)

    d_qkv, keep, send, mid_sel = attention_back(
        info, grads, dq_in, dk_in, dv_in, (mixed_n, mixed_f), (lse_n, lse_f),
        d_mix_w, d_qkv_w, selected, heads, width,
    )
    near = core_sum(keep, send)
    far = cross(near)
    mlp_part = near_grads(mlp_keep, mlp_send, after(mlp_other, near), first, mlp_f2)
    last_f = add(last[0], after(last_h[0], mlp_part))
    far, mlp_part, last_f = barrier((far, mlp_part, last_f))
    last_f2 = cross(last_f)
    mlp_hop = hop(mlp_part, 0, 1)
    my_picked = lax.dynamic_index_in_dim(picked_half, section, 0, keepdims=False)
    my_d_sel = sel_back(near, far, my_picked, my_update, mid_sel, d_gains)
    back = hop(my_d_sel, 1, 0)
    attn_part = attn_grads(
        info, after(d_qkv, my_d_sel), d_normed_rows, grads, (mixed_n, mixed_f)
    )
    back, attn_part, last_f2 = barrier((back, attn_part, last_f2))
    sel_other = core(jnp.concatenate([my_d_sel[None], back[None], both_half], 0))

    d_sel, r_d_mlp, r_d_pre, gain_two, keep2, send2 = routed_back_mlp(
        info, my_d_sel, back, sel_other, picked, attn, gains, slope, up_w, down_w
    )
    send2, mlp_hop = barrier((send2, mlp_hop))
    near = core_sum(keep2, send2)
    far = cross(near)
    r_mlp = routed_mlp_grads(
        info, normed2, r_d_pre, act, r_d_mlp, mlp_part, mlp_hop, last, last_h, last_f2
    )
    row_send, row_keep = spread_back(info, after(d_qkv, r_mlp), d_qkv_w, 4)
    far, row_send = barrier((far, row_send))
    row_core = core(row_send)
    half = add(near, far)
    other = core(half)
    row_far = cross(add(row_keep[1], row_core[1]))
    attn_hop = hop(attn_part, 0, 1)
    hidden = up_w.shape[1]
    r_d_mid, r_d_low, r_d_qkv, r_vec, keep2, send2 = routed_back_attn(
        info, half, other, d_sel, picked, attn, both_half, sel_other, gains, q, k, v,
        qkv_w, mix_w, heads,
    )
    near = core_sum(keep2, send2)
    near, row_far, attn_hop = barrier((near, row_far, attn_hop))
    far = cross(near)
    r_attn = routed_attn_grads(
        info, normed, r_d_qkv, r_d_low, mixed, after(attn_part, near), attn_hop
    )
    mlp_sum = lax.psum_scatter(r_mlp, "dp", scatter_dimension=0, tiled=True)
    d_mid = after(d_mid, r_attn)
    d_rows, row_vec = rows_back(row_keep, row_core, row_far, rows, d_mid, d_gains)
    d_rows_far = hop(d_rows, 1, 0)
    far, d_rows = barrier((far, d_rows))
    sent_result = hop(after(result_low, attn_hop), 0, 1)
    half = add(near, far)
    other = core(half)
    attn_sum = scatter_groups(r_attn)

    combined = finish(
        info, half, other, r_d_mid, picked, gains, selected, d_rows, d_rows_far, sent_result, result
    )
    share = d // group
    up_grad = mlp_sum[:, :hidden].astype(F32)
    down_grad = jnp.swapaxes(mlp_sum[:, hidden:], 0, 1).astype(F32)
    qkv_grad = jnp.swapaxes(attn_sum[:, : 3 * cols].reshape(share, 3, cols), 0, 1).astype(F32)
    mix_grad = jnp.swapaxes(attn_sum[:, 3 * cols : 4 * cols], 0, 1).astype(F32)

    vecs = jnp.concatenate([r_vec[0:1], gain_two, r_vec[1:2], row_vec, m_vec], 0)
    for axis in ("tensor", "dp"):
        bit = 1
        while bit < lax.axis_size(axis):
            vecs = vecs + swap(vecs, axis, bit)
            bit *= 2
    vecs = lax.dynamic_slice_in_dim(vecs, lax.axis_index("dp") * share, share, 1)
    dense_vec = vecs[3:6] + hop(vecs[3:6], 0, 1)
    vecs = jnp.where(is_dense, dense_vec, vecs[:3])
    return (
        combined[None],
        qkv_grad[None],
        mix_grad[None],
        up_grad[None],
        down_grad[None],
        vecs[None],
    )


def solution(mesh):
    placed = (
        P("dp", "tensor", None),
        P("section", None, None, "tensor"),
        P("section", "tensor", None),
        P("section", None, "tensor"),
        P("section", "tensor", None),
        P("section", None, None),
        P("dp"),
        P("dp", None),
        P("dp", "tensor", None),
    )
    return jax.shard_map(
        body,
        mesh=mesh,
        in_specs=placed,
        out_specs=(
            P("section", "dp", "tensor", None),
            P("section", None, "dp", "tensor"),
            P("section", "tensor", "dp"),
            P("section", "dp", "tensor"),
            P("section", "tensor", "dp"),
            P("section", None, "dp"),
        ),
        check_vma=False,
    )
```

```python
import functools

import jax
import jax.numpy as jnp
from jax import lax
from jax.experimental import pallas as pl
from jax.experimental.pallas import tpu as pltpu
from jax.sharding import PartitionSpec as P

HEADS = 12
EPSILON = 1e-06
NEGATIVE = -1e30
BF = jnp.bfloat16
F32 = jnp.float32
PAD = 256
MIB = 1 << 20


def swap(block, axis, bit):
    count = lax.axis_size(axis)
    return lax.ppermute(block, axis, [(i, i ^ bit) for i in range(count)])


def hop(block, source, target):
    return lax.ppermute(block, "section", [(source, target)])


def dot(left, right):
    return lax.dot_general(left, right, (((1,), (0,)), ((), ())), preferred_element_type=F32)


def dot_nt(left, right):
    return lax.dot_general(left, right, (((1,), (1,)), ((), ())), preferred_element_type=F32)


def dot_tn(left, right):
    return lax.dot_general(left, right, (((0,), (0,)), ((), ())), preferred_element_type=F32)


def unit_rows(values):
    scale = lax.rsqrt(jnp.mean(values * values, axis=-1, keepdims=True) + EPSILON)
    return values * scale, scale


def norm_back(unit, scale, gain, grad):
    e = grad * gain
    return scale * (e - unit * jnp.mean(e * unit, axis=-1, keepdims=True))


def gelu_pair(x):
    c = 0.7978845608028654
    a = 0.044715
    xx = x * x
    th = jnp.tanh(c * (x + a * (x * xx)))
    half = 0.5 * (1.0 + th)
    slope = half + (0.5 * x) * (1.0 - th * th) * (c * (1.0 + (3.0 * a) * xx))
    return x * half, slope


def lanes(rows, width):
    return lax.broadcasted_iota(jnp.int32, (rows, width), 1)


def subs(rows, width):
    return lax.broadcasted_iota(jnp.int32, (rows, width), 0)


def head_of(values, lane, head, width):
    zero = jnp.zeros_like(values)
    return jnp.where((lane >= head * width) & (lane < (head + 1) * width), values, zero)


def three_pieces(column):
    first = column.astype(BF)
    rest = column - first.astype(F32)
    second = rest.astype(BF)
    third = (rest - second.astype(F32)).astype(BF)
    return first, second, third


def params(limit=56, grid=None):
    if grid is None:
        return pltpu.CompilerParams(vmem_limit_bytes=limit * MIB)
    return pltpu.CompilerParams(
        vmem_limit_bytes=limit * MIB, dimension_semantics=("arbitrary",) * grid
    )


def cost(us):
    return pl.CostEstimate(
        flops=int(us * 1e8), bytes_accessed=int(us * 3.3e6), transcendentals=0
    )


def after(value, *others):
    return lax.optimization_barrier((value,) + others)[0]


VM = pl.BlockSpec(memory_space=pltpu.VMEM)
SM = pl.BlockSpec(memory_space=pltpu.SMEM)
HB = pl.BlockSpec(memory_space=pl.ANY)


def shape(dims, dtype):
    return jax.ShapeDtypeStruct(dims, dtype)


def halves_out(partial, low, keep_ref, send_ref):
    pick = partial.shape[0] // 2
    half = pick // 2
    for s in range(2):
        first = partial[s * pick : s * pick + half]
        second = partial[s * pick + half : (s + 1) * pick]
        keep_ref[s] = jnp.where(low == 0, first, second).astype(BF)
        send_ref[s] = jnp.where(low == 0, second, first).astype(BF)


def halves_in(own_ref, other_ref, low):
    parts = []
    for s in range(2):
        own, other = own_ref[s].astype(F32), other_ref[s].astype(F32)
        parts.append(jnp.where(low == 0, own, other))
        parts.append(jnp.where(low == 0, other, own))
    return jnp.concatenate(parts, 0)


def pick_kernel(rows_ref, sel_ref, keep_ref, send_ref):
    tensor = lax.axis_index("tensor")
    own = rows_ref.shape[1]
    pick = sel_ref.shape[1]
    parts = []
    for s in range(2):
        table = (sel_ref[s : s + 1, :] == subs(own, pick) + tensor * own).astype(F32).astype(BF)
        parts.append(dot_tn(table, rows_ref[s]))
    halves_out(jnp.concatenate(parts, 0), tensor & 1, keep_ref, send_ref)


def pick_rows(rows, selected):
    _, _, d = rows.shape
    out = shape((2, selected.shape[1] // 2, d), BF)
    return pl.pallas_call(
        pick_kernel,
        out_shape=(out, out),
        in_specs=[VM, VM],
        out_specs=(VM, VM),
        compiler_params=params(),
        cost_estimate=cost(3),
        name="pick",
    )(rows, selected)


def routed_attn_kernel(
    heads, info, own_ref, other_ref, gains_ref, qkv_ref, mix_ref,
    picked_ref, normed_ref, q_ref, k_ref, v_ref, mixed_ref, keep_ref, send_ref,
):
    low = info[2]
    picked = halves_in(own_ref, other_ref, low)
    picked_ref[...] = picked.astype(BF)
    unit, _ = unit_rows(picked)
    normed = (unit * gains_ref[0:1, :]).astype(BF)
    normed_ref[...] = normed
    width = qkv_ref.shape[1] // heads
    q = dot_nt(normed, qkv_ref[0]).astype(BF)
    k = dot_nt(normed, qkv_ref[1]).astype(BF)
    v = dot_nt(normed, qkv_ref[2]).astype(BF)
    q = (q.astype(F32) * width ** (-0.5)).astype(BF)
    q_ref[...] = q
    k_ref[...] = k
    v_ref[...] = v
    pick = picked.shape[0] // 2
    lane = lanes(pick, heads * width)
    allowed = lanes(pick, pick) <= subs(pick, pick)
    parts = []
    for s in range(2):
        span = slice(s * pick, (s + 1) * pick)
        total = jnp.zeros((pick, heads * width), F32)
        for h in range(heads):
            scores = dot_nt(head_of(q[span], lane, h, width), k[span])
            scores = jnp.where(allowed, scores, NEGATIVE)
            expos = jnp.exp(scores - jnp.max(scores, axis=-1, keepdims=True))
            probs = expos / jnp.sum(expos, axis=-1, keepdims=True)
            total = total + dot(probs.astype(BF), head_of(v[span], lane, h, width))
        parts.append(total.astype(BF))
    mixed = jnp.concatenate(parts, 0)
    mixed_ref[...] = mixed
    halves_out(dot(mixed, mix_ref[...]), low, keep_ref, send_ref)


def routed_attn(info, own, other, gains, qkv_w, mix_w, heads):
    _, half, d = own.shape
    rows = 4 * half
    cols = qkv_w.shape[1]
    part = shape((2, half, d), BF)
    wide, narrow = shape((rows, d), BF), shape((rows, cols), BF)
    return pl.pallas_call(
        functools.partial(routed_attn_kernel, heads),
        out_shape=(wide, wide, narrow, narrow, narrow, narrow, part, part),
        in_specs=[SM] + [VM] * 5,
        out_specs=(VM,) * 8,
        compiler_params=params(),
        cost_estimate=cost(5),
        name="routed_attn",
    )(info, own, other, gains, qkv_w, mix_w)


def routed_mlp_kernel(
    info, picked_ref, own_ref, other_ref, gains_ref, up_ref, down_ref,
    attn_ref, normed_ref, act_ref, slope_ref, keep_ref, send_ref,
):
    low = info[2]
    attn = halves_in(own_ref, other_ref, low)
    attn_ref[...] = attn.astype(BF)
    unit, _ = unit_rows(picked_ref[...].astype(F32) + attn)
    normed = (unit * gains_ref[1:2, :]).astype(BF)
    normed_ref[...] = normed
    act, slope = gelu_pair(dot(normed, up_ref[...]))
    act = act.astype(BF)
    act_ref[...] = act
    slope_ref[...] = slope
    halves_out(dot(act, down_ref[...]), low, keep_ref, send_ref)


def routed_mlp(info, picked, own, other, gains, up_w, down_w):
    rows, d = picked.shape
    hidden = up_w.shape[1]
    part = shape((2, rows // 4, d), BF)
    return pl.pallas_call(
        routed_mlp_kernel,
        out_shape=(
            shape((rows, d), BF), shape((rows, d), BF), shape((rows, hidden), BF),
            shape((rows, hidden), F32), part, part,
        ),
        in_specs=[SM] + [VM] * 6,
        out_specs=(VM,) * 6,
        compiler_params=params(),
        cost_estimate=cost(6),
        name="routed_mlp",
    )(info, picked, own, other, gains, up_w, down_w)


def update_kernel(picked_ref, attn_ref, mlp_ref, mlp2_ref, gains_ref, both_ref, update_ref):
    d = picked_ref.shape[2]
    weight = gains_ref[2:3, :] * d ** (-0.5)
    for s in range(2):
        router = jnp.sum(picked_ref[s].astype(F32) * weight, axis=-1, keepdims=True)
        both = attn_ref[s].astype(F32) + (mlp_ref[s].astype(F32) + mlp2_ref[s].astype(F32))
        both_ref[s] = both.astype(BF)
        update_ref[s] = (router * both).astype(BF)


def make_update(picked_half, attn_half, mlp_half, mlp_far, gains):
    out = shape(picked_half.shape, BF)
    return pl.pallas_call(
        update_kernel,
        out_shape=(out, out),
        in_specs=[VM] * 5,
        out_specs=(VM, VM),
        compiler_params=params(),
        cost_estimate=cost(2.5),
        name="update",
    )(picked_half, attn_half, mlp_half, mlp_far, gains)


def routed_back_mlp_kernel(
    info, sel_own, sel_back, sel_other, picked_ref, attn_ref, gains_ref, slope_ref, up_ref, down_ref,
    d_sel_ref, d_mlp_ref, d_pre_ref, gain_ref, keep_ref, send_ref,
):
    low = info[2]
    d = picked_ref.shape[1]
    parts = []
    for s, own in enumerate((sel_own[...], sel_back[...])):
        other = sel_other[s]
        parts += [jnp.where(low == 0, own, other), jnp.where(low == 0, other, own)]
    d_sel = jnp.concatenate(parts, 0).astype(F32)
    d_sel_ref[...] = d_sel
    picked = picked_ref[...].astype(F32)
    router = jnp.sum(picked * (gains_ref[2:3, :] * d ** (-0.5)), axis=-1, keepdims=True)
    d_mlp = (router * d_sel).astype(BF)
    d_mlp_ref[...] = d_mlp
    d_pre = (dot_nt(d_mlp, down_ref[...]) * slope_ref[...]).astype(BF)
    d_pre_ref[...] = d_pre
    d_normed = dot_nt(d_pre, up_ref[...])
    unit, _ = unit_rows(picked + attn_ref[...].astype(F32))
    gain_ref[...] = jnp.sum(d_normed * unit, axis=0, keepdims=True)
    halves_out(d_normed, low, keep_ref, send_ref)


def routed_back_mlp(info, sel_own, sel_back, sel_other, picked, attn, gains, slope, up_w, down_w):
    rows, d = picked.shape
    hidden = up_w.shape[1]
    part = shape((2, rows // 4, d), BF)
    return pl.pallas_call(
        routed_back_mlp_kernel,
        out_shape=(
            shape((rows, d), F32), shape((rows, d), BF), shape((rows, hidden), BF),
            shape((1, d), F32), part, part,
        ),
        in_specs=[SM] + [VM] * 9,
        out_specs=(VM,) * 6,
        compiler_params=params(),
        cost_estimate=cost(6),
        name="routed_back_mlp",
    )(info, sel_own, sel_back, sel_other, picked, attn, gains, slope, up_w, down_w)


def routed_back_attn_kernel(
    heads, info, own_ref, other_ref, d_sel_ref, picked_ref, attn_ref, both_own, both_other,
    gains_ref, q_ref, k_ref, v_ref, qkv_ref, mix_ref,
    d_mid_ref, d_low_ref, d_qkv_ref, vec_ref, keep_ref, send_ref,
):
    low = info[2]
    rows, d = picked_ref.shape
    d_normed2 = halves_in(own_ref, other_ref, low)
    picked = picked_ref[...].astype(F32)
    d_sel = d_sel_ref[...]
    router_row = gains_ref[2:3, :] * d ** (-0.5)
    router = jnp.sum(picked * router_row, axis=-1, keepdims=True)
    unit2, scale2 = unit_rows(picked + attn_ref[...].astype(F32))
    d_mid = norm_back(unit2, scale2, gains_ref[1:2, :], d_normed2)
    both = halves_in(both_own, both_other.at[2:], low)
    d_router = jnp.sum(d_sel * both, axis=-1, keepdims=True)
    d_mid_ref[...] = d_mid + d_router * router_row
    d_weight = jnp.sum(picked * d_router, axis=0, keepdims=True) * d ** (-0.5)
    vec_ref[1:2, :] = jnp.where(info[0] == 0, d_weight, jnp.zeros_like(d_weight))
    d_low = (router * d_sel + d_mid).astype(BF)
    d_low_ref[...] = d_low
    d_mixed = dot_nt(d_low, mix_ref[...]).astype(BF)
    width = qkv_ref.shape[1] // heads
    pick = rows // 2
    lane = lanes(pick, heads * width)
    allowed = subs(pick, pick) <= lanes(pick, pick)
    dq_parts, dk_parts, dv_parts = [], [], []
    for s in range(2):
        span = slice(s * pick, (s + 1) * pick)
        q, k, v, dm = q_ref[span, :], k_ref[span, :], v_ref[span, :], d_mixed[span]
        dq = jnp.zeros((pick, heads * width), F32)
        dk, dv = dq, dq
        for h in range(heads):
            qh, kh = head_of(q, lane, h, width), head_of(k, lane, h, width)
            dh = head_of(dm, lane, h, width)
            scores = jnp.where(allowed, dot_nt(k, qh), NEGATIVE)
            expos = jnp.exp(scores - jnp.max(scores, axis=0, keepdims=True))
            probs = expos / jnp.sum(expos, axis=0, keepdims=True)
            d_probs = dot_nt(v, dh)
            inner = jnp.sum(probs * d_probs, axis=0, keepdims=True)
            d_scores = (probs * (d_probs - inner)).astype(BF)
            dv = dv + dot(probs.astype(BF), dh)
            dk = dk + dot(d_scores, qh)
            dq = dq + dot_tn(d_scores, kh)
        dq_parts.append(dq * width ** (-0.5))
        dk_parts.append(dk)
        dv_parts.append(dv)
    d_normed = jnp.zeros((rows, d), F32)
    for i, parts in enumerate((dq_parts, dk_parts, dv_parts)):
        whole = jnp.concatenate(parts, 0).astype(BF)
        d_qkv_ref[i] = whole
        d_normed = d_normed + dot(whole, qkv_ref[i])
    unit, _ = unit_rows(picked)
    vec_ref[0:1, :] = jnp.sum(d_normed * unit, axis=0, keepdims=True)
    halves_out(d_normed, low, keep_ref, send_ref)


def routed_back_attn(
    info, own, other, d_sel, picked, attn, both_own, both_other, gains, q, k, v, qkv_w, mix_w, heads
):
    rows, d = picked.shape
    part = shape((2, rows // 4, d), BF)
    return pl.pallas_call(
        functools.partial(routed_back_attn_kernel, heads),
        out_shape=(
            shape((rows, d), F32), shape((rows, d), BF), shape((3,) + q.shape, BF),
            shape((2, d), F32), part, part,
        ),
        in_specs=[SM] + [VM] * 13,
        out_specs=(VM,) * 6,
        compiler_params=params(),
        cost_estimate=cost(8),
        name="routed_back_attn",
    )(info, own, other, d_sel, picked, attn, both_own, both_other, gains, q, k, v, qkv_w, mix_w)


def finish_kernel(
    info, own_ref, other_ref, d_mid_ref, picked_ref, gains_ref, sel_ref,
    d_rows_ref, far_ref, sent_ref, result_ref, out_ref,
):
    tensor, section, low = info[0], info[1], info[2]
    own = d_rows_ref.shape[0]
    pick = sel_ref.shape[1]

    @pl.when(section == 0)
    def _():
        d_normed = halves_in(own_ref, other_ref, low)
        unit, scale = unit_rows(picked_ref[...].astype(F32))
        d_picked = d_mid_ref[...] + norm_back(unit, scale, gains_ref[0:1, :], d_normed)
        d_picked = d_picked.astype(BF)
        for s in range(2):
            table = (sel_ref[s : s + 1, :] == subs(own, pick) + tensor * own).astype(F32).astype(BF)
            base = (d_rows_ref if s == 0 else far_ref)[...].astype(F32)
            out_ref[s] = base + dot(table, d_picked[s * pick : (s + 1) * pick])

    @pl.when(section != 0)
    def _():
        out_ref[0] = sent_ref[...].astype(F32)
        out_ref[1] = result_ref[...]


def finish(info, own, other, d_mid, picked, gains, sel_row, d_rows, far, sent, result):
    rows, d = d_rows.shape
    return pl.pallas_call(
        finish_kernel,
        out_shape=shape((2, rows, d), F32),
        in_specs=[SM] + [VM] * 10,
        out_specs=VM,
        compiler_params=params(),
        cost_estimate=cost(6),
        name="finish",
    )(info, own, other, d_mid, picked, gains, sel_row, d_rows, far, sent, result)


def pack_kernel(gains_ref, qkv_ref, mix_ref, out_ref):
    cols, d = mix_ref.shape
    for n in range(3):
        out_ref[n * cols : (n + 1) * cols, :] = qkv_ref[n]
    out_ref[3 * cols : 4 * cols, :] = mix_ref[...]
    rows = subs(16, d)
    extra = jnp.zeros((16, d), F32)
    for n in range(3):
        for p, piece in enumerate(three_pieces(gains_ref[n : n + 1, :])):
            extra = jnp.where(rows == 3 * n + p, piece.astype(F32), extra)
    out_ref[4 * cols :, :] = extra.astype(BF)


def pack_weights(gains, qkv_w, mix_w):
    cols, d = mix_w.shape
    return pl.pallas_call(
        pack_kernel,
        out_shape=shape((4 * cols + 16, d), BF),
        in_specs=[VM] * 3,
        out_specs=VM,
        compiler_params=params(),
        cost_estimate=cost(2),
        name="pack",
    )(gains, qkv_w, mix_w)


def prepare_kernel(info, g0, q0, m0, far_ref, gains_ref, qkv_ref, mix_ref):
    cols = m0.shape[0]
    own = info[1] == 1
    extra = far_ref[4 * cols :, :].astype(F32)
    for n in range(3):
        far = (extra[3 * n : 3 * n + 1] + extra[3 * n + 1 : 3 * n + 2]) + extra[3 * n + 2 : 3 * n + 3]
        gains_ref[n : n + 1, :] = jnp.where(own, g0[n : n + 1, :], far)
    qkv_ref[...] = jnp.zeros_like(qkv_ref)
    for n in range(3):
        qkv_ref[n, :cols, :] = jnp.where(own, q0[n], far_ref[n * cols : (n + 1) * cols, :])
    mix_ref[...] = jnp.zeros_like(mix_ref)
    mix_ref[:cols, :] = jnp.where(own, m0[...], far_ref[3 * cols : 4 * cols, :])


def prepare(info, gains, qkv_w, mix_w, far):
    d = mix_w.shape[1]
    return pl.pallas_call(
        prepare_kernel,
        out_shape=(shape(gains.shape, F32), shape((3, PAD, d), BF), shape((PAD, d), BF)),
        in_specs=[SM] + [VM] * 4,
        out_specs=(VM,) * 3,
        compiler_params=params(),
        cost_estimate=cost(2),
        name="prepare",
    )(info, gains, qkv_w, mix_w, far)


def project_kernel(
    heads, width, info, tok0, tok1, tok2a, tok2b, tok3a, tok3b, upd_own, upd_other, sel_ref,
    gains_ref, qkv_ref, rows_ref, normed_ref, q_ref, k_ref, v_ref, buf,
):
    tensor, low, length = info[0], info[2], info[3]
    r = pl.program_id(0)
    own, d = buf.shape
    for i, tok in enumerate((tok0, tok1)):
        @pl.when(r == i)
        def _():
            buf[...] = tok[...]

    for i, tok_a, tok_b in ((2, tok2a, tok2b), (3, tok3a, tok3b)):
        @pl.when(r == i)
        def _():
            buf[: own // 2] = tok_a[...]
            buf[own // 2 :] = tok_b[...]

    place = jnp.bitwise_xor(r, tensor) * own
    pick = sel_ref.shape[1]
    first, second = upd_own[...], upd_other[...]
    update = jnp.concatenate(
        [jnp.where(low == 0, first, second), jnp.where(low == 0, second, first)], 0
    )
    sel = jnp.where(info[1] == 0, sel_ref[0:1, :], sel_ref[1:2, :])
    table = (sel == subs(own, pick) + place).astype(F32).astype(BF)
    rows = (buf[...].astype(F32) + dot(table, update)).astype(BF)

    @pl.when(r == 0)
    def _():
        rows_ref[...] = rows

    unit, _ = unit_rows(rows.astype(F32))
    normed = (unit * gains_ref[0:1, :]).astype(BF)
    normed_ref[0] = normed
    lane = lanes(own, PAD)
    cols = heads * width
    one, zero = jnp.float32(1), jnp.float32(0)
    q = dot_nt(normed, qkv_ref[0]).astype(BF).astype(F32) * width ** (-0.5)
    q_ref[0] = jnp.where(lane == cols + 3, one, q).astype(BF)
    key_at = subs(own, PAD) + place
    extra = jnp.where(lane < cols + 3, one, jnp.where(key_at < length, zero, NEGATIVE))
    k = dot_nt(normed, qkv_ref[1])
    k_ref[0] = jnp.where((lane >= cols) & (lane < cols + 4), extra, k).astype(BF)
    v = dot_nt(normed, qkv_ref[2])
    v_ref[0] = jnp.where((lane >= cols) & (lane < cols + 3), one, v).astype(BF)


def project(info, toks, upd_own, upd_other, sel, gains, qkv_w, heads, width, count):
    own, d = toks[0].shape
    full = lambda dims: pl.BlockSpec(dims, lambda r, info: (0,) * len(dims))
    placed = lambda w: pl.BlockSpec((1, own, w), lambda r, info: (jnp.bitwise_xor(r, info[0]), 0, 0))
    padded = shape((count, own, PAD), BF)
    return pl.pallas_call(
        functools.partial(project_kernel, heads, width),
        out_shape=(shape((own, d), BF), shape((count, own, d), BF), padded, padded, padded),
        grid_spec=pltpu.PrefetchScalarGridSpec(
            num_scalar_prefetch=1,
            grid=(count,),
            in_specs=[full(tok.shape) for tok in toks]
            + [full(upd_own.shape)] * 2
            + [full(sel.shape), full(gains.shape), full(qkv_w.shape)],
            out_specs=(full((own, d)), placed(d), placed(PAD), placed(PAD), placed(PAD)),
            scratch_shapes=[pltpu.VMEM((own, d), BF)],
        ),
        compiler_params=params(grid=1),
        cost_estimate=cost(9),
        name="project",
    )(info, *toks, upd_own, upd_other, sel, gains, qkv_w)


def attention_kernel(
    heads, width, base, per, info, q_ref, k_ref, v_ref, mix_ref,
    send_ref, keep_ref, mixed_ref, lse_ref,
):
    i = pl.program_id(0)
    block = q_ref.shape[1]
    cols = heads * width
    steps = k_ref.shape[0] // block
    place = jnp.bitwise_xor(base + 1 - i // per, info[0]) * per + i % per

    def run(step):
        span = (step + 1) * block
        q = q_ref[0]
        lane = lanes(block, PAD)
        total = jnp.zeros((block, PAD), F32)
        lse = jnp.zeros((block, 128), F32)
        zero = jnp.zeros_like(q)
        for h in range(heads):
            here = (lane >= h * width) & (lane < (h + 1) * width)
            qh = jnp.where(here | (lane == cols + 3), q, zero)
            scores = dot_nt(qh, k_ref[0:span, :])
            causal = lanes(block, block) <= subs(block, block)
            tail = jnp.where(causal, scores[:, span - block :], NEGATIVE)
            high = jnp.max(tail, axis=-1, keepdims=True)
            if step:
                high = jnp.maximum(high, jnp.max(scores[:, : span - block], axis=-1, keepdims=True))
            probs = jnp.exp(tail - high).astype(BF)
            if step:
                probs = jnp.concatenate(
                    [jnp.exp(scores[:, : span - block] - high).astype(BF), probs], 1
                )
            out = dot(probs, v_ref[0:span, :])
            norm = jnp.sum(jnp.where(lane == cols, out, 0.0), axis=-1, keepdims=True)
            total = jnp.where(here, out / norm, total)
            lse = jnp.where(lanes(block, 128) == h, high + jnp.log(norm), lse)
        lse_ref[0] = lse
        mixed = total.astype(BF)
        mixed_ref[0] = mixed
        part = dot(mixed, mix_ref[...]).astype(BF)

        @pl.when(i < per)
        def _():
            send_ref[...] = part

        @pl.when(i >= per)
        def _():
            keep_ref[...] = part

    for step in range(steps):
        @pl.when(place == step)
        def _():
            run(step)


def attention(info, q, k, v, mix_w, heads, width, base, block=256):
    count, own, _ = q.shape
    total = count * own
    d = mix_w.shape[1]
    per = own // block
    k, v = k.reshape(total, PAD), v.reshape(total, PAD)
    full = lambda dims: pl.BlockSpec(dims, lambda i, info: (0,) * len(dims))
    rel = lambda w: pl.BlockSpec((1, block, w), lambda i, info: (1 - i // per, i % per, 0))
    out = shape((own, d), BF)
    return pl.pallas_call(
        functools.partial(attention_kernel, heads, width, base, per),
        out_shape=(out, out, shape((2, own, PAD), BF), shape((2, own, 128), F32)),
        grid_spec=pltpu.PrefetchScalarGridSpec(
            num_scalar_prefetch=1,
            grid=(2 * per,),
            in_specs=[
                pl.BlockSpec(
                    (1, block, PAD),
                    lambda i, info: (
                        jnp.bitwise_xor(base + 1 - i // per, info[0]), i % per, 0,
                    ),
                ),
                full(k.shape), full(v.shape), full(mix_w.shape),
            ],
            out_specs=(
                pl.BlockSpec((block, d), lambda i, info: (jnp.minimum(i, per - 1), 0)),
                pl.BlockSpec((block, d), lambda i, info: (jnp.maximum(i - per, 0), 0)),
                rel(PAD), rel(128),
            ),
        ),
        compiler_params=params(grid=1),
        cost_estimate=cost(0.3),
        name="attention",
    )(info, q, k, v, mix_w)


def mlp_kernel(
    half, rows_ref, keep_ref, near_ref, far_ref, cot_ref, gains_ref,
    p0a, p0b, p1a, p1b, p2a, p2b, p3a, p3b,
    result_ref, low_ref, d_mid_ref, d_mid_low_ref, keep_out, send_out,
    vec_ref, up_v, down_v, slope_v, act_v, pre_v, rows_v, result_v, low_v, sems, out_sems,
):
    leaving = []

    def leave(src, dst):
        copy = pltpu.make_async_copy(src, dst, out_sems.at[len(leaving)])
        copy.start()
        leaving.append(copy)

    parity = lax.axis_index("dp") & 1
    first = pl.ds(pl.multiple_of(parity * half, half), half)
    second = pl.ds(pl.multiple_of((1 - parity) * half, half), half)
    copies = {}
    count = 0
    for i in range(4):
        for n, (name, dest) in enumerate((("up", up_v), ("down", down_v))):
            a, b = ((p0a, p0b), (p1a, p1b), (p2a, p2b), (p3a, p3b))[i]
            moves = [(a.at[n], dest.at[i, first, :]), (b.at[n], dest.at[i, second, :])]
            some = []
            for src, dst in moves:
                copy = pltpu.make_async_copy(src, dst, sems.at[count])
                copy.start()
                some.append(copy)
                count += 1
            copies[name, i] = some
    attn = keep_ref[...].astype(F32) + near_ref[...].astype(F32) + far_ref[...].astype(F32)
    middle = rows_ref[...].astype(F32) + attn
    unit2, scale2 = unit_rows(middle)
    normed = (unit2 * gains_ref[1:2, :]).astype(BF)
    rows_v[0] = normed
    leave(rows_v.at[0], send_out.at[4])
    mlp = jnp.zeros_like(middle)
    for i in range(4):
        for copy in copies["up", i]:
            copy.wait()
        act, slope = gelu_pair(dot(normed, up_v[i]))
        act = act.astype(BF)
        act_v[i] = act
        leave(act_v.at[i], (keep_out if i % 2 == 0 else send_out).at[i // 2])
        slope_v[i] = slope
        for copy in copies["down", i]:
            copy.wait()
        mlp = mlp + dot(act, down_v[i])
    unit3, scale3 = unit_rows(middle + mlp)
    gain3 = gains_ref[2:3, :]
    result = unit3 * gain3
    result_v[...] = result
    leave(result_v, result_ref)
    low_v[...] = result.astype(BF)
    leave(low_v, low_ref)
    cot = cot_ref[0].astype(F32)
    vec_ref[1:2, :] = jnp.sum(cot * unit3, axis=0, keepdims=True)
    d_final = norm_back(unit3, scale3, gain3, cot)
    d_mlp = d_final.astype(BF)
    rows_v[1] = d_mlp
    leave(rows_v.at[1], send_out.at[5])
    d_normed = jnp.zeros_like(middle)
    for i in range(4):
        d_pre = (dot_nt(d_mlp, down_v[i]) * slope_v[i]).astype(BF)
        pre_v[i] = d_pre
        leave(pre_v.at[i], (keep_out if i % 2 == 0 else send_out).at[2 + i // 2])
        d_normed = d_normed + dot_nt(d_pre, up_v[i])
    vec_ref[0:1, :] = jnp.sum(d_normed * unit2, axis=0, keepdims=True)
    d_mid = d_final + norm_back(unit2, scale2, gains_ref[1:2, :], d_normed)
    d_mid_ref[...] = d_mid
    low = d_mid.astype(BF)
    d_mid_low_ref[...] = low
    rows_v[2] = low
    leave(rows_v.at[2], send_out.at[6])
    for copy in leaving:
        copy.wait()


def mlp_pass(rows, keep, near, far, cot, gains, pieces):
    own, d = rows.shape
    hidden = pieces[0].shape[2]
    half = d // 2
    wide, low = shape((own, d), F32), shape((own, d), BF)
    return pl.pallas_call(
        functools.partial(mlp_kernel, half),
        out_shape=(
            wide, low, wide, low, shape((4, own, d), BF), shape((7, own, d), BF), shape((2, d), F32)
        ),
        in_specs=[VM] * 6 + [HB] * 8,
        out_specs=(HB, HB, VM, VM, HB, HB, VM),
        scratch_shapes=[
            pltpu.VMEM((4, d, hidden), BF),
            pltpu.VMEM((4, hidden, d), BF),
            pltpu.VMEM((4, own, hidden), F32),
            pltpu.VMEM((4, own, hidden), BF),
            pltpu.VMEM((4, own, hidden), BF),
            pltpu.VMEM((3, own, d), BF),
            pltpu.VMEM((own, d), F32),
            pltpu.VMEM((own, d), BF),
            pltpu.SemaphoreType.DMA((16,)),
            pltpu.SemaphoreType.DMA((13,)),
        ],
        compiler_params=params(60),
        cost_estimate=cost(21),
        name="dense_mlp",
    )(rows, keep, near, far, cot, gains, *pieces)


FIRST = 8


def far_grads_kernel(
    act_ref, pre_ref, near_ref, own_ref, act2_ref, pre2_ref, near2_ref, rows2_ref,
    cross_ref, hop_ref, first_ref,
):
    i = pl.program_id(0)
    d = own_ref.shape[2]
    part = first_ref.shape[0]

    @pl.when(i == 0)
    def _():
        up = dot_tn(own_ref[0], pre_ref[0]) + dot_tn(rows2_ref[0], pre2_ref[0])
        cross_ref[:d] = up.astype(BF)

    @pl.when(i == 1)
    def _():
        rows, rows2 = own_ref[0], rows2_ref[0]
        down = (dot_tn(rows, act_ref[0]) + dot_tn(rows2, act2_ref[0])).astype(BF)
        cross_ref[d:] = down[:part]
        hop_ref[0] = down[part:]
        near = (dot_tn(rows, near_ref[0]) + dot_tn(rows2, near2_ref[0])).astype(BF)
        first_ref[...] = near[:part]
        hop_ref[1] = near[part:]


def near_grads_kernel(pre_ref, own_ref, pre2_ref, rows2_ref, first_ref, crossed_ref, out_ref):
    d = own_ref.shape[2]
    up = dot_tn(own_ref[0], pre_ref[0]) + dot_tn(rows2_ref[0], pre2_ref[0])
    out_ref[:d] = (up + crossed_ref[:d].astype(F32)).astype(BF)
    out_ref[d:] = (first_ref[...].astype(F32) + crossed_ref[d:].astype(F32)).astype(BF)


def far_grads(keep, send, other):
    _, own, d = keep.shape
    part = d // FIRST
    at = lambda n: pl.BlockSpec((1, own, d), lambda i: (n, 0, 0))
    pair = pl.BlockSpec((1, own, d), lambda i: (4 + i, 0, 0))
    return pl.pallas_call(
        far_grads_kernel,
        out_shape=(
            shape((d + part, d), BF), shape((2, d - part, d), BF), shape((part, d), BF)
        ),
        grid=(2,),
        in_specs=[at(1), at(3), at(0), pair, at(1), at(3), at(0), pair],
        out_specs=(
            pl.BlockSpec((d + part, d), lambda i: (0, 0)),
            pl.BlockSpec((2, d - part, d), lambda i: (0, 0, 0)),
            pl.BlockSpec((part, d), lambda i: (0, 0)),
        ),
        compiler_params=params(56, grid=1),
        cost_estimate=cost(5),
        name="far_grads",
    )(keep, keep, keep, send, other, other, other, other)


def near_grads(keep, send, other, first, crossed):
    _, own, d = keep.shape
    at = lambda n: pl.BlockSpec((1, own, d), lambda i: (n, 0, 0))
    full = lambda a: pl.BlockSpec(a.shape, lambda i: (0, 0))
    return pl.pallas_call(
        near_grads_kernel,
        out_shape=shape(crossed.shape, BF),
        grid=(1,),
        in_specs=[at(2), at(4), at(2), at(4), full(first), full(crossed)],
        out_specs=full(crossed),
        compiler_params=params(56, grid=1),
        cost_estimate=cost(5),
        name="near_grads",
    )(keep, send, other, other, first, crossed)


def attention_back_kernel(
    heads, width, block, info, g0, g1, g2, g3, q_ref, k_ref, v_ref, mixed_n, mixed_f, lse_n, lse_f,
    mix_ref, qkv_ref, sel_ref, d_qkv_ref, keep_ref, send_ref, mid_ref,
    qs, ds, dq_acc, dk_acc, dv_acc,
):
    tensor, low = info[0], info[2]
    own = g0.shape[0]
    cols = heads * width
    total = k_ref.shape[0]
    lane = lanes(own, PAD)
    zero = jnp.zeros((own, PAD), BF)
    grads = (g0[...], g1[0], g2[...], g3[...])
    for r, grad in enumerate(grads):
        at = pl.multiple_of(jnp.bitwise_xor(tensor, r) * own, own)
        span = pl.ds(at, own)
        d_mixed = dot_nt(grad, mix_ref[...]).astype(BF)
        inner = d_mixed.astype(F32) * (mixed_n if r < 2 else mixed_f)[r % 2].astype(F32)
        q = q_ref[span, :]
        lse = (lse_n if r < 2 else lse_f)[r % 2]
        for h in range(heads):
            here = (lane >= h * width) & (lane < (h + 1) * width)
            delta = -jnp.sum(jnp.where(here, inner, 0.0), axis=-1, keepdims=True)
            row_lse = -jnp.sum(jnp.where(lanes(own, 128) == h, lse, 0.0), axis=-1, keepdims=True)
            left = jnp.where(here | (lane == cols + 3), q, zero)
            right = jnp.where(here, d_mixed, zero)
            for p, (a, b) in enumerate(zip(three_pieces(row_lse), three_pieces(delta))):
                left = jnp.where(lane == cols + p, a, left)
                right = jnp.where(lane == cols + p, b, right)
            qs[h, span, :] = left
            ds[h, span, :] = right
    dq_acc[...] = jnp.zeros_like(dq_acc)
    lane_k = lanes(block, PAD)
    allowed = subs(block, block) <= lanes(block, block)
    for j in range(total // block):
        first = j * block
        k, v = k_ref[first : first + block, :], v_ref[first : first + block, :]
        dk = jnp.zeros((block, PAD), F32)
        dv = jnp.zeros((block, PAD), F32)
        stacked, keys = [], []
        for h in range(heads):
            qh, dh = qs[h, first:, :], ds[h, first:, :]
            scores = dot_nt(k, qh)
            d_probs = dot_nt(v, dh)
            head = jnp.where(allowed, scores[:, :block], NEGATIVE)
            probs = jnp.exp(head)
            if first + block < total:
                probs = jnp.concatenate([probs, jnp.exp(scores[:, block:])], 1)
            d_scores = (probs * d_probs).astype(BF)
            dv = dv + dot(probs.astype(BF), dh)
            dk = dk + dot(d_scores, qh)
            stacked.append(d_scores)
            keys.append(
                jnp.where((lane_k >= h * width) & (lane_k < (h + 1) * width), k, jnp.zeros_like(k))
            )
        dq_acc[first:, :] += dot_tn(jnp.concatenate(stacked, 0), jnp.concatenate(keys, 0))
        dk_acc[...] = dk
        dv_acc[...] = dv
        d_qkv_ref[1, first : first + block, :] = dk_acc[:, :cols].astype(BF)
        d_qkv_ref[2, first : first + block, :] = dv_acc[:, :cols].astype(BF)
    d_qkv_ref[0] = (dq_acc[:, :cols] * width ** (-0.5)).astype(BF)
    pick = sel_ref.shape[1]
    sel = jnp.where(info[1] == 0, sel_ref[0:1, :], sel_ref[1:2, :])
    table = (sel == subs(total, pick)).astype(F32).astype(BF)
    part = jnp.zeros((pick, qkv_ref.shape[2]), F32)
    for i in range(3):
        part = part + dot(dot_tn(table, d_qkv_ref[i]).astype(BF), qkv_ref[i][:cols, :])
    half = pick // 2
    keep_ref[...] = jnp.where(low == 0, part[:half], part[half:]).astype(BF)
    send_ref[...] = jnp.where(low == 0, part[half:], part[:half]).astype(BF)
    mine = jnp.where(low == 0, sel[:, :half], sel[:, half:])
    mid = jnp.zeros((half, qkv_ref.shape[2]), F32)
    for r, grad in enumerate(grads):
        table = (mine == subs(own, half) + jnp.bitwise_xor(tensor, r) * own).astype(F32).astype(BF)
        mid = mid + dot_tn(table, grad)
    mid_ref[...] = mid.astype(BF)


def attention_back(
    info, grads, q, k, v, mixed, lse, mix_w, qkv_w, selected, heads, width, block=256
):
    keep, other, far, far_other = grads
    own, d = keep.shape
    total = k.shape[0] * k.shape[1]
    flat = lambda a: a.reshape(total, PAD)
    half = shape((selected.shape[1] // 2, d), BF)
    at = lambda n: pl.BlockSpec((1, own, d), lambda i: (n, 0, 0))
    full = lambda a: pl.BlockSpec(a.shape, lambda i: (0,) * a.ndim)
    rest = (flat(q), flat(k), flat(v), *mixed, *lse, mix_w, qkv_w, selected)
    return pl.pallas_call(
        functools.partial(attention_back_kernel, heads, width, block),
        out_shape=(shape((3, total, heads * width), BF), half, half, half),
        grid=(1,),
        in_specs=[SM, full(keep), at(6), full(far), full(far_other)] + [full(a) for a in rest],
        out_specs=(
            pl.BlockSpec((3, total, heads * width), lambda i: (0, 0, 0)),
        ) + (pl.BlockSpec(half.shape, lambda i: (0, 0)),) * 3,
        scratch_shapes=[
            pltpu.VMEM((heads, total, PAD), BF),
            pltpu.VMEM((heads, total, PAD), BF),
            pltpu.VMEM((total, PAD), F32),
            pltpu.VMEM((block, PAD), F32),
            pltpu.VMEM((block, PAD), F32),
        ],
        compiler_params=params(60, grid=1),
        cost_estimate=cost(35),
        name="attention_back",
    )(info, keep, other, far, far_other, *rest)


def spread_back_kernel(cols, info, d_ref, qkv_ref, send_ref, keep_ref):
    i = pl.program_id(0)
    total = dot(d_ref[0, 0], qkv_ref[0][:cols, :])
    for n in (1, 2):
        total = total + dot(d_ref[n, 0], qkv_ref[n][:cols, :])
    total = total.astype(BF)

    @pl.when(i < 2)
    def _():
        send_ref[0] = total

    @pl.when(i >= 2)
    def _():
        keep_ref[0] = total


def spread_back(info, d_qkv, qkv_w, count):
    _, total, cols = d_qkv.shape
    own = total // count
    d = qkv_w.shape[2]
    pos = lambda i: jnp.where(i < 2, 3 - 2 * i, 6 - 2 * i)
    out = shape((2, own, d), BF)
    return pl.pallas_call(
        functools.partial(spread_back_kernel, cols),
        out_shape=(out, out),
        grid_spec=pltpu.PrefetchScalarGridSpec(
            num_scalar_prefetch=1,
            grid=(count,),
            in_specs=[
                pl.BlockSpec(
                    (3, 1, own, cols), lambda i, info: (0, jnp.bitwise_xor(pos(i), info[0]), 0, 0)
                ),
                pl.BlockSpec(qkv_w.shape, lambda i, info: (0, 0, 0)),
            ],
            out_specs=(
                pl.BlockSpec((1, own, d), lambda i, info: (1 - jnp.minimum(i, 1), 0, 0)),
                pl.BlockSpec((1, own, d), lambda i, info: (1 - jnp.maximum(i - 2, 0), 0, 0)),
            ),
        ),
        compiler_params=params(grid=1),
        cost_estimate=cost(5),
        name="spread_back",
    )(info, d_qkv.reshape(3, count, own, cols), qkv_w)


def attn_grads_kernel(
    cols, info, d_ref, normed_ref, g0, g1, g2, g3, mixed_n, mixed_f, pack_ref, acc,
):
    i = pl.program_id(0)

    @pl.when(i == 0)
    def _():
        acc[...] = jnp.zeros_like(acc)

    for n in range(3):
        acc[n * cols : (n + 1) * cols, :] += dot_tn(d_ref[n, 0], normed_ref[0])
    for r, grad in enumerate((g0, g1, g2, g3)):
        @pl.when(i == r)
        def _():
            mixed = (mixed_n if r < 2 else mixed_f)[r % 2]
            rows = grad[0] if r == 1 else grad[...]
            acc[3 * cols :, :] += dot_tn(mixed[:, :cols], rows)

    @pl.when(i == 3)
    def _():
        pack_ref[...] = jnp.transpose(acc[...]).astype(BF)


def attn_grads(info, d_qkv, normed, grads, mixed):
    _, total, cols = d_qkv.shape
    count, own, d = normed.shape
    full = lambda dims: pl.BlockSpec(dims, lambda i, info: (0,) * len(dims))
    return pl.pallas_call(
        functools.partial(attn_grads_kernel, cols),
        out_shape=shape((d, 4 * cols), BF),
        grid_spec=pltpu.PrefetchScalarGridSpec(
            num_scalar_prefetch=1,
            grid=(count,),
            in_specs=[
                pl.BlockSpec(
                    (3, 1, own, cols), lambda i, info: (0, jnp.bitwise_xor(i, info[0]), 0, 0)
                ),
                pl.BlockSpec((1, own, d), lambda i, info: (jnp.bitwise_xor(i, info[0]), 0, 0)),
            ]
            + [
                full((own, d)), pl.BlockSpec((1, own, d), lambda i, info: (6, 0, 0)),
                full((own, d)), full((own, d)),
            ]
            + [full(mixed[0].shape)] * 2,
            out_specs=full((d, 4 * cols)),
            scratch_shapes=[pltpu.VMEM((4 * cols, d), F32)],
        ),
        compiler_params=params(grid=1),
        cost_estimate=cost(8),
        name="attn_grads",
    )(info, d_qkv.reshape(3, count, own, cols), normed, *grads, *mixed)


def routed_mlp_grads_kernel(
    info, normed_ref, pre_ref, act_ref, grad_ref, part_ref, far_ref, last_ref, last_far, last_cross,
    pack_ref,
):
    hidden = pre_ref.shape[1]

    @pl.when(info[1] == 0)
    def _():
        pack_ref[:, :hidden] = dot_tn(normed_ref[...], pre_ref[...]).astype(BF)
        pack_ref[:, hidden:] = dot_tn(grad_ref[...], act_ref[...]).astype(BF)

    @pl.when(info[1] != 0)
    def _():
        d = normed_ref.shape[1]
        total = (part_ref[...].astype(F32) + far_ref[...].astype(F32)).astype(BF)
        part = part_ref.shape[0] - d
        pack_ref[:, :hidden] = total[:d]
        pack_ref[:part, hidden:] = total[d:]
        total = last_ref[1].astype(F32) + last_far[1].astype(F32) + last_cross[...].astype(F32)
        pack_ref[part:, hidden:] = total.astype(BF)


def routed_mlp_grads(info, normed, pre, act, grad, *dense):
    return pl.pallas_call(
        routed_mlp_grads_kernel,
        out_shape=shape((normed.shape[1], 2 * pre.shape[1]), BF),
        in_specs=[SM] + [VM] * 9,
        out_specs=VM,
        compiler_params=params(),
        cost_estimate=cost(5),
        name="routed_mlp_grads",
    )(info, normed, pre, act, grad, *dense)


def routed_attn_grads_kernel(
    info, normed_ref, d_ref, low_ref, mixed_ref, part_ref, hop_ref, pack_ref
):
    cols = mixed_ref.shape[1]

    @pl.when(info[1] == 0)
    def _():
        rows = [dot_tn(d_ref[n], normed_ref[...]) for n in range(3)]
        rows.append(dot_tn(mixed_ref[...], low_ref[...]))
        pack_ref[...] = jnp.transpose(jnp.concatenate(rows, 0)).astype(BF)

    @pl.when(info[1] != 0)
    def _():
        pack_ref[...] = (part_ref[...].astype(F32) + hop_ref[...].astype(F32)).astype(BF)


def routed_attn_grads(info, normed, d_qkv, d_low, mixed, part, far):
    return pl.pallas_call(
        routed_attn_grads_kernel,
        out_shape=shape((normed.shape[1], 4 * mixed.shape[1]), BF),
        in_specs=[SM] + [VM] * 6,
        out_specs=VM,
        compiler_params=params(),
        cost_estimate=cost(3),
        name="routed_attn_grads",
    )(info, normed, d_qkv, d_low, mixed, part, far)


def rows_back_kernel(keep_ref, near_ref, far_ref, rows_ref, d_mid_ref, gains_ref, d_rows_ref, vec_ref):
    d_normed = keep_ref[0].astype(F32) + near_ref[0].astype(F32) + far_ref[...].astype(F32)
    unit, scale = unit_rows(rows_ref[...].astype(F32))
    vec_ref[...] = jnp.sum(d_normed * unit, axis=0, keepdims=True)
    d_rows = d_mid_ref[...] + norm_back(unit, scale, gains_ref[0:1, :], d_normed)
    d_rows_ref[...] = d_rows.astype(BF)


def rows_back(keep, near, far, rows, d_mid, gains):
    own, d = rows.shape
    return pl.pallas_call(
        rows_back_kernel,
        out_shape=(shape((own, d), BF), shape((1, d), F32)),
        in_specs=[VM] * 6,
        out_specs=(VM, VM),
        compiler_params=params(),
        cost_estimate=cost(4),
        name="rows_back",
    )(keep, near, far, rows, d_mid, gains)


def sel_back_kernel(near_ref, far_ref, picked_ref, upd_ref, mid_ref, gains_ref, out_ref):
    d_normed = near_ref[...].astype(F32) + far_ref[...].astype(F32)
    rows = (picked_ref[...].astype(F32) + upd_ref[...].astype(F32)).astype(BF).astype(F32)
    unit, scale = unit_rows(rows)
    d_rows = mid_ref[...].astype(F32) + norm_back(unit, scale, gains_ref[0:1, :], d_normed)
    out_ref[...] = d_rows.astype(BF)


def sel_back(near, far, picked, upd, mid, gains):
    return pl.pallas_call(
        sel_back_kernel,
        out_shape=shape(near.shape, BF),
        in_specs=[VM] * 6,
        out_specs=VM,
        compiler_params=params(),
        cost_estimate=cost(2.3),
        name="sel_back",
    )(near, far, picked, upd, mid, gains)


def add(a, b):
    return (a.astype(F32) + b.astype(F32)).astype(BF)


def core_sum(keep, send):
    return add(keep, swap(send, "tensor", 1))


def whole_sum(keep, send):
    near = core_sum(keep, send)
    return add(near, swap(near, "tensor", 2))


def scatter_groups(pack, later):
    count, me = lax.axis_size("dp"), lax.axis_index("dp")
    if count != 4:
        return lax.psum_scatter(pack, "dp", scatter_dimension=0, tiled=True), later
    for bit in (1, 2):
        rows = pack.shape[0] // 2
        side = (me // bit) % 2
        if bit == 1:
            quarters = pack.reshape(2, 2, rows // 2, pack.shape[1])
            take = lambda at: lax.dynamic_index_in_dim(quarters, at, 1, keepdims=False)
            keep, send = take(side), take(1 - side)
        else:
            keep = lax.dynamic_index_in_dim(pack, side, 0, keepdims=False)
            send = lax.dynamic_index_in_dim(pack, 1 - side, 0, keepdims=False)
        pack = add(keep, swap(send, "dp", bit))
        if bit == 1:
            later = after(later, pack)
    return pack, later


def body(
    tokens, qkv_weight, out_weight, up_weight, down_weight, vectors, lengths, selected, cotangent
):
    section = lax.axis_index("section")
    tensor = lax.axis_index("tensor")
    group = lax.axis_size("dp")
    heads = HEADS // lax.axis_size("tensor")
    low = tensor & 1
    is_dense = section == 1
    gains = vectors[0]
    qkv_w = jnp.swapaxes(qkv_weight[0], 1, 2)
    mix_w, up_w, down_w = out_weight[0], up_weight[0], down_weight[0]
    cols = qkv_w.shape[1]
    width = cols // heads
    d = mix_w.shape[1]

    barrier = lax.optimization_barrier
    core = lambda block: swap(block, "tensor", 1)
    cross = lambda block: swap(block, "tensor", 2)

    halves = up_w.shape[0] // 2
    parity = lax.axis_index("dp") & 1
    take = lambda w, at: lax.dynamic_slice_in_dim(w, at * halves, halves, 0)
    mine = (take(up_w, parity), take(down_w, parity))
    up_far = hop(mine[0], 1, 0)
    down_far = hop(after(mine[1], up_far), 1, 0)

    near = core_sum(*pick_rows(tokens, selected))
    far = cross(near)
    info = jnp.stack([tensor, section, low, lengths[section]]).astype(jnp.int32)
    my_tokens = lax.dynamic_index_in_dim(tokens, section, 0, keepdims=False)
    part = my_tokens.shape[0] // 2
    tok_a, tok_b = my_tokens[:part], my_tokens[part:]
    far, my_tokens, info, tok_a, tok_b = barrier((far, my_tokens, info, tok_a, tok_b))
    tok2a = cross(after(tok_a, far))
    packed = pack_weights(gains, qkv_w, mix_w)
    picked_half = add(near, far)
    picked_other = core(picked_half)

    picked, normed, q, k, v, mixed, keep, send = routed_attn(
        info, picked_half, picked_other, gains, qkv_w, mix_w, heads
    )
    send, tok2a, up_far = barrier((send, tok2a, up_far))
    near = core_sum(keep, send)
    far = cross(near)
    far, packed, down_far = barrier((far, packed, down_far))
    attn_half = add(near, far)
    tok2b = cross(after(tok_b, far))
    tok1 = core(my_tokens)
    attn_other = core(attn_half)
    packed_far = hop(after(packed, down_far), 1, 0)
    attn, normed2, act, slope, keep, send = routed_mlp(
        info, picked, attn_half, attn_other, gains, up_w, down_w
    )
    piece0a = jnp.stack(
        [jnp.where(is_dense, own, far) for own, far in zip(mine, (up_far, down_far))]
    )
    send, tok2b = barrier((send, tok2b))
    near = core_sum(keep, send)
    far = cross(near)
    far, piece0a = barrier((far, piece0a))
    both_half, update_half = make_update(picked_half, attn_half, near, far, gains)
    piece2a = cross(after(piece0a, far))
    piece1a = core(piece0a)
    tok3a, tok3b = core(tok2a), core(tok2b)
    arrived = hop(update_half[1], 0, 1)
    my_update = jnp.where(is_dense, arrived, update_half[0])
    my_update, piece1a, packed_far = barrier((my_update, piece1a, packed_far))
    d_gains, d_qkv_w, d_mix_w = prepare(info, gains, qkv_w, mix_w, packed_far)
    my_update_other = core(my_update)
    my_update_other, d_gains = barrier((my_update_other, d_gains))
    toks = (my_tokens, tok1, tok2a, tok2b, tok3a, tok3b)

    piece0b = swap(piece0a, "dp", 1)
    piece2a, piece0b = barrier((after(piece2a, my_update_other), piece0b))
    piece2b = swap(piece2a, "dp", 1)

    rows, d_normed_rows, dq_in, dk_in, dv_in = project(
        info, toks, my_update, my_update_other, selected, d_gains, d_qkv_w, heads, width,
        lax.axis_size("tensor"),
    )
    send, keep, mixed_f, lse_f = attention(info, dq_in, dk_in, dv_in, d_mix_w, heads, width, 2)
    send, piece2b = barrier((send, piece2b))
    near = core_sum(keep, send)
    far = cross(near)
    send, keep, mixed_n, lse_n = attention(info, dq_in, dk_in, dv_in, d_mix_w, heads, width, 0)
    piece3a = core(after(piece2a, send))
    piece3b = core(after(piece2b, send))
    piece1b = core(after(piece0b, send))
    send, far = barrier((send, far))
    near = core(send)
    my_cot = lax.dynamic_slice_in_dim(cotangent, section, 1, 0)
    result, result_low, d_mid, d_mid_low, mlp_keep, mlp_send, m_vec = mlp_pass(
        rows, keep, near, far, my_cot, d_gains,
        (piece0a, piece0b, piece1a, piece1b, piece2a, piece2b, piece3a, piece3b),
    )
    grad_f = cross(d_mid_low)
    mlp_other = core(mlp_send)
    mlp_f, last, first = far_grads(mlp_keep, mlp_send, mlp_other)
    grad_f, mlp_f, last = barrier((grad_f, mlp_f, last))
    grads = (d_mid_low, mlp_other, grad_f, core(grad_f))
    mlp_f2 = cross(mlp_f)
    last_h = hop(last, 0, 1)

    d_qkv, keep, send, mid_sel = attention_back(
        info, grads, dq_in, dk_in, dv_in, (mixed_n, mixed_f), (lse_n, lse_f),
        d_mix_w, d_qkv_w, selected, heads, width,
    )
    near = core_sum(keep, send)
    far = cross(near)
    mlp_part = near_grads(mlp_keep, mlp_send, after(mlp_other, near), first, mlp_f2)
    last_f = add(last[0], after(last_h[0], mlp_part))
    far, mlp_part, last_f = barrier((far, mlp_part, last_f))
    last_f2 = cross(last_f)
    mlp_hop = hop(mlp_part, 0, 1)
    my_picked = lax.dynamic_index_in_dim(picked_half, section, 0, keepdims=False)
    my_d_sel = sel_back(near, far, my_picked, my_update, mid_sel, d_gains)
    back = hop(my_d_sel, 1, 0)
    attn_part = attn_grads(
        info, after(d_qkv, my_d_sel), d_normed_rows, grads, (mixed_n, mixed_f)
    )
    back, attn_part, last_f2 = barrier((back, attn_part, last_f2))
    sel_other = core(jnp.concatenate([my_d_sel[None], back[None], both_half], 0))

    d_sel, r_d_mlp, r_d_pre, gain_two, keep2, send2 = routed_back_mlp(
        info, my_d_sel, back, sel_other, picked, attn, gains, slope, up_w, down_w
    )
    send2, mlp_hop = barrier((send2, mlp_hop))
    near = core_sum(keep2, send2)
    far = cross(near)
    r_mlp = routed_mlp_grads(
        info, normed2, r_d_pre, act, r_d_mlp, mlp_part, mlp_hop, last, last_h, last_f2
    )
    row_send, row_keep = spread_back(info, after(d_qkv, r_mlp), d_qkv_w, 4)
    far, row_send = barrier((far, row_send))
    row_core = core(row_send)
    half = add(near, far)
    other = core(half)
    row_far = cross(add(row_keep[1], row_core[1]))
    attn_hop = hop(attn_part, 0, 1)
    hidden = up_w.shape[1]
    r_d_mid, r_d_low, r_d_qkv, r_vec, keep2, send2 = routed_back_attn(
        info, half, other, d_sel, picked, attn, both_half, sel_other, gains, q, k, v,
        qkv_w, mix_w, heads,
    )
    near = core_sum(keep2, send2)
    near, row_far, attn_hop = barrier((near, row_far, attn_hop))
    far = cross(near)
    r_attn = routed_attn_grads(
        info, normed, r_d_qkv, r_d_low, mixed, after(attn_part, near), attn_hop
    )
    mlp_sum = lax.psum_scatter(r_mlp, "dp", scatter_dimension=0, tiled=True)
    d_mid = after(d_mid, r_attn)
    d_rows, row_vec = rows_back(row_keep, row_core, row_far, rows, d_mid, d_gains)
    d_rows_far = hop(d_rows, 1, 0)
    far, d_rows = barrier((far, d_rows))
    sent_result = hop(after(result_low, attn_hop), 0, 1)
    half = add(near, far)
    other = core(half)
    vecs = jnp.concatenate([r_vec[0:1], gain_two, r_vec[1:2], row_vec, m_vec], 0)
    vecs = vecs + core(vecs)
    vecs = vecs + cross(vecs)
    attn_sum, vecs = scatter_groups(r_attn, vecs)

    combined = finish(
        info, half, other, r_d_mid, picked, gains, selected, d_rows, d_rows_far, sent_result, result
    )
    share = d // group
    up_grad = mlp_sum[:, :hidden].astype(F32)
    down_grad = jnp.swapaxes(mlp_sum[:, hidden:], 0, 1).astype(F32)
    qkv_grad = jnp.swapaxes(attn_sum[:, : 3 * cols].reshape(share, 3, cols), 0, 1).astype(F32)
    mix_grad = jnp.swapaxes(attn_sum[:, 3 * cols : 4 * cols], 0, 1).astype(F32)

    bit = 1
    while bit < lax.axis_size("dp"):
        vecs = vecs + swap(vecs, "dp", bit)
        bit *= 2
    vecs = lax.dynamic_slice_in_dim(vecs, lax.axis_index("dp") * share, share, 1)
    dense_vec = vecs[3:6] + hop(vecs[3:6], 0, 1)
    vecs = jnp.where(is_dense, dense_vec, vecs[:3])
    return (
        combined[None],
        qkv_grad[None],
        mix_grad[None],
        up_grad[None],
        down_grad[None],
        vecs[None],
    )


def solution(mesh):
    placed = (
        P("dp", "tensor", None),
        P("section", None, None, "tensor"),
        P("section", "tensor", None),
        P("section", None, "tensor"),
        P("section", "tensor", None),
        P("section", None, None),
        P("dp"),
        P("dp", None),
        P("dp", "tensor", None),
    )
    return jax.shard_map(
        body,
        mesh=mesh,
        in_specs=placed,
        out_specs=(
            P("section", "dp", "tensor", None),
            P("section", None, "dp", "tensor"),
            P("section", "tensor", "dp"),
            P("section", "dp", "tensor"),
            P("section", "tensor", "dp"),
            P("section", None, "dp"),
        ),
        check_vma=False,
    )
```
